32 devices in a mesh: adapter: 8 (over z, y), tensor: 4 (over x, core).
Axes of the slice: x: 2, y: 2, z: 4, core: 2. Of those that a mesh axis runs over, the one named last changes fastest.
Arguments:
- queries: bfloat16 [1024, 4, 4096], P('adapter', None, 'tensor'), may hold values from -160 to 160
- shared_prefix_cache: bfloat16 [2, 16, 2048, 1024], P(None, 'adapter', None, 'tensor'), may hold values from -6 to 6
- rollout_suffix_cache: bfloat16 [2, 1024, 32, 1024], P(None, 'adapter', None, 'tensor'), may hold values from -9 to 9
- fresh_key_value: bfloat16 [2, 1024, 4, 1024], P(None, 'adapter', None, 'tensor'), may hold values from -9 to 9
- rollout_prefix_index: int32 [1024], P('adapter'), may hold values from 0 to 15, as said below
- rollout_suffix_length: int32 [1024], P('adapter'), may hold values from 1 to 32, as said below
- rollout_adapter_index: int32 [1024, 1], P('adapter'), may hold values from 0 to 31; in each aligned block of 128 rows (0 to 127, 128 to 255, ...) at most 5 rows name the same one
- output_projection_weight: bfloat16 [4096, 4096], P('tensor'), may hold values from -0.75 to 0.75
- adapter_shrink_weight: bfloat16 [32, 64, 4096], P('adapter', None, 'tensor'), may hold values from -0.75 to 0.75
- adapter_expand_weight: bfloat16 [32, 64, 4096], P('adapter', None, 'tensor'), may hold values from -0.75 to 0.75
Outputs:
- mixed: bfloat16 [1024, 4, 4096], P('adapter', None, 'tensor')
The draws below stay inside these ranges and needn't reach their ends.
Inputs may be any that keep to these rules, and one draw needn't show every extreme that they name: rollout_prefix_index[r] // 2 == r // 128: a rollout's prefix is held with it, and the rollouts of one device name each of its 2 prefixes. `rollout_suffix_length`: among the rollouts of one device some has generated 32 tokens. `rollout_adapter_index`: within the rollouts of one device (aligned blocks of 128 rows) no adapter is named more than 5 times, a bound that some block reaches.
All inputs are finite; a program needn't handle non-finite values.
Results may differ from the reference program's by a relative error of at most 0.015.
Values may be sent and summed in bfloat16 or wider, within the bound.
No kernel may reach another device: no remote copies, remote signals or barrier semaphores. Data moves between devices by JAX's collectives and lax.ppermute only.
A program may use at most 128 MiB of HBM per device.

```python
import math
from functools import partial
import jax
import jax.numpy as jnp
import numpy as np
from jax import lax

HEAD_SIZE = 128
QUERY_HEADS = 32
KVH = 8
OUTPUT_FEATURES = 4096
ADAPTER_RANK = 64
MOST = 5
STEPS = 4
PLEN = 2048
SUF = 32
PREF_DEV = 2
ROLL_DEV = 128
ROLLOUTS = 1024
PREFIXES = 16
ADAPTER_COUNT = 32
N_TENSOR = 4


def prefix_ids(key):
    first_key, second_key = jax.random.split(jax.random.fold_in(key, 101))
    block_count = ROLLOUTS // ROLL_DEV
    inner_index = (jnp.arange(ROLLOUTS, dtype=jnp.int32) % ROLL_DEV).reshape(block_count, ROLL_DEV)
    drawn_scores = jax.random.randint(first_key, (block_count, ROLL_DEV), 0, 1 << 20, dtype=jnp.int32) * ROLL_DEV + inner_index
    rank_order = jnp.argsort(jnp.argsort(drawn_scores, axis=1), axis=1).reshape(ROLLOUTS).astype(jnp.int32)
    picked = jax.random.randint(second_key, (ROLLOUTS,), 0, PREF_DEV, dtype=jnp.int32)
    local_index = jnp.where(rank_order < PREF_DEV, rank_order, picked)
    return jnp.arange(ROLLOUTS, dtype=jnp.int32) // ROLL_DEV * PREF_DEV + local_index


def prefix_cache(key):
    cache_key = jax.random.fold_in(key, 202)
    grid_shape = (2, PREFIXES, PLEN, KVH * HEAD_SIZE)
    cache_draw = jnp.clip(jax.random.normal(cache_key, grid_shape, jnp.float32), -6.0, 6.0)
    return cache_draw


def draw_shared_prefix_cache(key, part):
    return prefix_cache(key).astype(jnp.bfloat16)


def draw_rollout_prefix_index(key, part):
    return prefix_ids(key)


def draw_rollout_suffix_length(key, part):
    first_key, second_key = jax.random.split(jax.random.fold_in(key, 404))
    drawn_lengths = jax.random.randint(first_key, (ROLLOUTS,), 1, SUF + 1, dtype=jnp.int32)
    block_count = ROLLOUTS // ROLL_DEV
    picked = jax.random.randint(second_key, (block_count,), 0, ROLL_DEV, dtype=jnp.int32)
    longest = jnp.arange(ROLLOUTS, dtype=jnp.int32) % ROLL_DEV == jnp.repeat(picked, ROLL_DEV)
    return jnp.where(longest, SUF, drawn_lengths).astype(jnp.int32)


def draw_queries(key, part):
    query_key = jax.random.fold_in(key, 303)
    grid_shape = (ROLLOUTS, STEPS, QUERY_HEADS * HEAD_SIZE)
    drawn = jnp.clip(2.0 * jax.random.normal(query_key, grid_shape, jnp.float32), -12.0, 12.0)
    return drawn.astype(jnp.bfloat16)


def block_levels(own_key, dims, cuts, least, top_value):
    def one(dim, shards_of):
        draws = jax.random.uniform(jax.random.fold_in(jax.random.fold_in(own_key, 6), dim), (shards_of,), jnp.float32, least / len(cuts), top_value / len(cuts))
        return jnp.repeat(jnp.exp(draws), dims[dim] // shards_of).reshape((-1,) + (1,) * (len(dims) - dim - 1))

    loudness = one(*cuts[0])
    for cut in cuts[1:]:
        loudness = loudness * one(*cut)
    return loudness


def routed_block(stream_key, own, number, rows, amount, top, most, skew):
    ranking = jax.random.permutation(stream_key, amount)
    packed, common = load_shares(amount, rows * top, most, skew, True), load_shares(amount, rows * top, most, skew, False)
    places = jnp.arange(amount)

    def named(lengths, turn):
        used = int((lengths > 0).sum())
        fixed = max(1, used // 4)
        shifted = fixed + (places - fixed + turn * (used - fixed)) % max(1, amount - fixed)
        return jnp.zeros((amount,), jnp.int32).at[ranking[jnp.where(places < fixed, places, shifted)]].set(jnp.asarray(lengths, jnp.int32))

    lengths = jnp.where(number % 4 == 0, named(packed, number // 4), named(common, number - number // 4 - 1))
    mixed = jax.random.permutation(jax.random.fold_in(own, 3), amount)
    source_of, taker = mixed[0:amount // 2 * 2:2], mixed[1:amount // 2 * 2:2]
    margin = jnp.minimum(lengths[source_of] - 1, most - lengths[taker]) // 2
    margin = jnp.where((source_of == ranking[0]) | (taker == ranking[0]) | (lengths[taker] == 0), 0, jnp.maximum(margin, 0))
    shifted = jax.random.randint(jax.random.fold_in(own, 4), (amount // 2,), 0, 1 << 20) % (margin + 1)
    lengths = lengths.at[source_of].add(-shifted).at[taker].add(shifted)
    labels = jnp.searchsorted(jnp.cumsum(lengths), jnp.arange(rows * top), side="right").astype(jnp.int32)
    table = labels.reshape(top, rows).T
    table = table[jax.random.permutation(jax.random.fold_in(own, 1), rows)]
    turn = jax.random.randint(jax.random.fold_in(own, 2), (rows, 1), 0, top)
    return jnp.take_along_axis(table, (jnp.arange(top)[None, :] + turn) % top, axis=1)


def load_shares(amount, total, reach, lean, full):
    portions = [(1 << 20) // math.isqrt(rank ** lean) + 1 for rank in range(1, amount + 1)]
    largest = reach if full else min(reach, max(-(-total // amount), total * portions[0] // sum(portions)))
    least = 1 if total - largest >= amount - 1 else 0
    given, surplus = [largest] + [least] * (amount - 1), total - largest - least * (amount - 1)
    while surplus > 0:
        movable = [i for i in range(1, amount) if given[i] < largest] or [i for i in range(1, amount) if given[i] < reach]
        mass, left = sum([portions[i] for i in movable]), surplus
        for i in movable:
            extra = min(reach - given[i], max(1, left * portions[i] // mass), surplus)
            given[i] = given[i] + extra
            surplus = surplus - extra
    return np.array(given)


def noise(stream_key, dims, width, bound, cuts=(), held_as=jnp.bfloat16):
    array = width * jax.random.normal(stream_key, dims, jnp.float32)
    if cuts:
        array = array * block_levels(stream_key, dims, cuts, -0.22, 0.18)
    return jnp.clip(array, -bound, bound).astype(held_as)


def setup_inputs(seed: int = 0) -> dict:
    streams_of = jax.random.split(jax.random.key(seed), 11)
    queries = draw_queries(jax.random.fold_in(streams_of[10], 71), 0)
    shared_prefix_cache = draw_shared_prefix_cache(jax.random.fold_in(streams_of[10], 71), 0)
    rollout_suffix_cache = noise(streams_of[2], (2, ROLLOUTS, SUF, KVH * HEAD_SIZE), 1.5, 9.0, ((1, 8), (3, 4)))
    fresh_key_value = noise(streams_of[3], (2, ROLLOUTS, STEPS, KVH * HEAD_SIZE), 1.5, 9.0, ((1, 8), (3, 4)))
    rollout_prefix_index = draw_rollout_prefix_index(jax.random.fold_in(streams_of[10], 71), 0)
    rollout_suffix_length = draw_rollout_suffix_length(jax.random.fold_in(streams_of[10], 71), 0)
    rollout_adapter_index_keys = jax.random.split(jax.random.fold_in(streams_of[6], 1), ROLLOUTS // ROLL_DEV)
    rollout_adapter_index_turns = jax.random.permutation(jax.random.fold_in(streams_of[6], 3), ROLLOUTS // ROLL_DEV)
    rollout_adapter_index = jax.vmap(lambda own, number: routed_block(jax.random.fold_in(streams_of[6], 2), own, number, ROLL_DEV, ADAPTER_COUNT, 1, MOST, 2))(rollout_adapter_index_keys, rollout_adapter_index_turns).reshape((ROLLOUTS, 1))
    output_projection_weight = noise(streams_of[7], (QUERY_HEADS * HEAD_SIZE, OUTPUT_FEATURES), (QUERY_HEADS * HEAD_SIZE // 64) ** -0.5, 0.75, ((0, 4),))
    adapter_shrink_weight = noise(streams_of[8], (ADAPTER_COUNT, ADAPTER_RANK, QUERY_HEADS * HEAD_SIZE), (QUERY_HEADS * HEAD_SIZE // 64) ** -0.5, 0.75, ((0, 8), (2, 4)))
    adapter_expand_weight = noise(streams_of[9], (ADAPTER_COUNT, ADAPTER_RANK, OUTPUT_FEATURES), ADAPTER_RANK ** -0.5, 0.75, ((0, 8), (2, 4)))
    return {"queries": queries, "shared_prefix_cache": shared_prefix_cache, "rollout_suffix_cache": rollout_suffix_cache, "fresh_key_value": fresh_key_value, "rollout_prefix_index": rollout_prefix_index, "rollout_suffix_length": rollout_suffix_length, "rollout_adapter_index": rollout_adapter_index, "output_projection_weight": output_projection_weight, "adapter_shrink_weight": adapter_shrink_weight, "adapter_expand_weight": adapter_expand_weight}


def attend_rollout(shared_prefix_cache, query_rows, suffix_part, fresh_part, prefix_index, length):
    chosen = lax.dynamic_index_in_dim(shared_prefix_cache, prefix_index, axis=1, keepdims=False)
    joined = jnp.concatenate([chosen, suffix_part, fresh_part], axis=1)
    total_keys = PLEN + SUF + STEPS
    key_rows = joined[0].astype(jnp.float32).reshape(total_keys, KVH, HEAD_SIZE)
    values = joined[1].astype(jnp.float32).reshape(total_keys, KVH, HEAD_SIZE)
    grouped = query_rows.astype(jnp.float32).reshape(STEPS, KVH, QUERY_HEADS // KVH, HEAD_SIZE)
    scores = jnp.einsum("skgd,tkd->skgt", grouped, key_rows) * (HEAD_SIZE ** -0.5)
    position = jnp.arange(total_keys)[None, :]
    step_ids = jnp.arange(STEPS)[:, None]
    visible = (position < PLEN) | ((position < PLEN + SUF) & (position - PLEN < length)) | ((position >= PLEN + SUF) & (position - PLEN - SUF <= step_ids))
    scores = jnp.where(visible[:, None, None, :], scores, -jnp.inf)
    row_top = jnp.max(scores, axis=-1, keepdims=True)
    exponent = jnp.exp(scores - row_top)
    weights = (exponent / jnp.sum(exponent, axis=-1, keepdims=True)).astype(jnp.bfloat16)
    attention_output = jnp.einsum("skgt,tkd->skgd", weights.astype(jnp.float32), values)
    return attention_output.reshape(STEPS, QUERY_HEADS * HEAD_SIZE).astype(jnp.bfloat16)


def apply_rollout_adapter(adapter_shrink_weight, adapter_expand_weight, bundle_member):
    rows_here, identity_value = bundle_member
    shrink_table = lax.dynamic_index_in_dim(adapter_shrink_weight, identity_value, axis=0, keepdims=False)
    expand_table = lax.dynamic_index_in_dim(adapter_expand_weight, identity_value, axis=0, keepdims=False)
    rank_features = jnp.dot(rows_here, shrink_table.T, preferred_element_type=jnp.float32).astype(jnp.bfloat16)
    return jnp.dot(rank_features, expand_table, preferred_element_type=jnp.float32).astype(jnp.bfloat16)


def reference(queries, shared_prefix_cache, rollout_suffix_cache, fresh_key_value, rollout_prefix_index, rollout_suffix_length, rollout_adapter_index, output_projection_weight, adapter_shrink_weight, adapter_expand_weight):
    bundle = 4
    groups = ROLLOUTS // bundle
    suffix_rows = jnp.moveaxis(rollout_suffix_cache, 1, 0).reshape(groups, bundle, 2, SUF, KVH * HEAD_SIZE)
    fresh_rows = jnp.moveaxis(fresh_key_value, 1, 0).reshape(groups, bundle, 2, STEPS, KVH * HEAD_SIZE)

    def attend_bundle(bundle_member):
        query_part, suffix_part, fresh_part, prefix_part, length_part = bundle_member
        return jax.vmap(partial(attend_rollout, shared_prefix_cache))(query_part, suffix_part, fresh_part, prefix_part, length_part)

    attention_output = lax.map(attend_bundle, (queries.reshape(groups, bundle, STEPS, QUERY_HEADS * HEAD_SIZE), suffix_rows, fresh_rows, rollout_prefix_index.reshape(groups, bundle), rollout_suffix_length.reshape(groups, bundle)))
    attention_output = attention_output.reshape(ROLLOUTS, STEPS, QUERY_HEADS * HEAD_SIZE)
    flat_rows = attention_output.reshape(ROLLOUTS * STEPS, QUERY_HEADS * HEAD_SIZE)
    group_width = QUERY_HEADS * HEAD_SIZE // N_TENSOR
    base_sum = jnp.zeros((ROLLOUTS * STEPS, OUTPUT_FEATURES), jnp.float32)
    for group_index in range(N_TENSOR):
        lower = group_index * group_width
        partial_sum = jnp.dot(flat_rows[:, lower:lower + group_width], output_projection_weight[lower:lower + group_width], preferred_element_type=jnp.float32)
        rounded = lax.optimization_barrier(partial_sum.astype(jnp.bfloat16))
        base_sum = base_sum + rounded.astype(jnp.float32)
    adapter_correction = lax.map(partial(apply_rollout_adapter, adapter_shrink_weight, adapter_expand_weight), (attention_output, rollout_adapter_index[:, 0]))
    mixed = base_sum.reshape(ROLLOUTS, STEPS, OUTPUT_FEATURES) + adapter_correction.astype(jnp.float32)
    return mixed.astype(jnp.bfloat16)
```

```python
import functools
import math

import jax
import jax.numpy as jnp
from jax import lax
from jax.experimental import pallas as pl
from jax.experimental.pallas import tpu as pltpu
from jax.sharding import PartitionSpec as P

HEAD_SIZE = 128
BLOCK_ROLLS = 16
KEY_CHUNK = 512
NEG = float("-inf")
MIB = 1 << 20


def dot_nt(a, b):
    return lax.dot_general(a, b, (((1,), (1,)), ((), ())), preferred_element_type=jnp.float32)


def dot_nn(a, b):
    return jnp.dot(a, b, preferred_element_type=jnp.float32)


def attend_kernel(
    code_ref, q_ref, kv_ref, suf_ref, fr_ref, o_ref, s_ref, m_ref, *, steps, group
):
    prefix_count, prefix_len = kv_ref.shape[1], kv_ref.shape[2]
    key_heads = kv_ref.shape[3] // HEAD_SIZE
    rolls, suf_len = suf_ref.shape[1], suf_ref.shape[2]
    block_rows = BLOCK_ROLLS * steps
    rows = block_rows * group
    blocks = rolls // BLOCK_ROLLS
    suf_rolls = HEAD_SIZE // suf_len
    suf_rows = suf_rolls * steps
    suf_groups = BLOCK_ROLLS // suf_rolls
    window_rolls = HEAD_SIZE // steps
    windows = window_rolls // BLOCK_ROLLS
    factor = HEAD_SIZE ** (-0.5) * math.log2(math.e)
    chunks = prefix_len // KEY_CHUNK
    span = prefix_len

    def row_codes(block):
        shape = (block_rows, rolls)
        mine = block * BLOCK_ROLLS + lax.broadcasted_iota(jnp.int32, shape, 0) // steps
        lane = lax.broadcasted_iota(jnp.int32, shape, 1)
        code = jnp.broadcast_to(code_ref[...].astype(jnp.float32), shape)
        col = jnp.sum(jnp.where(mine == lane, code, 0.0), axis=1, keepdims=True)
        col = jnp.broadcast_to(col, (block_rows, HEAD_SIZE)).astype(jnp.int32)
        return col // prefix_count, col % prefix_count

    def tile_rows(x):
        return jnp.concatenate([x] * group, axis=0)

    def load_q(block, h):
        start = pl.multiple_of(block * block_rows, block_rows)
        return [
            q_ref[pl.ds(start, block_rows), pl.ds((h * group + g) * HEAD_SIZE, HEAD_SIZE)]
            for g in range(group)
        ]

    def head_lanes(h):
        return pl.ds(h * HEAD_SIZE, HEAD_SIZE)

    def suffix_tile(which, block, i, h):
        start = block * BLOCK_ROLLS + i * suf_rolls
        tile = suf_ref[which, pl.ds(start, suf_rolls), :, head_lanes(h)]
        return tile.reshape(HEAD_SIZE, HEAD_SIZE)

    def fresh_tile(which, block, h):
        start = pl.multiple_of(block // windows * HEAD_SIZE, HEAD_SIZE)
        return fr_ref[which, pl.ds(start, HEAD_SIZE), head_lanes(h)]

    def prefix_tile(which, c, h):
        return jnp.concatenate(
            [
                kv_ref[which, p, pl.ds(c * KEY_CHUNK, KEY_CHUNK), head_lanes(h)]
                for p in range(prefix_count)
            ],
            axis=1,
        )

    def scores(block, h, slot):
        length, local = row_codes(block)
        parts = load_q(block, h)
        stacked = jnp.concatenate(parts, axis=0)
        wide = jnp.concatenate(
            [
                jnp.concatenate(
                    [jnp.where(local == p, x, jnp.zeros_like(x)) for x in parts], axis=0
                )
                for p in range(prefix_count)
            ],
            axis=1,
        )
        shape = (block_rows, HEAD_SIZE)
        row = lax.broadcasted_iota(jnp.int32, shape, 0)
        lane = lax.broadcasted_iota(jnp.int32, shape, 1)
        roll = row // steps
        keep = (roll % suf_rolls == lane // suf_len) & (lane % suf_len < length)
        suf_bias = jnp.where(keep, 0.0, NEG)
        in_window = (block % windows) * BLOCK_ROLLS + roll
        keep = (in_window == lane // steps) & (lane % steps <= row % steps)
        fr_bias = jnp.where(keep, 0.0, NEG)
        suf = []
        for i in range(suf_groups):
            piece = jnp.concatenate(
                [x[i * suf_rows : (i + 1) * suf_rows] for x in parts], axis=0
            )
            suf.append(dot_nt(piece, suffix_tile(0, block, i, h)))
        suf = jnp.concatenate(
            [
                jnp.concatenate([x[g * suf_rows : (g + 1) * suf_rows] for x in suf], axis=0)
                for g in range(group)
            ],
            axis=0,
        ) + tile_rows(suf_bias)
        fr = dot_nt(stacked, fresh_tile(0, block, h)) + tile_rows(fr_bias)
        s_ref[slot, :, pl.ds(span, HEAD_SIZE)] = suf
        s_ref[slot, :, pl.ds(span + HEAD_SIZE, HEAD_SIZE)] = fr
        top = jnp.maximum(suf, fr)
        yield
        for c in range(chunks):
            s = dot_nt(wide, prefix_tile(0, c, h))
            s_ref[slot, :, pl.ds(c * KEY_CHUNK, KEY_CHUNK)] = s
            for j in range(KEY_CHUNK // HEAD_SIZE):
                top = jnp.maximum(top, s[:, j * HEAD_SIZE : (j + 1) * HEAD_SIZE])
            if c == chunks - 1:
                top = jnp.max(top, axis=1, keepdims=True) * factor
                m_ref[slot] = jnp.broadcast_to(top, (rows, HEAD_SIZE))
            yield

    def outputs(block, h, slot):
        top = m_ref[slot]

        def weigh(start, width):
            x = s_ref[slot, :, pl.ds(start, width)]
            wide_top = jnp.concatenate([top] * (width // HEAD_SIZE), axis=1)
            return jnp.exp2(x * factor - wide_top)

        both = weigh(span, 2 * HEAD_SIZE)
        total = both[:, :HEAD_SIZE] + both[:, HEAD_SIZE:]
        both = both.astype(jnp.bfloat16)
        fr = dot_nn(both[:, HEAD_SIZE:], fresh_tile(1, block, h))
        suf = []
        for i in range(suf_groups):
            piece = jnp.concatenate(
                [
                    both[
                        g * block_rows + i * suf_rows : g * block_rows + (i + 1) * suf_rows,
                        :HEAD_SIZE,
                    ]
                    for g in range(group)
                ],
                axis=0,
            )
            suf.append(dot_nn(piece, suffix_tile(1, block, i, h)))
        extra = fr + jnp.concatenate(
            [
                jnp.concatenate([x[g * suf_rows : (g + 1) * suf_rows] for x in suf], axis=0)
                for g in range(group)
            ],
            axis=0,
        )
        yield
        acc = None
        for c in range(chunks):
            p = weigh(c * KEY_CHUNK, KEY_CHUNK)
            for j in range(KEY_CHUNK // HEAD_SIZE):
                total = total + p[:, j * HEAD_SIZE : (j + 1) * HEAD_SIZE]
            part = dot_nn(p.astype(jnp.bfloat16), prefix_tile(1, c, h))
            acc = part if acc is None else acc + part
            if c == chunks - 1:
                _, local = row_codes(block)
                local = tile_rows(local)
                chosen = acc[:, :HEAD_SIZE]
                for q in range(1, prefix_count):
                    chosen = jnp.where(
                        local == q, acc[:, q * HEAD_SIZE : (q + 1) * HEAD_SIZE], chosen
                    )
                weight = 1.0 / jnp.sum(total, axis=1, keepdims=True)
                out = ((chosen + extra) * weight).astype(o_ref.dtype)
                start = pl.multiple_of(block * block_rows, block_rows)
                for g in range(group):
                    o_ref[
                        pl.ds(start, block_rows),
                        pl.ds((h * group + g) * HEAD_SIZE, HEAD_SIZE),
                    ] = out[g * block_rows : (g + 1) * block_rows]
            yield

    def run(*streams):
        for _ in range(chunks + 1):
            for stream in streams:
                next(stream)

    run(scores(0, 0, 0))

    def body(block, carry):
        for h in range(key_heads):
            if h + 1 < key_heads:
                run(scores(block, h + 1, h + 1), outputs(block, h, h))
            elif key_heads > 1:
                following = jnp.minimum(block + 1, blocks - 1)
                run(scores(following, 0, 0), outputs(block, h, h))
            else:
                run(outputs(block, h, h))
                run(scores(jnp.minimum(block + 1, blocks - 1), 0, 0))
        return carry

    lax.fori_loop(0, blocks, body, 0)


def attend(code, queries, prefix, suffix, fresh, steps):
    rows, width = queries.shape
    key_heads = prefix.shape[3] // HEAD_SIZE
    group = width // HEAD_SIZE // key_heads
    unit_rows = BLOCK_ROLLS * steps * group
    span = prefix.shape[2] + 2 * HEAD_SIZE
    elements = rows * width // HEAD_SIZE * prefix.shape[2]
    vmem = pl.BlockSpec(memory_space=pltpu.VMEM)
    return pl.pallas_call(
        functools.partial(attend_kernel, steps=steps, group=group),
        out_shape=jax.ShapeDtypeStruct((rows, width), jnp.bfloat16),
        in_specs=[vmem] * 5,
        out_specs=vmem,
        scratch_shapes=[
            pltpu.VMEM((key_heads, unit_rows, span), jnp.float32),
            pltpu.VMEM((key_heads, unit_rows, HEAD_SIZE), jnp.float32),
        ],
        compiler_params=pltpu.CompilerParams(vmem_limit_bytes=40 * MIB),
        cost_estimate=pl.CostEstimate(
            flops=elements * 8 * HEAD_SIZE, bytes_accessed=12 * MIB, transcendentals=elements
        ),
    )(code, queries, prefix, suffix, fresh)


def local(
    queries,
    shared_prefix_cache,
    rollout_suffix_cache,
    fresh_key_value,
    rollout_prefix_index,
    rollout_suffix_length,
    rollout_adapter_index,
    output_projection_weight,
    adapter_shrink_weight,
    adapter_expand_weight,
):
    rolls, steps, width = queries.shape
    rows = rolls * steps
    prefix_count = shared_prefix_cache.shape[1]
    rank, out_width = adapter_expand_weight.shape[1:]
    shrink = lax.all_gather(adapter_shrink_weight, "adapter", axis=0, tiled=True)
    expand = lax.all_gather(adapter_expand_weight, "adapter", axis=0, tiled=True)
    adapters = shrink.shape[0]
    shrink = shrink.reshape(adapters * rank, width)
    expand = expand.reshape(adapters * rank, out_width)
    code = rollout_suffix_length * prefix_count + rollout_prefix_index % prefix_count
    attended = attend(
        code[None, :],
        queries.reshape(rows, width),
        shared_prefix_cache,
        rollout_suffix_cache,
        fresh_key_value.reshape(2, rows, -1),
        steps,
    )
    partial_sum = jnp.dot(
        attended, output_projection_weight, preferred_element_type=jnp.float32
    ).astype(jnp.bfloat16)
    base = lax.psum_scatter(partial_sum, "tensor", scatter_dimension=1, tiled=True)
    row_adapter = jnp.repeat(rollout_adapter_index[:, 0], steps)
    mine = row_adapter[:, None] == jnp.arange(adapters, dtype=jnp.int32)[None, :]
    every = lax.dot_general(
        attended, shrink, (((1,), (1,)), ((), ())), preferred_element_type=jnp.float32
    ).reshape(rows, adapters, rank)
    codes = jnp.sum(jnp.where(mine[:, :, None], every, 0.0), axis=1)
    codes = lax.psum(codes.astype(jnp.bfloat16), "tensor")
    spread = jnp.where(mine[:, :, None], codes[:, None, :], jnp.zeros((), jnp.bfloat16))
    delta = jnp.dot(
        spread.reshape(rows, adapters * rank), expand, preferred_element_type=jnp.float32
    )
    mixed = base.astype(jnp.float32) + delta.astype(jnp.bfloat16).astype(jnp.float32)
    return mixed.astype(jnp.bfloat16).reshape(rolls, steps, out_width)


def solution(mesh):
    placed = (
        P("adapter", None, "tensor"),
        P(None, "adapter", None, "tensor"),
        P(None, "adapter", None, "tensor"),
        P(None, "adapter", None, "tensor"),
        P("adapter"),
        P("adapter"),
        P("adapter", None),
        P("tensor", None),
        P("adapter", None, "tensor"),
        P("adapter", None, "tensor"),
    )
    return jax.shard_map(
        local, mesh=mesh, in_specs=placed, out_specs=P("adapter", None, "tensor"), check_vma=False
    )
```

```python
import functools
import math

import jax
import jax.numpy as jnp
from jax import lax
from jax.experimental import pallas as pl
from jax.experimental.pallas import tpu as pltpu
from jax.sharding import PartitionSpec as P

HEAD_SIZE = 128
MOST = 5
FOLD = 2
PARTS = 2
BLOCK_ROLLS = 16
KEY_CHUNK = 512
NEG = float("-inf")
MIB = 1 << 20
BRIEF = pl.CostEstimate(flops=1024, bytes_accessed=1024, transcendentals=0)
VMEM = pl.BlockSpec(memory_space=pltpu.VMEM)


def dot_nt(a, b):
    return lax.dot_general(a, b, (((1,), (1,)), ((), ())), preferred_element_type=jnp.float32)


def dot_nn(a, b):
    return jnp.dot(a, b, preferred_element_type=jnp.float32)


def attend_kernel(
    code_ref, q_ref, kv_ref, suf_ref, fr_ref, o_ref, s_ref, m_ref, *, steps, group, first, blocks
):
    prefix_count, prefix_len = kv_ref.shape[1], kv_ref.shape[2]
    key_heads = kv_ref.shape[3] // HEAD_SIZE
    rolls, suf_len = suf_ref.shape[1], suf_ref.shape[2]
    block_rows = BLOCK_ROLLS * steps
    rows = block_rows * group
    last = first + blocks - 1
    suf_rolls = HEAD_SIZE // suf_len
    suf_rows = suf_rolls * steps
    suf_groups = BLOCK_ROLLS // suf_rolls
    window_rolls = HEAD_SIZE // steps
    windows = window_rolls // BLOCK_ROLLS
    factor = HEAD_SIZE ** (-0.5) * math.log2(math.e)
    chunks = prefix_len // KEY_CHUNK
    span = prefix_len

    def row_codes(block):
        shape = (block_rows, rolls)
        mine = block * BLOCK_ROLLS + lax.broadcasted_iota(jnp.int32, shape, 0) // steps
        lane = lax.broadcasted_iota(jnp.int32, shape, 1)
        code = jnp.broadcast_to(code_ref[...].astype(jnp.float32), shape)
        col = jnp.sum(jnp.where(mine == lane, code, 0.0), axis=1, keepdims=True)
        col = jnp.broadcast_to(col, (block_rows, HEAD_SIZE)).astype(jnp.int32)
        return col // prefix_count, col % prefix_count

    def tile_rows(x):
        return jnp.concatenate([x] * group, axis=0)

    def load_q(block, h):
        start = pl.multiple_of(block * block_rows, block_rows)
        return [
            q_ref[pl.ds(start, block_rows), pl.ds((h * group + g) * HEAD_SIZE, HEAD_SIZE)]
            for g in range(group)
        ]

    def head_lanes(h):
        return pl.ds(h * HEAD_SIZE, HEAD_SIZE)

    def suffix_tile(which, block, i, h):
        start = block * BLOCK_ROLLS + i * suf_rolls
        tile = suf_ref[which, pl.ds(start, suf_rolls), :, head_lanes(h)]
        return tile.reshape(HEAD_SIZE, HEAD_SIZE)

    def fresh_tile(which, block, h):
        start = pl.multiple_of(block // windows * HEAD_SIZE, HEAD_SIZE)
        return fr_ref[which, pl.ds(start, HEAD_SIZE), head_lanes(h)]

    def prefix_tile(which, c, h):
        return jnp.concatenate(
            [
                kv_ref[which, p, pl.ds(c * KEY_CHUNK, KEY_CHUNK), head_lanes(h)]
                for p in range(prefix_count)
            ],
            axis=1,
        )

    def scores(block, h, slot):
        length, local = row_codes(block)
        parts = load_q(block, h)
        stacked = jnp.concatenate(parts, axis=0)
        wide = jnp.concatenate(
            [
                jnp.concatenate(
                    [jnp.where(local == p, x, jnp.zeros_like(x)) for x in parts], axis=0
                )
                for p in range(prefix_count)
            ],
            axis=1,
        )
        shape = (block_rows, HEAD_SIZE)
        row = lax.broadcasted_iota(jnp.int32, shape, 0)
        lane = lax.broadcasted_iota(jnp.int32, shape, 1)
        roll = row // steps
        keep = (roll % suf_rolls == lane // suf_len) & (lane % suf_len < length)
        suf_bias = jnp.where(keep, 0.0, NEG)
        in_window = (block % windows) * BLOCK_ROLLS + roll
        keep = (in_window == lane // steps) & (lane % steps <= row % steps)
        fr_bias = jnp.where(keep, 0.0, NEG)
        suf = []
        for i in range(suf_groups):
            piece = jnp.concatenate(
                [x[i * suf_rows : (i + 1) * suf_rows] for x in parts], axis=0
            )
            suf.append(dot_nt(piece, suffix_tile(0, block, i, h)))
        suf = jnp.concatenate(
            [
                jnp.concatenate([x[g * suf_rows : (g + 1) * suf_rows] for x in suf], axis=0)
                for g in range(group)
            ],
            axis=0,
        ) + tile_rows(suf_bias)
        fr = dot_nt(stacked, fresh_tile(0, block, h)) + tile_rows(fr_bias)
        s_ref[slot, :, pl.ds(span, HEAD_SIZE)] = suf
        s_ref[slot, :, pl.ds(span + HEAD_SIZE, HEAD_SIZE)] = fr
        top = jnp.maximum(suf, fr)
        yield
        for c in range(chunks):
            s = dot_nt(wide, prefix_tile(0, c, h))
            s_ref[slot, :, pl.ds(c * KEY_CHUNK, KEY_CHUNK)] = s
            for j in range(KEY_CHUNK // HEAD_SIZE):
                top = jnp.maximum(top, s[:, j * HEAD_SIZE : (j + 1) * HEAD_SIZE])
            if c == chunks - 1:
                top = jnp.max(top, axis=1, keepdims=True) * factor
                m_ref[slot] = jnp.broadcast_to(top, (rows, HEAD_SIZE))
            yield

    def outputs(block, h, slot):
        top = m_ref[slot]

        def weigh(start, width):
            x = s_ref[slot, :, pl.ds(start, width)]
            wide_top = jnp.concatenate([top] * (width // HEAD_SIZE), axis=1)
            return jnp.exp2(x * factor - wide_top)

        both = weigh(span, 2 * HEAD_SIZE)
        total = both[:, :HEAD_SIZE] + both[:, HEAD_SIZE:]
        both = both.astype(jnp.bfloat16)
        fr = dot_nn(both[:, HEAD_SIZE:], fresh_tile(1, block, h))
        suf = []
        for i in range(suf_groups):
            piece = jnp.concatenate(
                [
                    both[
                        g * block_rows + i * suf_rows : g * block_rows + (i + 1) * suf_rows,
                        :HEAD_SIZE,
                    ]
                    for g in range(group)
                ],
                axis=0,
            )
            suf.append(dot_nn(piece, suffix_tile(1, block, i, h)))
        extra = fr + jnp.concatenate(
            [
                jnp.concatenate([x[g * suf_rows : (g + 1) * suf_rows] for x in suf], axis=0)
                for g in range(group)
            ],
            axis=0,
        )
        yield
        acc = None
        for c in range(chunks):
            p = weigh(c * KEY_CHUNK, KEY_CHUNK)
            for j in range(KEY_CHUNK // HEAD_SIZE):
                total = total + p[:, j * HEAD_SIZE : (j + 1) * HEAD_SIZE]
            part = dot_nn(p.astype(jnp.bfloat16), prefix_tile(1, c, h))
            acc = part if acc is None else acc + part
            if c == chunks - 1:
                _, local = row_codes(block)
                local = tile_rows(local)
                chosen = acc[:, :HEAD_SIZE]
                for q in range(1, prefix_count):
                    chosen = jnp.where(
                        local == q, acc[:, q * HEAD_SIZE : (q + 1) * HEAD_SIZE], chosen
                    )
                weight = 1.0 / jnp.sum(total, axis=1, keepdims=True)
                out = ((chosen + extra) * weight).astype(o_ref.dtype)
                start = pl.multiple_of((block - first) * block_rows, block_rows)
                for g in range(group):
                    o_ref[
                        pl.ds(start, block_rows),
                        pl.ds((h * group + g) * HEAD_SIZE, HEAD_SIZE),
                    ] = out[g * block_rows : (g + 1) * block_rows]
            yield

    def run(*streams):
        for _ in range(chunks + 1):
            for stream in streams:
                next(stream)

    run(scores(first, 0, 0))

    def body(block, carry):
        for h in range(key_heads):
            if h + 1 < key_heads:
                run(scores(block, h + 1, h + 1), outputs(block, h, h))
            elif key_heads > 1:
                following = jnp.minimum(block + 1, last)
                run(scores(following, 0, 0), outputs(block, h, h))
            else:
                run(outputs(block, h, h))
                run(scores(jnp.minimum(block + 1, last), 0, 0))
        return carry

    lax.fori_loop(first, first + blocks, body, 0)


def attend(code, queries, prefix, suffix, fresh, steps, part):
    rows, width = queries.shape
    rows = rows // PARTS
    key_heads = prefix.shape[3] // HEAD_SIZE
    group = width // HEAD_SIZE // key_heads
    unit_rows = BLOCK_ROLLS * steps * group
    span = prefix.shape[2] + 2 * HEAD_SIZE
    blocks = suffix.shape[1] // BLOCK_ROLLS // PARTS
    return pl.pallas_call(
        functools.partial(
            attend_kernel, steps=steps, group=group, first=part * blocks, blocks=blocks
        ),
        out_shape=jax.ShapeDtypeStruct((rows, width), jnp.bfloat16),
        in_specs=[VMEM] * 5,
        out_specs=VMEM,
        scratch_shapes=[
            pltpu.VMEM((key_heads, unit_rows, span), jnp.float32),
            pltpu.VMEM((key_heads, unit_rows, HEAD_SIZE), jnp.float32),
        ],
        compiler_params=pltpu.CompilerParams(vmem_limit_bytes=30 * MIB),
        cost_estimate=BRIEF,
    )(code, queries, prefix, suffix, fresh)


def project_kernel(core_ref, a_ref, w_ref, send_ref, keep_ref, *, count):
    step = pl.program_id(0)
    part = dot_nn(a_ref[...], w_ref[...]).astype(jnp.bfloat16)

    @pl.when(step < count)
    def _():
        send_ref[0] = part

    @pl.when(step >= count)
    def _():
        keep_ref[0] = part


def project(core, attended, weight, out_width):
    rows, width = attended.shape
    count = weight.shape[1] // out_width // 2

    def column(j, core):
        parity = jnp.where(j < count, 1 - core[0], core[0])
        return (0, (j % count) * 2 + parity)

    shape = jax.ShapeDtypeStruct((count, rows, out_width), jnp.bfloat16)
    return pl.pallas_call(
        functools.partial(project_kernel, count=count),
        grid_spec=pltpu.PrefetchScalarGridSpec(
            num_scalar_prefetch=1,
            grid=(2 * count,),
            in_specs=[
                pl.BlockSpec((rows, width), lambda j, core: (0, 0)),
                pl.BlockSpec((width, out_width), column),
            ],
            out_specs=[
                pl.BlockSpec((1, rows, out_width), lambda j, core: (jnp.minimum(j, count - 1), 0, 0)),
                pl.BlockSpec((1, rows, out_width), lambda j, core: (jnp.maximum(j - count, 0), 0, 0)),
            ],
        ),
        out_shape=[shape, shape],
        compiler_params=pltpu.CompilerParams(vmem_limit_bytes=24 * MIB),
        cost_estimate=BRIEF,
    )(core, attended, weight)


def pack_kernel(target_ref, *refs):
    parts, outs = refs[:PARTS], refs[PARTS:]
    slots = outs[0].shape[0]
    part_rows = parts[0].shape[0]
    for d, out in enumerate(outs):
        total = None
        for k, part in enumerate(parts):
            row = d * slots + lax.broadcasted_iota(jnp.int32, (slots, part_rows), 0)
            chosen = row == target_ref[:, k * part_rows : (k + 1) * part_rows]
            term = dot_nn(jnp.where(chosen, 1.0, 0.0).astype(jnp.bfloat16), part[...])
            total = term if total is None else total + term
        out[...] = total.astype(jnp.bfloat16)


def pack(target, parts, count, slots):
    rows, width = parts[0].shape
    return pl.pallas_call(
        pack_kernel,
        out_shape=[jax.ShapeDtypeStruct((slots, width), jnp.bfloat16)] * count,
        in_specs=[VMEM] * (1 + len(parts)),
        out_specs=[VMEM] * count,
        compiler_params=pltpu.CompilerParams(vmem_limit_bytes=24 * MIB),
        cost_estimate=BRIEF,
    )(target, *parts)


def adapter_mask(rows, per_adapter, rank, tile):
    lane = lax.broadcasted_iota(jnp.int32, (rows, HEAD_SIZE), 1) + tile * HEAD_SIZE
    row = lax.broadcasted_iota(jnp.int32, (rows, HEAD_SIZE), 0)
    return lane // rank == row // per_adapter


def shrink_kernel(*refs, per_adapter, rank, count):
    weights, pieces, out = refs[:FOLD], refs[FOLD : FOLD + count], refs[-1]
    rows = pieces[0].shape[0] // FOLD
    for k in range(FOLD):
        span = pl.ds(k * rows, rows)
        every = dot_nt(
            jnp.concatenate([p[span, :] for p in pieces], axis=0),
            weights[k][...],
        )
        for d in range(count):
            total = None
            for tile in range(every.shape[1] // HEAD_SIZE):
                x = every[d * rows : (d + 1) * rows, tile * HEAD_SIZE : (tile + 1) * HEAD_SIZE]
                x = jnp.where(adapter_mask(rows, per_adapter, rank, tile), x, 0.0)
                total = x if total is None else total + x
            summed = total
            for turn in range(1, HEAD_SIZE // rank):
                summed = summed + pltpu.roll(total, turn * rank, axis=1)
            out[pl.ds((d * FOLD + k) * rows, rows), :] = summed


def shrink_rows(weights, pieces, per_adapter, rank):
    count = len(pieces)
    rows, width = pieces[0].shape
    return pl.pallas_call(
        functools.partial(shrink_kernel, per_adapter=per_adapter, rank=rank, count=count),
        out_shape=jax.ShapeDtypeStruct((count * rows, HEAD_SIZE), jnp.float32),
        in_specs=[VMEM] * (FOLD + count),
        out_specs=VMEM,
        compiler_params=pltpu.CompilerParams(vmem_limit_bytes=24 * MIB),
        cost_estimate=BRIEF,
    )(*weights, *pieces)


def expand_kernel(*refs, per_adapter, rank, count, terms):
    weights, sums, outs = refs[:FOLD], refs[FOLD : FOLD + terms], refs[FOLD + terms :]
    depth = weights[0].shape[0]
    rows = outs[0].shape[0] // FOLD
    for k in range(FOLD):
        spread = []
        for d in range(count):
            span = pl.ds((d * FOLD + k) * rows, rows)
            code = sums[0][span, :].astype(jnp.float32)
            for other in sums[1:]:
                code = code + other[span, :].astype(jnp.float32)
            spread.append(
                jnp.concatenate(
                    [
                        jnp.where(adapter_mask(rows, per_adapter, rank, tile), code, 0.0)
                        for tile in range(depth // HEAD_SIZE)
                    ],
                    axis=1,
                ).astype(jnp.bfloat16)
            )
        wide = dot_nn(jnp.concatenate(spread, axis=0), weights[k][...])
        wide = wide.astype(jnp.bfloat16)
        for d in range(count):
            outs[d][pl.ds(k * rows, rows), :] = wide[d * rows : (d + 1) * rows]


def expand_rows(weights, sums, per_adapter, rank, count):
    rows = sums[0].shape[0] // count
    width = weights[0].shape[1]
    return pl.pallas_call(
        functools.partial(
            expand_kernel, per_adapter=per_adapter, rank=rank, count=count, terms=len(sums)
        ),
        out_shape=[jax.ShapeDtypeStruct((rows, width), jnp.bfloat16)] * count,
        in_specs=[VMEM] * (FOLD + len(sums)),
        out_specs=[VMEM] * count,
        compiler_params=pltpu.CompilerParams(vmem_limit_bytes=24 * MIB),
        cost_estimate=BRIEF,
    )(*weights, *sums)


def combine_kernel(target_ref, *refs, count, terms):
    pieces, sums, out = refs[:count], refs[count:-1], refs[-1]
    slots = pieces[0].shape[0]
    part_rows = out.shape[0] // PARTS
    for k in range(PARTS):
        target = target_ref[pl.ds(k * part_rows, part_rows), :]
        delta = None
        for d, piece in enumerate(pieces):
            slot = d * slots + lax.broadcasted_iota(jnp.int32, (part_rows, slots), 1)
            chosen = jnp.where(target == slot, 1.0, 0.0).astype(jnp.bfloat16)
            term = dot_nn(chosen, piece[...])
            delta = term if delta is None else delta + term
        for x in sums[k * terms : (k + 1) * terms]:
            delta = delta + x[...].astype(jnp.float32)
        out[pl.ds(k * part_rows, part_rows), :] = delta.astype(jnp.bfloat16)


def combine(target, pieces, sums):
    terms = len(sums[0])
    part_rows, width = sums[0][0].shape
    count = len(pieces)
    flat = [x for part in sums for x in part]
    rows = part_rows * len(sums)
    return pl.pallas_call(
        functools.partial(combine_kernel, count=count, terms=terms),
        out_shape=jax.ShapeDtypeStruct((rows, width), jnp.bfloat16),
        in_specs=[VMEM] * (1 + count + len(flat)),
        out_specs=VMEM,
        compiler_params=pltpu.CompilerParams(vmem_limit_bytes=24 * MIB),
        cost_estimate=BRIEF,
    )(target, *pieces, *flat)


def local(
    queries,
    shared_prefix_cache,
    rollout_suffix_cache,
    fresh_key_value,
    rollout_prefix_index,
    rollout_suffix_length,
    rollout_adapter_index,
    output_projection_weight,
    adapter_shrink_weight,
    adapter_expand_weight,
):
    rolls, steps, width = queries.shape
    rows = rolls * steps
    prefix_count = shared_prefix_cache.shape[1]
    resident, rank, out_width = adapter_expand_weight.shape
    holders, sides = lax.axis_size("adapter"), lax.axis_size("tensor")
    block, chips = holders // FOLD, sides // 2
    here, side = lax.axis_index("adapter"), lax.axis_index("tensor")
    chip, core = side // 2, side % 2

    def in_block(shift):
        return [(i, i // block * block + (i + shift) % block) for i in range(holders)]

    cores = [(t, t // 2 * 2 + (t + 1) % 2) for t in range(sides)]

    def over_chips(shift):
        return [(t, (t // 2 + shift) % chips * 2 + t % 2) for t in range(sides)]

    own_shrink = adapter_shrink_weight.reshape(resident * rank, width)
    own_expand = adapter_expand_weight.reshape(resident * rank, out_width)
    shrinks, expands = [own_shrink], [own_expand]
    for fold in range(1, FOLD):
        far = [(i, (i + fold * block) % holders) for i in range(holders)]
        shrinks.append(lax.ppermute(own_shrink, "adapter", far))
        expands.append(lax.ppermute(own_expand, "adapter", far))

    adapter = rollout_adapter_index[:, 0]
    holder = adapter // resident
    order = jnp.arange(rolls, dtype=jnp.int32)
    same = (adapter[:, None] == adapter[None, :]) & (order[None, :] < order[:, None])
    turn = jnp.sum(same.astype(jnp.int32), axis=1)
    fold = (here // block - holder // block) % FOLD
    place = (holder % block - here % block) % block
    slot = ((place * FOLD + fold) * resident + adapter % resident) * MOST + turn
    target = (slot[:, None] * steps + jnp.arange(steps, dtype=jnp.int32)[None, :]).reshape(rows)
    slots = FOLD * resident * MOST * steps
    per_adapter = MOST * steps

    code = (rollout_suffix_length * prefix_count + rollout_prefix_index % prefix_count)[None, :]
    flat_queries = queries.reshape(rows, width)
    flat_fresh = fresh_key_value.reshape(2, rows, -1)
    core_index = core.reshape(1).astype(jnp.int32)
    parts, sums = [], []
    for part in range(PARTS):
        attended = attend(
            code, flat_queries, shared_prefix_cache, rollout_suffix_cache, flat_fresh, steps, part
        )
        parts.append(attended)
        send, keep = project(core_index, attended, output_projection_weight, out_width)
        pair = keep.astype(jnp.float32) + lax.ppermute(send, "tensor", cores).astype(jnp.float32)
        terms = [lax.dynamic_index_in_dim(pair, chip, 0, keepdims=False).astype(jnp.bfloat16)]
        for shift in range(1, chips):
            away = lax.dynamic_index_in_dim(pair, (chip + shift) % chips, 0, keepdims=False)
            terms.append(lax.ppermute(away.astype(jnp.bfloat16), "tensor", over_chips(shift)))
        sums.append(terms)

    parts[-1], *shrinks[1:] = lax.optimization_barrier([parts[-1]] + shrinks[1:])
    packed = pack(target[None, :], parts, block, slots)
    pieces = [packed[0]] + [
        lax.ppermute(packed[d], "adapter", in_block(d)) for d in range(1, block)
    ]
    pieces[0], *expands[1:] = lax.optimization_barrier([pieces[0]] + expands[1:])
    codes = shrink_rows(shrinks, pieces, per_adapter, rank)
    codes = codes + lax.ppermute(codes, "tensor", cores)
    brief = codes.astype(jnp.bfloat16)
    codes = [brief] + [lax.ppermute(brief, "tensor", over_chips(s)) for s in range(1, chips)]
    wide = expand_rows(expands, codes, per_adapter, rank, block)
    back = [wide[0]] + [
        lax.ppermute(wide[d], "adapter", in_block(block - d)) for d in range(1, block)
    ]
    mixed = combine(target[:, None], back, sums)
    return mixed.reshape(rolls, steps, out_width)


def solution(mesh):
    placed = (
        P("adapter", None, "tensor"),
        P(None, "adapter", None, "tensor"),
        P(None, "adapter", None, "tensor"),
        P(None, "adapter", None, "tensor"),
        P("adapter"),
        P("adapter"),
        P("adapter", None),
        P("tensor", None),
        P("adapter", None, "tensor"),
        P("adapter", None, "tensor"),
    )
    return jax.shard_map(
        local, mesh=mesh, in_specs=placed, out_specs=P("adapter", None, "tensor"), check_vma=False
    )
```

```python
import functools
import math

import jax
import jax.numpy as jnp
from jax import lax
from jax.experimental import pallas as pl
from jax.experimental.pallas import tpu as pltpu
from jax.sharding import PartitionSpec as P

HEAD_SIZE = 128
MOST = 5
FOLD = 2
CUTS = 2
PARTS = 2
BLOCK_ROLLS = 16
KEY_CHUNK = 512
NEG = float("-inf")
MIB = 1 << 20
BRIEF = pl.CostEstimate(flops=1024, bytes_accessed=1024, transcendentals=0)
LENGTHY = pl.CostEstimate(flops=1 << 33, bytes_accessed=1 << 24, transcendentals=0)
VMEM = pl.BlockSpec(memory_space=pltpu.VMEM)


def dot_nt(a, b):
    return lax.dot_general(a, b, (((1,), (1,)), ((), ())), preferred_element_type=jnp.float32)


def dot_nn(a, b):
    return jnp.dot(a, b, preferred_element_type=jnp.float32)


def attend_kernel(
    code_ref, q_ref, kv_ref, suf_ref, fr_ref, o_ref, s_ref, m_ref, *, steps, group, first, blocks
):
    prefix_count, prefix_len = kv_ref.shape[1], kv_ref.shape[2]
    key_heads = kv_ref.shape[3] // HEAD_SIZE
    rolls, suf_len = suf_ref.shape[1], suf_ref.shape[2]
    block_rows = BLOCK_ROLLS * steps
    rows = block_rows * group
    last = first + blocks - 1
    suf_rolls = HEAD_SIZE // suf_len
    suf_rows = suf_rolls * steps
    suf_groups = BLOCK_ROLLS // suf_rolls
    window_rolls = HEAD_SIZE // steps
    windows = window_rolls // BLOCK_ROLLS
    factor = HEAD_SIZE ** (-0.5) * math.log2(math.e)
    chunks = prefix_len // KEY_CHUNK
    span = prefix_len

    def row_codes(block):
        shape = (block_rows, rolls)
        mine = block * BLOCK_ROLLS + lax.broadcasted_iota(jnp.int32, shape, 0) // steps
        lane = lax.broadcasted_iota(jnp.int32, shape, 1)
        code = jnp.broadcast_to(code_ref[...].astype(jnp.float32), shape)
        col = jnp.sum(jnp.where(mine == lane, code, 0.0), axis=1, keepdims=True)
        col = jnp.broadcast_to(col, (block_rows, HEAD_SIZE)).astype(jnp.int32)
        return col // prefix_count, col % prefix_count

    def tile_rows(x):
        return jnp.concatenate([x] * group, axis=0)

    def load_q(block, h):
        start = pl.multiple_of(block * block_rows, block_rows)
        return [
            q_ref[pl.ds(start, block_rows), pl.ds((h * group + g) * HEAD_SIZE, HEAD_SIZE)]
            for g in range(group)
        ]

    def head_lanes(h):
        return pl.ds(h * HEAD_SIZE, HEAD_SIZE)

    def suffix_tile(which, block, i, h):
        start = block * BLOCK_ROLLS + i * suf_rolls
        tile = suf_ref[which, pl.ds(start, suf_rolls), :, head_lanes(h)]
        return tile.reshape(HEAD_SIZE, HEAD_SIZE)

    def fresh_tile(which, block, h):
        start = pl.multiple_of(block // windows * HEAD_SIZE, HEAD_SIZE)
        return fr_ref[which, pl.ds(start, HEAD_SIZE), head_lanes(h)]

    def prefix_tile(which, c, h):
        return jnp.concatenate(
            [
                kv_ref[which, p, pl.ds(c * KEY_CHUNK, KEY_CHUNK), head_lanes(h)]
                for p in range(prefix_count)
            ],
            axis=1,
        )

    def scores(block, h, slot):
        length, local = row_codes(block)
        parts = load_q(block, h)
        stacked = jnp.concatenate(parts, axis=0)
        wide = jnp.concatenate(
            [
                jnp.concatenate(
                    [jnp.where(local == p, x, jnp.zeros_like(x)) for x in parts], axis=0
                )
                for p in range(prefix_count)
            ],
            axis=1,
        )
        shape = (block_rows, HEAD_SIZE)
        row = lax.broadcasted_iota(jnp.int32, shape, 0)
        lane = lax.broadcasted_iota(jnp.int32, shape, 1)
        roll = row // steps
        keep = (roll % suf_rolls == lane // suf_len) & (lane % suf_len < length)
        suf_bias = jnp.where(keep, 0.0, NEG)
        in_window = (block % windows) * BLOCK_ROLLS + roll
        keep = (in_window == lane // steps) & (lane % steps <= row % steps)
        fr_bias = jnp.where(keep, 0.0, NEG)
        suf = []
        for i in range(suf_groups):
            piece = jnp.concatenate(
                [x[i * suf_rows : (i + 1) * suf_rows] for x in parts], axis=0
            )
            suf.append(dot_nt(piece, suffix_tile(0, block, i, h)))
        suf = jnp.concatenate(
            [
                jnp.concatenate([x[g * suf_rows : (g + 1) * suf_rows] for x in suf], axis=0)
                for g in range(group)
            ],
            axis=0,
        ) + tile_rows(suf_bias)
        fr = dot_nt(stacked, fresh_tile(0, block, h)) + tile_rows(fr_bias)
        s_ref[slot, :, pl.ds(span, HEAD_SIZE)] = suf
        s_ref[slot, :, pl.ds(span + HEAD_SIZE, HEAD_SIZE)] = fr
        top = jnp.maximum(suf, fr)
        yield
        for c in range(chunks):
            s = dot_nt(wide, prefix_tile(0, c, h))
            s_ref[slot, :, pl.ds(c * KEY_CHUNK, KEY_CHUNK)] = s
            for j in range(KEY_CHUNK // HEAD_SIZE):
                top = jnp.maximum(top, s[:, j * HEAD_SIZE : (j + 1) * HEAD_SIZE])
            if c == chunks - 1:
                top = jnp.max(top, axis=1, keepdims=True) * factor
                m_ref[slot] = jnp.broadcast_to(top, (rows, HEAD_SIZE))
            yield

    def outputs(block, h, slot):
        top = m_ref[slot]

        def weigh(start, width):
            x = s_ref[slot, :, pl.ds(start, width)]
            wide_top = jnp.concatenate([top] * (width // HEAD_SIZE), axis=1)
            return jnp.exp2(x * factor - wide_top)

        both = weigh(span, 2 * HEAD_SIZE)
        total = both[:, :HEAD_SIZE] + both[:, HEAD_SIZE:]
        both = both.astype(jnp.bfloat16)
        fr = dot_nn(both[:, HEAD_SIZE:], fresh_tile(1, block, h))
        suf = []
        for i in range(suf_groups):
            piece = jnp.concatenate(
                [
                    both[
                        g * block_rows + i * suf_rows : g * block_rows + (i + 1) * suf_rows,
                        :HEAD_SIZE,
                    ]
                    for g in range(group)
                ],
                axis=0,
            )
            suf.append(dot_nn(piece, suffix_tile(1, block, i, h)))
        extra = fr + jnp.concatenate(
            [
                jnp.concatenate([x[g * suf_rows : (g + 1) * suf_rows] for x in suf], axis=0)
                for g in range(group)
            ],
            axis=0,
        )
        yield
        acc = None
        for c in range(chunks):
            p = weigh(c * KEY_CHUNK, KEY_CHUNK)
            for j in range(KEY_CHUNK // HEAD_SIZE):
                total = total + p[:, j * HEAD_SIZE : (j + 1) * HEAD_SIZE]
            part = dot_nn(p.astype(jnp.bfloat16), prefix_tile(1, c, h))
            acc = part if acc is None else acc + part
            if c == chunks - 1:
                _, local = row_codes(block)
                local = tile_rows(local)
                chosen = acc[:, :HEAD_SIZE]
                for q in range(1, prefix_count):
                    chosen = jnp.where(
                        local == q, acc[:, q * HEAD_SIZE : (q + 1) * HEAD_SIZE], chosen
                    )
                weight = 1.0 / jnp.sum(total, axis=1, keepdims=True)
                out = ((chosen + extra) * weight).astype(o_ref.dtype)
                start = pl.multiple_of((block - first) * block_rows, block_rows)
                for g in range(group):
                    o_ref[
                        pl.ds(start, block_rows),
                        pl.ds((h * group + g) * HEAD_SIZE, HEAD_SIZE),
                    ] = out[g * block_rows : (g + 1) * block_rows]
            yield

    def run(*streams):
        for _ in range(chunks + 1):
            for stream in streams:
                next(stream)

    run(scores(first, 0, 0))

    def body(block, carry):
        for h in range(key_heads):
            if h + 1 < key_heads:
                run(scores(block, h + 1, h + 1), outputs(block, h, h))
            elif key_heads > 1:
                following = jnp.minimum(block + 1, last)
                run(scores(following, 0, 0), outputs(block, h, h))
            else:
                run(outputs(block, h, h))
                run(scores(jnp.minimum(block + 1, last), 0, 0))
        return carry

    lax.fori_loop(first, first + blocks, body, 0)


def attend(code, queries, prefix, suffix, fresh, steps, part):
    rows, width = queries.shape
    rows = rows // PARTS
    key_heads = prefix.shape[3] // HEAD_SIZE
    group = width // HEAD_SIZE // key_heads
    unit_rows = BLOCK_ROLLS * steps * group
    span = prefix.shape[2] + 2 * HEAD_SIZE
    blocks = suffix.shape[1] // BLOCK_ROLLS // PARTS
    return pl.pallas_call(
        functools.partial(
            attend_kernel, steps=steps, group=group, first=part * blocks, blocks=blocks
        ),
        out_shape=jax.ShapeDtypeStruct((rows, width), jnp.bfloat16),
        in_specs=[VMEM] * 5,
        out_specs=VMEM,
        scratch_shapes=[
            pltpu.VMEM((key_heads, unit_rows, span), jnp.float32),
            pltpu.VMEM((key_heads, unit_rows, HEAD_SIZE), jnp.float32),
        ],
        compiler_params=pltpu.CompilerParams(vmem_limit_bytes=20 * MIB),
        cost_estimate=LENGTHY,
    )(code, queries, prefix, suffix, fresh)


def project_kernel(core_ref, a_ref, w_ref, send_ref, keep_ref, *, count):
    step = pl.program_id(0)
    part = dot_nn(a_ref[...], w_ref[...]).astype(jnp.bfloat16)

    @pl.when(step < count)
    def _():
        send_ref[0] = part

    @pl.when(step >= count)
    def _():
        keep_ref[0] = part


def project(core, attended, weight, out_width):
    rows, width = attended.shape
    count = weight.shape[1] // out_width // 2

    def column(j, core):
        parity = jnp.where(j < count, 1 - core[0], core[0])
        return (0, (j % count) * 2 + parity)

    shape = jax.ShapeDtypeStruct((count, rows, out_width), jnp.bfloat16)
    return pl.pallas_call(
        functools.partial(project_kernel, count=count),
        grid_spec=pltpu.PrefetchScalarGridSpec(
            num_scalar_prefetch=1,
            grid=(2 * count,),
            in_specs=[
                pl.BlockSpec((rows, width), lambda j, core: (0, 0)),
                pl.BlockSpec((width, out_width), column),
            ],
            out_specs=[
                pl.BlockSpec((1, rows, out_width), lambda j, core: (jnp.minimum(j, count - 1), 0, 0)),
                pl.BlockSpec((1, rows, out_width), lambda j, core: (jnp.maximum(j - count, 0), 0, 0)),
            ],
        ),
        out_shape=[shape, shape],
        compiler_params=pltpu.CompilerParams(vmem_limit_bytes=8 * MIB),
        cost_estimate=BRIEF,
    )(core, attended, weight)


def pair_kernel(chip_ref, keep_ref, come_ref, *outs):
    chips = len(outs)
    for shift, out in enumerate(outs):
        index = (chip_ref[0] + shift) % chips
        pair = keep_ref[index].astype(jnp.float32) + come_ref[index].astype(jnp.float32)
        out[...] = pair.astype(jnp.bfloat16)


def pair_sums(chip, keep, come):
    chips, rows, width = keep.shape
    return pl.pallas_call(
        pair_kernel,
        out_shape=[jax.ShapeDtypeStruct((rows, width), jnp.bfloat16)] * chips,
        in_specs=[pl.BlockSpec(memory_space=pltpu.SMEM), VMEM, VMEM],
        out_specs=[VMEM] * chips,
        compiler_params=pltpu.CompilerParams(vmem_limit_bytes=8 * MIB),
        cost_estimate=BRIEF,
    )(chip, keep, come)


def pack_kernel(target_ref, *refs):
    parts, outs = refs[:PARTS], refs[PARTS:]
    slots = outs[0].shape[0]
    part_rows = parts[0].shape[0]
    for d, out in enumerate(outs):
        total = None
        for k, part in enumerate(parts):
            row = d * slots + lax.broadcasted_iota(jnp.int32, (slots, part_rows), 0)
            chosen = row == target_ref[:, k * part_rows : (k + 1) * part_rows]
            term = dot_nn(jnp.where(chosen, 1.0, 0.0).astype(jnp.bfloat16), part[...])
            total = term if total is None else total + term
        out[...] = total.astype(jnp.bfloat16)


def pack(target, parts, count, slots):
    rows, width = parts[0].shape
    return pl.pallas_call(
        pack_kernel,
        out_shape=[jax.ShapeDtypeStruct((slots, width), jnp.bfloat16)] * count,
        in_specs=[VMEM] * (1 + len(parts)),
        out_specs=[VMEM] * count,
        compiler_params=pltpu.CompilerParams(vmem_limit_bytes=8 * MIB),
        cost_estimate=BRIEF,
    )(target, *parts)


def adapter_mask(rows, per_adapter, rank, tile):
    lane = lax.broadcasted_iota(jnp.int32, (rows, HEAD_SIZE), 1) + tile * HEAD_SIZE
    row = lax.broadcasted_iota(jnp.int32, (rows, HEAD_SIZE), 0)
    return lane // rank == row // per_adapter


def shrink_kernel(*refs, per_adapter, rank, count):
    weights, pieces, out = refs[:FOLD], refs[FOLD : FOLD + count], refs[-1]
    rows = pieces[0].shape[0] // FOLD
    for k in range(FOLD):
        span = pl.ds(k * rows, rows)
        every = dot_nt(
            jnp.concatenate([p[span, :] for p in pieces], axis=0),
            weights[k][...],
        )
        for d in range(count):
            total = None
            for tile in range(every.shape[1] // HEAD_SIZE):
                x = every[d * rows : (d + 1) * rows, tile * HEAD_SIZE : (tile + 1) * HEAD_SIZE]
                x = jnp.where(adapter_mask(rows, per_adapter, rank, tile), x, 0.0)
                total = x if total is None else total + x
            summed = total
            for turn in range(1, HEAD_SIZE // rank):
                summed = summed + pltpu.roll(total, turn * rank, axis=1)
            out[pl.ds((d * FOLD + k) * rows, rows), :] = summed


def shrink_rows(weights, pieces, per_adapter, rank):
    count = len(pieces)
    rows, width = pieces[0].shape
    return pl.pallas_call(
        functools.partial(shrink_kernel, per_adapter=per_adapter, rank=rank, count=count),
        out_shape=jax.ShapeDtypeStruct((count * rows, HEAD_SIZE), jnp.float32),
        in_specs=[VMEM] * (FOLD + count),
        out_specs=VMEM,
        compiler_params=pltpu.CompilerParams(vmem_limit_bytes=8 * MIB),
        cost_estimate=LENGTHY,
    )(*weights, *pieces)


def expand_kernel(*refs, per_adapter, rank, count, terms):
    own, sums, outs = refs[0], refs[1 + CUTS : 1 + CUTS + terms], refs[1 + CUTS + terms :]
    weights = [own[...], jnp.concatenate([x[...] for x in refs[1 : 1 + CUTS]], axis=0)]
    depth = own.shape[0]
    rows = outs[0].shape[0] // FOLD
    for k in range(FOLD):
        spread = []
        for d in range(count):
            span = pl.ds((d * FOLD + k) * rows, rows)
            code = sums[0][span, :].astype(jnp.float32)
            for other in sums[1:]:
                code = code + other[span, :].astype(jnp.float32)
            spread.append(
                jnp.concatenate(
                    [
                        jnp.where(adapter_mask(rows, per_adapter, rank, tile), code, 0.0)
                        for tile in range(depth // HEAD_SIZE)
                    ],
                    axis=1,
                ).astype(jnp.bfloat16)
            )
        wide = dot_nn(jnp.concatenate(spread, axis=0), weights[k])
        wide = wide.astype(jnp.bfloat16)
        for d in range(count):
            outs[d][pl.ds(k * rows, rows), :] = wide[d * rows : (d + 1) * rows]


def expand_rows(weights, sums, per_adapter, rank, count):
    rows = sums[0].shape[0] // count
    width = weights[0].shape[1]
    return pl.pallas_call(
        functools.partial(
            expand_kernel, per_adapter=per_adapter, rank=rank, count=count, terms=len(sums)
        ),
        out_shape=[jax.ShapeDtypeStruct((rows, width), jnp.bfloat16)] * count,
        in_specs=[VMEM] * (1 + CUTS + len(sums)),
        out_specs=[VMEM] * count,
        compiler_params=pltpu.CompilerParams(vmem_limit_bytes=8 * MIB),
        cost_estimate=BRIEF,
    )(*weights, *sums)


def combine_kernel(target_ref, *refs, count, terms):
    pieces, sums, out = refs[:count], refs[count:-1], refs[-1]
    slots = pieces[0].shape[0]
    part_rows = out.shape[0] // PARTS
    for k in range(PARTS):
        target = target_ref[pl.ds(k * part_rows, part_rows), :]
        delta = None
        for d, piece in enumerate(pieces):
            slot = d * slots + lax.broadcasted_iota(jnp.int32, (part_rows, slots), 1)
            chosen = jnp.where(target == slot, 1.0, 0.0).astype(jnp.bfloat16)
            term = dot_nn(chosen, piece[...])
            delta = term if delta is None else delta + term
        for x in sums[k * terms : (k + 1) * terms]:
            delta = delta + x[...].astype(jnp.float32)
        out[pl.ds(k * part_rows, part_rows), :] = delta.astype(jnp.bfloat16)


def combine(target, pieces, sums):
    terms = len(sums[0])
    part_rows, width = sums[0][0].shape
    count = len(pieces)
    flat = [x for part in sums for x in part]
    rows = part_rows * len(sums)
    return pl.pallas_call(
        functools.partial(combine_kernel, count=count, terms=terms),
        out_shape=jax.ShapeDtypeStruct((rows, width), jnp.bfloat16),
        in_specs=[VMEM] * (1 + count + len(flat)),
        out_specs=VMEM,
        compiler_params=pltpu.CompilerParams(vmem_limit_bytes=8 * MIB),
        cost_estimate=BRIEF,
    )(target, *pieces, *flat)


def local(
    queries,
    shared_prefix_cache,
    rollout_suffix_cache,
    fresh_key_value,
    rollout_prefix_index,
    rollout_suffix_length,
    rollout_adapter_index,
    output_projection_weight,
    adapter_shrink_weight,
    adapter_expand_weight,
):
    rolls, steps, width = queries.shape
    rows = rolls * steps
    prefix_count = shared_prefix_cache.shape[1]
    resident, rank, out_width = adapter_expand_weight.shape
    holders, sides = lax.axis_size("adapter"), lax.axis_size("tensor")
    block, chips = holders // FOLD, sides // 2
    here, side = lax.axis_index("adapter"), lax.axis_index("tensor")
    chip, core = side // 2, side % 2

    def in_block(shift):
        return [(i, i // block * block + (i + shift) % block) for i in range(holders)]

    cores = [(t, t // 2 * 2 + (t + 1) % 2) for t in range(sides)]

    def over_chips(shift):
        return [(t, (t // 2 + shift) % chips * 2 + t % 2) for t in range(sides)]

    own_shrink = adapter_shrink_weight.reshape(resident * rank, width)
    own_expand = adapter_expand_weight.reshape(resident * rank, out_width)
    far = [(i, (i + block) % holders) for i in range(holders)]

    adapter = rollout_adapter_index[:, 0]
    holder = adapter // resident
    order = jnp.arange(rolls, dtype=jnp.int32)
    same = (adapter[:, None] == adapter[None, :]) & (order[None, :] < order[:, None])
    turn = jnp.sum(same.astype(jnp.int32), axis=1)
    fold = (here // block - holder // block) % FOLD
    place = (holder % block - here % block) % block
    slot = ((place * FOLD + fold) * resident + adapter % resident) * MOST + turn
    target = (slot[:, None] * steps + jnp.arange(steps, dtype=jnp.int32)[None, :]).reshape(rows)
    slots = FOLD * resident * MOST * steps
    per_adapter = MOST * steps

    code = (rollout_suffix_length * prefix_count + rollout_prefix_index % prefix_count)[None, :]
    flat_queries = queries.reshape(rows, width)
    flat_fresh = fresh_key_value.reshape(2, rows, -1)
    core_index = core.reshape(1).astype(jnp.int32)
    chip_index = chip.reshape(1).astype(jnp.int32)
    cut = own_expand.shape[0] // CUTS
    cuts = [own_expand[k * cut : (k + 1) * cut] for k in range(CUTS)]
    tie = lax.optimization_barrier

    def attend_part(code, part):
        return attend(
            code, flat_queries, shared_prefix_cache, rollout_suffix_cache, flat_fresh, steps, part
        )

    def send_over_chips(pairs):
        return [lax.ppermute(pairs[s], "tensor", over_chips(s)) for s in range(1, chips)]

    code, target, cuts = tie((code, target, cuts))
    shrink = lax.ppermute(own_shrink, "adapter", far)
    first = attend_part(code, 0)
    send, keep = project(core_index, first, output_projection_weight, out_width)
    come = lax.ppermute(send, "tensor", cores)
    code, shrink, keep, cuts[0] = tie((code, shrink, keep, cuts[0]))
    expands = [lax.ppermute(cuts[0], "adapter", far)]
    second = attend_part(code, 1)
    pairs = pair_sums(chip_index, keep, come)
    second, expands[0], cuts[1], *pairs = tie((second, expands[0], cuts[1], *pairs))
    expands.append(lax.ppermute(cuts[1], "adapter", far))
    early = send_over_chips(pairs)
    packed = list(pack(target[None, :], [first, second], block, slots))
    second, packed[0] = tie((second, packed[0]))
    pieces = [packed[0]] + [
        lax.ppermute(packed[d], "adapter", in_block(d)) for d in range(1, block)
    ]
    send, keep = project(core_index, second, output_projection_weight, out_width)
    late_pairs = pair_sums(chip_index, keep, lax.ppermute(send, "tensor", cores))
    pieces[0], expands[1], early = tie((pieces[0], expands[1], early))
    codes = shrink_rows([own_shrink, shrink], pieces, per_adapter, rank)
    codes = codes + lax.ppermute(codes, "tensor", cores)
    brief = codes.astype(jnp.bfloat16)
    codes = [brief] + [lax.ppermute(brief, "tensor", over_chips(s)) for s in range(1, chips)]
    codes, late_pairs = tie((codes, late_pairs))
    late = send_over_chips(late_pairs)
    wide = expand_rows([own_expand, *expands], codes, per_adapter, rank, block)
    back = [wide[0]] + [
        lax.ppermute(wide[d], "adapter", in_block(block - d)) for d in range(1, block)
    ]
    sums = [[pairs[0], *early], [late_pairs[0], *late]]
    mixed = combine(target[:, None], back, sums)
    return mixed.reshape(rolls, steps, out_width)


def solution(mesh):
    placed = (
        P("adapter", None, "tensor"),
        P(None, "adapter", None, "tensor"),
        P(None, "adapter", None, "tensor"),
        P(None, "adapter", None, "tensor"),
        P("adapter"),
        P("adapter"),
        P("adapter", None),
        P("tensor", None),
        P("adapter", None, "tensor"),
        P("adapter", None, "tensor"),
    )
    return jax.shard_map(
        local, mesh=mesh, in_specs=placed, out_specs=P("adapter", None, "tensor"), check_vma=False
    )
```

```python
import functools
import math

import jax
import jax.numpy as jnp
from jax import lax
from jax.experimental import pallas as pl
from jax.experimental.pallas import tpu as pltpu
from jax.sharding import PartitionSpec as P

HEAD_SIZE = 128
MOST = 5
FOLD = 2
CUTS = 1
BLOCK_ROLLS = 16
KEY_CHUNK = 512
NEG = float("-inf")
MIB = 1 << 20
BRIEF = pl.CostEstimate(flops=1024, bytes_accessed=1024, transcendentals=0)
LENGTHY = pl.CostEstimate(flops=1 << 33, bytes_accessed=1 << 24, transcendentals=0)
VMEM = pl.BlockSpec(memory_space=pltpu.VMEM)
ANY = pl.BlockSpec(memory_space=pl.ANY)
SMEM = pl.BlockSpec(memory_space=pltpu.SMEM)


def dot_nt(a, b):
    return lax.dot_general(a, b, (((1,), (1,)), ((), ())), preferred_element_type=jnp.float32)


def dot_nn(a, b):
    return jnp.dot(a, b, preferred_element_type=jnp.float32)


def attend_kernel(
    length_ref, prefix_ref, q_ref, kv_hbm, suf_hbm, fr_ref, o_ref,
    s_ref, m_ref, kv_ref, suf_ref, sems,
    *, steps, group, first, blocks
):
    prefix_count, prefix_len = kv_ref.shape[1], kv_ref.shape[2]
    key_heads = kv_ref.shape[3] // HEAD_SIZE
    rolls, suf_len = suf_hbm.shape[1], suf_hbm.shape[2]
    block_rows = BLOCK_ROLLS * steps
    rows = block_rows * group
    last = first + blocks - 1
    suf_rolls = HEAD_SIZE // suf_len
    suf_rows = suf_rolls * steps
    suf_groups = BLOCK_ROLLS // suf_rolls
    window_rolls = HEAD_SIZE // steps
    windows = window_rolls // BLOCK_ROLLS
    factor = HEAD_SIZE ** (-0.5) * math.log2(math.e)
    chunks = prefix_len // KEY_CHUNK
    span = prefix_len

    def row_codes(block):
        shape = (block_rows, rolls)
        mine = block * BLOCK_ROLLS + lax.broadcasted_iota(jnp.int32, shape, 0) // steps
        lane = lax.broadcasted_iota(jnp.int32, shape, 1)
        code = length_ref[...] * prefix_count + prefix_ref[...] % prefix_count
        code = jnp.broadcast_to(code.astype(jnp.float32), shape)
        col = jnp.sum(jnp.where(mine == lane, code, 0.0), axis=1, keepdims=True)
        col = jnp.broadcast_to(col, (block_rows, HEAD_SIZE)).astype(jnp.int32)
        return col // prefix_count, col % prefix_count

    mine = pl.ds(first * BLOCK_ROLLS, blocks * BLOCK_ROLLS)
    loads = []
    for which in range(2):
        loads.append(pltpu.make_async_copy(kv_hbm.at[which], kv_ref.at[which], sems.at[2 * which]))
        loads.append(
            pltpu.make_async_copy(suf_hbm.at[which, mine], suf_ref.at[which], sems.at[2 * which + 1])
        )
    for load in loads:
        load.start()

    def tile_rows(x):
        return jnp.concatenate([x] * group, axis=0)

    def load_q(block, h):
        start = pl.multiple_of(block * block_rows, block_rows)
        return [
            q_ref[pl.ds(start, block_rows), pl.ds((h * group + g) * HEAD_SIZE, HEAD_SIZE)]
            for g in range(group)
        ]

    def head_lanes(h):
        return pl.ds(h * HEAD_SIZE, HEAD_SIZE)

    def suffix_tile(which, block, i, h):
        start = (block - first) * BLOCK_ROLLS + i * suf_rolls
        tile = suf_ref[which, pl.ds(start, suf_rolls), :, head_lanes(h)]
        return tile.reshape(HEAD_SIZE, HEAD_SIZE)

    def fresh_tile(which, block, h):
        start = pl.multiple_of(block // windows * HEAD_SIZE, HEAD_SIZE)
        return fr_ref[which, pl.ds(start, HEAD_SIZE), head_lanes(h)]

    def prefix_tile(which, c, h):
        return jnp.concatenate(
            [
                kv_ref[which, p, pl.ds(c * KEY_CHUNK, KEY_CHUNK), head_lanes(h)]
                for p in range(prefix_count)
            ],
            axis=1,
        )

    def scores(block, h, slot):
        length, local = row_codes(block)
        parts = load_q(block, h)
        stacked = jnp.concatenate(parts, axis=0)
        wide = jnp.concatenate(
            [
                jnp.concatenate(
                    [jnp.where(local == p, x, jnp.zeros_like(x)) for x in parts], axis=0
                )
                for p in range(prefix_count)
            ],
            axis=1,
        )
        shape = (block_rows, HEAD_SIZE)
        row = lax.broadcasted_iota(jnp.int32, shape, 0)
        lane = lax.broadcasted_iota(jnp.int32, shape, 1)
        roll = row // steps
        keep = (roll % suf_rolls == lane // suf_len) & (lane % suf_len < length)
        suf_bias = jnp.where(keep, 0.0, NEG)
        in_window = (block % windows) * BLOCK_ROLLS + roll
        keep = (in_window == lane // steps) & (lane % steps <= row % steps)
        fr_bias = jnp.where(keep, 0.0, NEG)
        suf = []
        for i in range(suf_groups):
            piece = jnp.concatenate(
                [x[i * suf_rows : (i + 1) * suf_rows] for x in parts], axis=0
            )
            suf.append(dot_nt(piece, suffix_tile(0, block, i, h)))
        suf = jnp.concatenate(
            [
                jnp.concatenate([x[g * suf_rows : (g + 1) * suf_rows] for x in suf], axis=0)
                for g in range(group)
            ],
            axis=0,
        ) + tile_rows(suf_bias)
        fr = dot_nt(stacked, fresh_tile(0, block, h)) + tile_rows(fr_bias)
        s_ref[slot, :, pl.ds(span, HEAD_SIZE)] = suf
        s_ref[slot, :, pl.ds(span + HEAD_SIZE, HEAD_SIZE)] = fr
        top = jnp.maximum(suf, fr)
        yield
        for c in range(chunks):
            s = dot_nt(wide, prefix_tile(0, c, h))
            s_ref[slot, :, pl.ds(c * KEY_CHUNK, KEY_CHUNK)] = s
            for j in range(KEY_CHUNK // HEAD_SIZE):
                top = jnp.maximum(top, s[:, j * HEAD_SIZE : (j + 1) * HEAD_SIZE])
            if c == chunks - 1:
                top = jnp.max(top, axis=1, keepdims=True) * factor
                m_ref[slot] = jnp.broadcast_to(top, (rows, HEAD_SIZE))
            yield

    def outputs(block, h, slot):
        top = m_ref[slot]

        def weigh(start, width):
            x = s_ref[slot, :, pl.ds(start, width)]
            wide_top = jnp.concatenate([top] * (width // HEAD_SIZE), axis=1)
            return jnp.exp2(x * factor - wide_top)

        both = weigh(span, 2 * HEAD_SIZE)
        total = both[:, :HEAD_SIZE] + both[:, HEAD_SIZE:]
        both = both.astype(jnp.bfloat16)
        fr = dot_nn(both[:, HEAD_SIZE:], fresh_tile(1, block, h))
        suf = []
        for i in range(suf_groups):
            piece = jnp.concatenate(
                [
                    both[
                        g * block_rows + i * suf_rows : g * block_rows + (i + 1) * suf_rows,
                        :HEAD_SIZE,
                    ]
                    for g in range(group)
                ],
                axis=0,
            )
            suf.append(dot_nn(piece, suffix_tile(1, block, i, h)))
        extra = fr + jnp.concatenate(
            [
                jnp.concatenate([x[g * suf_rows : (g + 1) * suf_rows] for x in suf], axis=0)
                for g in range(group)
            ],
            axis=0,
        )
        yield
        acc = None
        for c in range(chunks):
            p = weigh(c * KEY_CHUNK, KEY_CHUNK)
            for j in range(KEY_CHUNK // HEAD_SIZE):
                total = total + p[:, j * HEAD_SIZE : (j + 1) * HEAD_SIZE]
            part = dot_nn(p.astype(jnp.bfloat16), prefix_tile(1, c, h))
            acc = part if acc is None else acc + part
            if c == chunks - 1:
                _, local = row_codes(block)
                local = tile_rows(local)
                chosen = acc[:, :HEAD_SIZE]
                for q in range(1, prefix_count):
                    chosen = jnp.where(
                        local == q, acc[:, q * HEAD_SIZE : (q + 1) * HEAD_SIZE], chosen
                    )
                weight = 1.0 / jnp.sum(total, axis=1, keepdims=True)
                out = ((chosen + extra) * weight).astype(o_ref.dtype)
                start = pl.multiple_of((block - first) * block_rows, block_rows)
                for g in range(group):
                    o_ref[
                        pl.ds(start, block_rows),
                        pl.ds((h * group + g) * HEAD_SIZE, HEAD_SIZE),
                    ] = out[g * block_rows : (g + 1) * block_rows]
            yield

    def run(*streams):
        for _ in range(chunks + 1):
            for stream in streams:
                next(stream)

    for load in loads[:2]:
        load.wait()
    run(scores(first, 0, 0))
    for load in loads[2:]:
        load.wait()

    def body(block, carry):
        for h in range(key_heads):
            if h + 1 < key_heads:
                run(scores(block, h + 1, h + 1), outputs(block, h, h))
            elif key_heads > 1:
                following = jnp.minimum(block + 1, last)
                run(scores(following, 0, 0), outputs(block, h, h))
            else:
                run(outputs(block, h, h))
                run(scores(jnp.minimum(block + 1, last), 0, 0))
        return carry

    lax.fori_loop(first, first + blocks, body, 0)


def attend(lengths, prefixes, queries, prefix, suffix, fresh, steps, first, blocks):
    width = queries.shape[-1]
    rows = blocks * BLOCK_ROLLS * steps
    key_heads = prefix.shape[3] // HEAD_SIZE
    group = width // HEAD_SIZE // key_heads
    unit_rows = BLOCK_ROLLS * steps * group
    span = prefix.shape[2] + 2 * HEAD_SIZE
    held = (2, blocks * BLOCK_ROLLS) + suffix.shape[2:]
    return pl.pallas_call(
        functools.partial(attend_kernel, steps=steps, group=group, first=first, blocks=blocks),
        out_shape=jax.ShapeDtypeStruct((rows, width), jnp.bfloat16),
        in_specs=[VMEM, VMEM, VMEM, ANY, ANY, VMEM],
        out_specs=VMEM,
        scratch_shapes=[
            pltpu.VMEM((key_heads, unit_rows, span), jnp.float32),
            pltpu.VMEM((key_heads, unit_rows, HEAD_SIZE), jnp.float32),
            pltpu.VMEM(prefix.shape, prefix.dtype),
            pltpu.VMEM(held, suffix.dtype),
            pltpu.SemaphoreType.DMA((4,)),
        ],
        compiler_params=pltpu.CompilerParams(vmem_limit_bytes=52 * MIB),
        cost_estimate=LENGTHY,
    )(lengths, prefixes, queries, prefix, suffix, fresh)


def project_kernel(core_ref, a_ref, w_ref, send_ref, keep_ref, *, count):
    step = pl.program_id(0)
    part = dot_nn(a_ref[...], w_ref[...]).astype(jnp.bfloat16)

    @pl.when(step < count)
    def _():
        send_ref[0] = part

    @pl.when(step >= count)
    def _():
        keep_ref[0] = part


def project(core, attended, weight, out_width):
    rows, width = attended.shape
    count = weight.shape[1] // out_width // 2

    def column(j, core):
        parity = jnp.where(j < count, 1 - core[0], core[0])
        return (0, (j % count) * 2 + parity)

    shape = jax.ShapeDtypeStruct((count, rows, out_width), jnp.bfloat16)
    return pl.pallas_call(
        functools.partial(project_kernel, count=count),
        grid_spec=pltpu.PrefetchScalarGridSpec(
            num_scalar_prefetch=1,
            grid=(2 * count,),
            in_specs=[
                pl.BlockSpec((rows, width), lambda j, core: (0, 0)),
                pl.BlockSpec((width, out_width), column),
            ],
            out_specs=[
                pl.BlockSpec((1, rows, out_width), lambda j, core: (jnp.minimum(j, count - 1), 0, 0)),
                pl.BlockSpec((1, rows, out_width), lambda j, core: (jnp.maximum(j - count, 0), 0, 0)),
            ],
        ),
        out_shape=[shape, shape],
        compiler_params=pltpu.CompilerParams(vmem_limit_bytes=8 * MIB),
        cost_estimate=BRIEF,
    )(core, attended, weight)


def pair_kernel(chip_ref, keep_ref, come_ref, own_ref, *outs, cuts):
    chips = keep_ref.shape[0]
    for shift in range(chips):
        index = (chip_ref[0] + shift) % chips
        pair = keep_ref[index].astype(jnp.float32) + come_ref[index].astype(jnp.float32)
        pair = pair.astype(jnp.bfloat16)
        if shift == 0:
            own_ref[...] = pair
        else:
            for k in range(cuts):
                out = outs[(shift - 1) * cuts + k]
                rows = out.shape[0]
                out[...] = pair[k * rows : (k + 1) * rows]


def pair_sums(chip, keep, come, cuts):
    chips, rows, width = keep.shape
    away = [jax.ShapeDtypeStruct((rows // cuts, width), jnp.bfloat16)] * ((chips - 1) * cuts)
    return pl.pallas_call(
        functools.partial(pair_kernel, cuts=cuts),
        out_shape=[jax.ShapeDtypeStruct((rows, width), jnp.bfloat16)] + away,
        in_specs=[SMEM, VMEM, VMEM],
        out_specs=[VMEM] * (1 + len(away)),
        compiler_params=pltpu.CompilerParams(vmem_limit_bytes=12 * MIB),
        cost_estimate=BRIEF,
    )(chip, keep, come)


def slot_of(row, turn, here, resident, holders):
    block = holders // FOLD
    holder = row // resident
    fold = (here // block - holder // block + FOLD) % FOLD
    place = (holder % block - here % block + block) % block
    return ((place * FOLD + fold) * resident + row % resident) * MOST + turn


def row_slots(row_ref, here, resident, holders):
    row = row_ref[...]
    shape = (row.shape[1], row.shape[1])
    across = jnp.broadcast_to(row, shape)
    down, lane = lax.broadcasted_iota(jnp.int32, shape, 0), lax.broadcasted_iota(jnp.int32, shape, 1)
    values = across.astype(jnp.float32)
    col = jnp.sum(jnp.where(down == lane, values, 0.0), axis=1, keepdims=True)
    same = jnp.broadcast_to(col, shape) == values
    turn_row = jnp.sum(jnp.where(same & (down < lane), 1.0, 0.0), axis=0, keepdims=True)
    turn_col = jnp.sum(jnp.where(same & (lane < down), 1.0, 0.0), axis=1, keepdims=True)
    place_row = slot_of(row, turn_row.astype(jnp.int32), here, resident, holders)
    place_col = slot_of(
        jnp.broadcast_to(col, shape).astype(jnp.int32),
        jnp.broadcast_to(turn_col, shape).astype(jnp.int32),
        here,
        resident,
        holders,
    )
    return place_row, place_col[:, :1]


def pack_kernel(here_ref, row_ref, *refs, steps, resident, holders, count):
    parts, outs = refs[:-count], refs[-count:]
    slots, rolls = outs[0].shape[0], row_ref.shape[1]
    place, _ = row_slots(row_ref, here_ref[0], resident, holders)
    for d, out in enumerate(outs):
        shape = (slots, rolls)
        slot = (d * slots + lax.broadcasted_iota(jnp.int32, shape, 0)) // steps
        picked = jnp.where(slot == jnp.broadcast_to(place, shape), 1.0, 0.0).astype(jnp.bfloat16)
        total, start = None, 0
        for part in parts:
            rows = part.shape[0]
            shape = (rolls, rows)
            spread = lax.broadcasted_iota(jnp.int32, shape, 0) == (
                start + lax.broadcasted_iota(jnp.int32, shape, 1)
            ) // steps
            chosen = dot_nn(picked, jnp.where(spread, 1.0, 0.0).astype(jnp.bfloat16))
            shape = (slots, rows)
            step = lax.broadcasted_iota(jnp.int32, shape, 0) % steps
            aligned = step == (start + lax.broadcasted_iota(jnp.int32, shape, 1)) % steps
            chosen = jnp.where(aligned, chosen, 0.0).astype(jnp.bfloat16)
            term = dot_nn(chosen, part[...])
            total = term if total is None else total + term
            start += rows
        out[...] = total.astype(jnp.bfloat16)


def pack(here, adapter_row, parts, count, slots, steps, resident, holders):
    width = parts[0].shape[1]
    return pl.pallas_call(
        functools.partial(
            pack_kernel, steps=steps, resident=resident, holders=holders, count=count
        ),
        out_shape=[jax.ShapeDtypeStruct((slots, width), jnp.bfloat16)] * count,
        in_specs=[SMEM] + [VMEM] * (1 + len(parts)),
        out_specs=[VMEM] * count,
        compiler_params=pltpu.CompilerParams(vmem_limit_bytes=12 * MIB),
        cost_estimate=BRIEF,
    )(here, adapter_row, *parts)


def adapter_mask(rows, per_adapter, rank, tile):
    lane = lax.broadcasted_iota(jnp.int32, (rows, HEAD_SIZE), 1) + tile * HEAD_SIZE
    row = lax.broadcasted_iota(jnp.int32, (rows, HEAD_SIZE), 0)
    return lane // rank == row // per_adapter


def shrink_kernel(*refs, per_adapter, rank, count):
    weights, pieces, out = refs[:FOLD], refs[FOLD : FOLD + count], refs[-1]
    rows = pieces[0].shape[0] // FOLD
    found = []
    for k in range(FOLD):
        span = pl.ds(k * rows, rows)
        every = dot_nt(
            jnp.concatenate([p[span, :] for p in pieces], axis=0),
            weights[k][...],
        )
        for d in range(count):
            total = None
            for tile in range(every.shape[1] // HEAD_SIZE):
                x = every[d * rows : (d + 1) * rows, tile * HEAD_SIZE : (tile + 1) * HEAD_SIZE]
                x = jnp.where(adapter_mask(rows, per_adapter, rank, tile), x, 0.0)
                total = x if total is None else total + x
            summed = total
            for turn in range(1, HEAD_SIZE // rank):
                summed = summed + pltpu.roll(total, turn * rank, axis=1)
            found.append(summed)
    lane = lax.broadcasted_iota(jnp.int32, (rows, HEAD_SIZE), 1)
    for d in range(count):
        both = jnp.where(lane < rank, found[d], found[count + d])
        out[pl.ds(d * rows, rows), :] = both


def shrink_rows(weights, pieces, per_adapter, rank):
    count = len(pieces)
    rows, width = pieces[0].shape
    return pl.pallas_call(
        functools.partial(shrink_kernel, per_adapter=per_adapter, rank=rank, count=count),
        out_shape=jax.ShapeDtypeStruct((count * rows // FOLD, HEAD_SIZE), jnp.float32),
        in_specs=[VMEM] * (FOLD + count),
        out_specs=VMEM,
        compiler_params=pltpu.CompilerParams(vmem_limit_bytes=8 * MIB),
        cost_estimate=LENGTHY,
    )(*weights, *pieces)


def expand_kernel(*refs, per_adapter, rank, count, terms):
    weights, sums, outs = refs[:FOLD], refs[FOLD : FOLD + terms], refs[FOLD + terms :]
    depth = weights[0].shape[0]
    rows = outs[0].shape[0] // FOLD
    for k in range(FOLD):
        spread = []
        for d in range(count):
            span = pl.ds(d * rows, rows)
            code = sums[0][span, :].astype(jnp.float32)
            for other in sums[1:]:
                code = code + other[span, :].astype(jnp.float32)
            lane = lax.broadcasted_iota(jnp.int32, (rows, HEAD_SIZE), 1)
            turned = pltpu.roll(code, rank, axis=1)
            code = jnp.where((lane < rank) == (k == 0), code, turned)
            spread.append(
                jnp.concatenate(
                    [
                        jnp.where(adapter_mask(rows, per_adapter, rank, tile), code, 0.0)
                        for tile in range(depth // HEAD_SIZE)
                    ],
                    axis=1,
                ).astype(jnp.bfloat16)
            )
        wide = dot_nn(jnp.concatenate(spread, axis=0), weights[k][...])
        wide = wide.astype(jnp.bfloat16)
        for d in range(count):
            outs[d][pl.ds(k * rows, rows), :] = wide[d * rows : (d + 1) * rows]


def expand_rows(weights, sums, per_adapter, rank, count):
    rows = sums[0].shape[0] // count * FOLD
    width = weights[0].shape[1]
    return pl.pallas_call(
        functools.partial(
            expand_kernel, per_adapter=per_adapter, rank=rank, count=count, terms=len(sums)
        ),
        out_shape=[jax.ShapeDtypeStruct((rows, width), jnp.bfloat16)] * count,
        in_specs=[VMEM] * (FOLD + len(sums)),
        out_specs=[VMEM] * count,
        compiler_params=pltpu.CompilerParams(vmem_limit_bytes=8 * MIB),
        cost_estimate=BRIEF,
    )(*weights, *sums)


def combine_kernel(here_ref, row_ref, *refs, steps, resident, holders, count, starts):
    pieces, sums, out = refs[:count], refs[count:-3], refs[-3]
    chosen_ref, total_ref = refs[-2:]
    slots, rolls = pieces[0].shape[0], row_ref.shape[1]
    rows = out.shape[0]

    @pl.when(pl.program_id(0) == 0)
    def _():
        _, place = row_slots(row_ref, here_ref[0], resident, holders)
        shape = (rolls, count * slots)
        slot = lax.broadcasted_iota(jnp.int32, shape, 1) // steps
        picked = jnp.where(slot == jnp.broadcast_to(place, shape), 1.0, 0.0).astype(jnp.bfloat16)
        shape = (rows, rolls)
        roll = lax.broadcasted_iota(jnp.int32, shape, 0) // steps
        spread = roll == lax.broadcasted_iota(jnp.int32, shape, 1)
        chosen = dot_nn(jnp.where(spread, 1.0, 0.0).astype(jnp.bfloat16), picked)
        shape = (rows, count * slots)
        step = lax.broadcasted_iota(jnp.int32, shape, 0) % steps
        aligned = step == lax.broadcasted_iota(jnp.int32, shape, 1) % steps
        chosen_ref[...] = jnp.where(aligned, chosen, 0.0).astype(jnp.bfloat16)

    stacked = jnp.concatenate([x[...] for x in pieces], axis=0)
    total_ref[...] = dot_nn(chosen_ref[...], stacked)
    for start, x in zip(starts, sums):
        span = pl.ds(start, x.shape[0])
        total_ref[span, :] += x[...].astype(jnp.float32)
    out[...] = total_ref[...].astype(jnp.bfloat16)


def combine(here, adapter_row, pieces, sums, steps, resident, holders):
    width = pieces[0].shape[1]
    count = len(pieces)
    starts, flat = zip(*sums)
    rows = adapter_row.shape[1] * steps
    block = min(width, 2 * HEAD_SIZE)

    def columns(x):
        return pl.BlockSpec((x, block), lambda j: (0, j))

    return pl.pallas_call(
        functools.partial(
            combine_kernel,
            steps=steps,
            resident=resident,
            holders=holders,
            count=count,
            starts=starts,
        ),
        grid=(width // block,),
        out_shape=jax.ShapeDtypeStruct((rows, width), jnp.bfloat16),
        in_specs=[SMEM, pl.BlockSpec(adapter_row.shape, lambda j: (0, 0))]
        + [columns(x.shape[0]) for x in (*pieces, *flat)],
        out_specs=columns(rows),
        scratch_shapes=[
            pltpu.VMEM((rows, count * pieces[0].shape[0]), jnp.bfloat16),
            pltpu.VMEM((rows, block), jnp.float32),
        ],
        compiler_params=pltpu.CompilerParams(vmem_limit_bytes=20 * MIB),
        cost_estimate=BRIEF,
    )(here, adapter_row, *pieces, *flat)


def local(
    queries,
    shared_prefix_cache,
    rollout_suffix_cache,
    fresh_key_value,
    rollout_prefix_index,
    rollout_suffix_length,
    rollout_adapter_index,
    output_projection_weight,
    adapter_shrink_weight,
    adapter_expand_weight,
):
    rolls, steps, width = queries.shape
    rows = rolls * steps
    prefix_count = shared_prefix_cache.shape[1]
    resident, rank, out_width = adapter_expand_weight.shape
    holders, sides = lax.axis_size("adapter"), lax.axis_size("tensor")
    block, chips = holders // FOLD, sides // 2
    here, side = lax.axis_index("adapter"), lax.axis_index("tensor")
    chip, core = side // 2, side % 2

    def in_block(shift):
        return [(i, i // block * block + (i + shift) % block) for i in range(holders)]

    cores = [(t, t // 2 * 2 + (t + 1) % 2) for t in range(sides)]

    def over_chips(shift):
        return [(t, (t // 2 + shift) % chips * 2 + t % 2) for t in range(sides)]

    own_shrink = adapter_shrink_weight.reshape(resident * rank, width)
    own_expand = adapter_expand_weight.reshape(resident * rank, out_width)
    far = [(i, (i + block) % holders) for i in range(holders)]

    slots = FOLD * resident * MOST * steps
    per_adapter = MOST * steps
    adapter_row = rollout_adapter_index.reshape(1, rolls)
    lengths, prefixes = rollout_suffix_length[None, :], rollout_prefix_index[None, :]
    flat_queries = queries.reshape(rows, width)
    flat_fresh = fresh_key_value.reshape(2, rows, -1)
    here = here.reshape(1).astype(jnp.int32)
    core = core.reshape(1).astype(jnp.int32)
    chip_index = chip.reshape(1).astype(jnp.int32)
    blocks = rolls // BLOCK_ROLLS
    early_blocks = blocks // 2
    tie = lax.optimization_barrier

    def attend_part(lengths, start, count):
        return attend(
            lengths, prefixes, flat_queries, shared_prefix_cache, rollout_suffix_cache,
            flat_fresh, steps, start, count,
        )

    def send_over_chips(away, cuts):
        return [
            lax.ppermute(x, "tensor", over_chips(1 + k // cuts)) for k, x in enumerate(away)
        ]

    def placed(start, own, came, cuts):
        rows = own.shape[0] // cuts
        return [(start, own)] + [(start + k % cuts * rows, x) for k, x in enumerate(came)]

    shrink = lax.ppermute(own_shrink, "adapter", far)
    first = attend_part(lengths, 0, early_blocks)
    send, keep = project(core, first, output_projection_weight, out_width)
    come = lax.ppermute(send, "tensor", cores)
    lengths, shrink, keep, moved_expand = tie((lengths, shrink, keep, own_expand))
    expand = lax.ppermute(moved_expand, "adapter", far)
    second = attend_part(lengths, early_blocks, blocks - early_blocks)
    own_early, *away = pair_sums(chip_index, keep, come, CUTS)
    packed = list(
        pack(here, adapter_row, [first, second], block, slots, steps, resident, holders)
    )
    second, packed[0], away = tie((second, packed[0], away))
    early = send_over_chips(away, CUTS)
    pieces = [packed[0]] + [
        lax.ppermute(packed[d], "adapter", in_block(d)) for d in range(1, block)
    ]
    send, keep = project(core, second, output_projection_weight, out_width)
    own_late, *away = pair_sums(chip_index, keep, lax.ppermute(send, "tensor", cores), 1)
    pieces[0], expand, early = tie((pieces[0], expand, early))
    codes = shrink_rows([own_shrink, shrink], pieces, per_adapter, rank)
    codes = codes + lax.ppermute(codes, "tensor", cores)
    brief = codes.astype(jnp.bfloat16)
    codes = [brief] + [lax.ppermute(brief, "tensor", over_chips(s)) for s in range(1, chips)]
    codes, away = tie((codes, away))
    late = send_over_chips(away, 1)
    wide = expand_rows([own_expand, expand], codes, per_adapter, rank, block)
    back = [wide[0]] + [
        lax.ppermute(wide[d], "adapter", in_block(block - d)) for d in range(1, block)
    ]
    sums = placed(0, own_early, early, CUTS) + placed(first.shape[0], own_late, late, 1)
    mixed = combine(here, adapter_row, back, sums, steps, resident, holders)
    return mixed.reshape(rolls, steps, out_width)


def solution(mesh):
    placed = (
        P("adapter", None, "tensor"),
        P(None, "adapter", None, "tensor"),
        P(None, "adapter", None, "tensor"),
        P(None, "adapter", None, "tensor"),
        P("adapter"),
        P("adapter"),
        P("adapter", None),
        P("tensor", None),
        P("adapter", None, "tensor"),
        P("adapter", None, "tensor"),
    )
    return jax.shard_map(
        local, mesh=mesh, in_specs=placed, out_specs=P("adapter", None, "tensor"), check_vma=False
    )
```

```python
import functools
import math

import jax
import jax.numpy as jnp
from jax import lax
from jax.experimental import pallas as pl
from jax.experimental.pallas import tpu as pltpu
from jax.sharding import PartitionSpec as P

HEAD_SIZE = 128
MOST = 5
FOLD = 2
CUTS = 1
BLOCK_ROLLS = 16
KEY_CHUNK = 512
NEG = float("-inf")
MIB = 1 << 20
BRIEF = pl.CostEstimate(flops=1024, bytes_accessed=1024, transcendentals=0)
LENGTHY = pl.CostEstimate(flops=1 << 36, bytes_accessed=1 << 27, transcendentals=0)
VMEM = pl.BlockSpec(memory_space=pltpu.VMEM)
ANY = pl.BlockSpec(memory_space=pl.ANY)
SMEM = pl.BlockSpec(memory_space=pltpu.SMEM)


def dot_nt(a, b):
    return lax.dot_general(a, b, (((1,), (1,)), ((), ())), preferred_element_type=jnp.float32)


def dot_nn(a, b):
    return jnp.dot(a, b, preferred_element_type=jnp.float32)


def attend_kernel(
    length_ref, prefix_ref, q_ref, kv_hbm, suf_hbm, fr_ref, o_ref,
    s_ref, m_ref, kv_ref, suf_ref, sems,
    *, steps, group, first, blocks
):
    prefix_count, prefix_len = kv_ref.shape[1], kv_ref.shape[2]
    key_heads = kv_ref.shape[3] // HEAD_SIZE
    rolls, suf_len = suf_hbm.shape[1], suf_hbm.shape[2]
    block_rows = BLOCK_ROLLS * steps
    rows = block_rows * group
    last = first + blocks - 1
    suf_rolls = HEAD_SIZE // suf_len
    suf_rows = suf_rolls * steps
    suf_groups = BLOCK_ROLLS // suf_rolls
    window_rolls = HEAD_SIZE // steps
    windows = window_rolls // BLOCK_ROLLS
    factor = HEAD_SIZE ** (-0.5) * math.log2(math.e)
    chunks = prefix_len // KEY_CHUNK
    span = prefix_len

    def row_codes(block):
        shape = (block_rows, rolls)
        mine = block * BLOCK_ROLLS + lax.broadcasted_iota(jnp.int32, shape, 0) // steps
        lane = lax.broadcasted_iota(jnp.int32, shape, 1)
        code = length_ref[...] * prefix_count + prefix_ref[...] % prefix_count
        code = jnp.broadcast_to(code.astype(jnp.float32), shape)
        col = jnp.sum(jnp.where(mine == lane, code, 0.0), axis=1, keepdims=True)
        col = jnp.broadcast_to(col, (block_rows, HEAD_SIZE)).astype(jnp.int32)
        return col // prefix_count, col % prefix_count

    mine = pl.ds(first * BLOCK_ROLLS, blocks * BLOCK_ROLLS)
    loads = []
    for which in range(2):
        loads.append(pltpu.make_async_copy(kv_hbm.at[which], kv_ref.at[which], sems.at[2 * which]))
        loads.append(
            pltpu.make_async_copy(suf_hbm.at[which, mine], suf_ref.at[which], sems.at[2 * which + 1])
        )
    for load in loads:
        load.start()

    def tile_rows(x):
        return jnp.concatenate([x] * group, axis=0)

    def load_q(block, h):
        span = pl.ds(block * BLOCK_ROLLS, BLOCK_ROLLS)
        return [
            q_ref[span, :, pl.ds((h * group + g) * HEAD_SIZE, HEAD_SIZE)].reshape(
                block_rows, HEAD_SIZE
            )
            for g in range(group)
        ]

    def head_lanes(h):
        return pl.ds(h * HEAD_SIZE, HEAD_SIZE)

    def suffix_tile(which, block, i, h):
        start = (block - first) * BLOCK_ROLLS + i * suf_rolls
        tile = suf_ref[which, pl.ds(start, suf_rolls), :, head_lanes(h)]
        return tile.reshape(HEAD_SIZE, HEAD_SIZE)

    def fresh_tile(which, block, h):
        span = pl.ds(block // windows * window_rolls, window_rolls)
        return fr_ref[which, span, :, head_lanes(h)].reshape(HEAD_SIZE, HEAD_SIZE)

    def prefix_tile(which, c, h):
        return jnp.concatenate(
            [
                kv_ref[which, p, pl.ds(c * KEY_CHUNK, KEY_CHUNK), head_lanes(h)]
                for p in range(prefix_count)
            ],
            axis=1,
        )

    def scores(block, h, slot):
        length, local = row_codes(block)
        parts = load_q(block, h)
        stacked = jnp.concatenate(parts, axis=0)
        wide = jnp.concatenate(
            [
                jnp.concatenate(
                    [jnp.where(local == p, x, jnp.zeros_like(x)) for x in parts], axis=0
                )
                for p in range(prefix_count)
            ],
            axis=1,
        )
        shape = (block_rows, HEAD_SIZE)
        row = lax.broadcasted_iota(jnp.int32, shape, 0)
        lane = lax.broadcasted_iota(jnp.int32, shape, 1)
        roll = row // steps
        keep = (roll % suf_rolls == lane // suf_len) & (lane % suf_len < length)
        suf_bias = jnp.where(keep, 0.0, NEG)
        in_window = (block % windows) * BLOCK_ROLLS + roll
        keep = (in_window == lane // steps) & (lane % steps <= row % steps)
        fr_bias = jnp.where(keep, 0.0, NEG)
        suf = []
        for i in range(suf_groups):
            piece = jnp.concatenate(
                [x[i * suf_rows : (i + 1) * suf_rows] for x in parts], axis=0
            )
            suf.append(dot_nt(piece, suffix_tile(0, block, i, h)))
        suf = jnp.concatenate(
            [
                jnp.concatenate([x[g * suf_rows : (g + 1) * suf_rows] for x in suf], axis=0)
                for g in range(group)
            ],
            axis=0,
        ) + tile_rows(suf_bias)
        fr = dot_nt(stacked, fresh_tile(0, block, h)) + tile_rows(fr_bias)
        s_ref[slot, :, pl.ds(span, HEAD_SIZE)] = suf
        s_ref[slot, :, pl.ds(span + HEAD_SIZE, HEAD_SIZE)] = fr
        top = jnp.maximum(suf, fr)
        yield
        for c in range(chunks):
            s = dot_nt(wide, prefix_tile(0, c, h))
            s_ref[slot, :, pl.ds(c * KEY_CHUNK, KEY_CHUNK)] = s
            for j in range(KEY_CHUNK // HEAD_SIZE):
                top = jnp.maximum(top, s[:, j * HEAD_SIZE : (j + 1) * HEAD_SIZE])
            if c == chunks - 1:
                top = jnp.max(top, axis=1, keepdims=True) * factor
                m_ref[slot] = jnp.broadcast_to(top, (rows, HEAD_SIZE))
            yield

    def outputs(block, h, slot):
        top = m_ref[slot]

        def weigh(start, width):
            x = s_ref[slot, :, pl.ds(start, width)]
            wide_top = jnp.concatenate([top] * (width // HEAD_SIZE), axis=1)
            return jnp.exp2(x * factor - wide_top)

        both = weigh(span, 2 * HEAD_SIZE)
        total = both[:, :HEAD_SIZE] + both[:, HEAD_SIZE:]
        both = both.astype(jnp.bfloat16)
        fr = dot_nn(both[:, HEAD_SIZE:], fresh_tile(1, block, h))
        suf = []
        for i in range(suf_groups):
            piece = jnp.concatenate(
                [
                    both[
                        g * block_rows + i * suf_rows : g * block_rows + (i + 1) * suf_rows,
                        :HEAD_SIZE,
                    ]
                    for g in range(group)
                ],
                axis=0,
            )
            suf.append(dot_nn(piece, suffix_tile(1, block, i, h)))
        extra = fr + jnp.concatenate(
            [
                jnp.concatenate([x[g * suf_rows : (g + 1) * suf_rows] for x in suf], axis=0)
                for g in range(group)
            ],
            axis=0,
        )
        yield
        acc = None
        for c in range(chunks):
            p = weigh(c * KEY_CHUNK, KEY_CHUNK)
            for j in range(KEY_CHUNK // HEAD_SIZE):
                total = total + p[:, j * HEAD_SIZE : (j + 1) * HEAD_SIZE]
            part = dot_nn(p.astype(jnp.bfloat16), prefix_tile(1, c, h))
            acc = part if acc is None else acc + part
            if c == chunks - 1:
                _, local = row_codes(block)
                local = tile_rows(local)
                chosen = acc[:, :HEAD_SIZE]
                for q in range(1, prefix_count):
                    chosen = jnp.where(
                        local == q, acc[:, q * HEAD_SIZE : (q + 1) * HEAD_SIZE], chosen
                    )
                weight = 1.0 / jnp.sum(total, axis=1, keepdims=True)
                out = ((chosen + extra) * weight).astype(o_ref.dtype)
                start = pl.multiple_of((block - first) * block_rows, block_rows)
                for g in range(group):
                    o_ref[
                        pl.ds(start, block_rows),
                        pl.ds((h * group + g) * HEAD_SIZE, HEAD_SIZE),
                    ] = out[g * block_rows : (g + 1) * block_rows]
            yield

    def run(*streams):
        for _ in range(chunks + 1):
            for stream in streams:
                next(stream)

    for load in loads[:2]:
        load.wait()
    run(scores(first, 0, 0))
    for load in loads[2:]:
        load.wait()

    def body(block, carry):
        for h in range(key_heads):
            if h + 1 < key_heads:
                run(scores(block, h + 1, h + 1), outputs(block, h, h))
            elif key_heads > 1:
                following = jnp.minimum(block + 1, last)
                run(scores(following, 0, 0), outputs(block, h, h))
            else:
                run(outputs(block, h, h))
                run(scores(jnp.minimum(block + 1, last), 0, 0))
        return carry

    lax.fori_loop(first, first + blocks, body, 0)


def attend(lengths, prefixes, queries, prefix, suffix, fresh, steps, first, blocks):
    width = queries.shape[-1]
    rows = blocks * BLOCK_ROLLS * steps
    key_heads = prefix.shape[3] // HEAD_SIZE
    group = width // HEAD_SIZE // key_heads
    unit_rows = BLOCK_ROLLS * steps * group
    span = prefix.shape[2] + 2 * HEAD_SIZE
    held = (2, blocks * BLOCK_ROLLS) + suffix.shape[2:]
    return pl.pallas_call(
        functools.partial(attend_kernel, steps=steps, group=group, first=first, blocks=blocks),
        out_shape=jax.ShapeDtypeStruct((rows, width), jnp.bfloat16),
        in_specs=[VMEM, VMEM, VMEM, ANY, ANY, VMEM],
        out_specs=VMEM,
        scratch_shapes=[
            pltpu.VMEM((key_heads, unit_rows, span), jnp.float32),
            pltpu.VMEM((key_heads, unit_rows, HEAD_SIZE), jnp.float32),
            pltpu.VMEM(prefix.shape, prefix.dtype),
            pltpu.VMEM(held, suffix.dtype),
            pltpu.SemaphoreType.DMA((4,)),
        ],
        compiler_params=pltpu.CompilerParams(vmem_limit_bytes=52 * MIB),
        cost_estimate=LENGTHY,
    )(lengths, prefixes, queries, prefix, suffix, fresh)


def project_kernel(core_ref, a_ref, w_ref, send_ref, keep_ref, *, count):
    step = pl.program_id(0)
    part = dot_nn(a_ref[...], w_ref[...]).astype(jnp.bfloat16)

    @pl.when(step < count)
    def _():
        send_ref[0] = part

    @pl.when(step >= count)
    def _():
        keep_ref[0] = part


def project(core, attended, weight, out_width):
    rows, width = attended.shape
    count = weight.shape[1] // out_width // 2

    def column(j, core):
        parity = jnp.where(j < count, 1 - core[0], core[0])
        return (0, (j % count) * 2 + parity)

    shape = jax.ShapeDtypeStruct((count, rows, out_width), jnp.bfloat16)
    return pl.pallas_call(
        functools.partial(project_kernel, count=count),
        grid_spec=pltpu.PrefetchScalarGridSpec(
            num_scalar_prefetch=1,
            grid=(2 * count,),
            in_specs=[
                pl.BlockSpec((rows, width), lambda j, core: (0, 0)),
                pl.BlockSpec((width, out_width), column),
            ],
            out_specs=[
                pl.BlockSpec((1, rows, out_width), lambda j, core: (jnp.minimum(j, count - 1), 0, 0)),
                pl.BlockSpec((1, rows, out_width), lambda j, core: (jnp.maximum(j - count, 0), 0, 0)),
            ],
        ),
        out_shape=[shape, shape],
        compiler_params=pltpu.CompilerParams(vmem_limit_bytes=8 * MIB),
        cost_estimate=BRIEF,
    )(core, attended, weight)


def pair_kernel(chip_ref, keep_ref, come_ref, own_ref, *outs, cuts):
    chips = keep_ref.shape[0]
    for shift in range(chips):
        index = (chip_ref[0] + shift) % chips
        pair = keep_ref[index].astype(jnp.float32) + come_ref[index].astype(jnp.float32)
        pair = pair.astype(jnp.bfloat16)
        if shift == 0:
            own_ref[...] = pair
        else:
            for k in range(cuts):
                out = outs[(shift - 1) * cuts + k]
                rows = out.shape[0]
                out[...] = pair[k * rows : (k + 1) * rows]


def pair_sums(chip, keep, come, cuts):
    chips, rows, width = keep.shape
    away = [jax.ShapeDtypeStruct((rows // cuts, width), jnp.bfloat16)] * ((chips - 1) * cuts)
    return pl.pallas_call(
        functools.partial(pair_kernel, cuts=cuts),
        out_shape=[jax.ShapeDtypeStruct((rows, width), jnp.bfloat16)] + away,
        in_specs=[SMEM, VMEM, VMEM],
        out_specs=[VMEM] * (1 + len(away)),
        compiler_params=pltpu.CompilerParams(vmem_limit_bytes=12 * MIB),
        cost_estimate=BRIEF,
    )(chip, keep, come)


def slot_of(row, turn, here, resident, holders):
    block = holders // FOLD
    holder = row // resident
    fold = (here // block - holder // block + FOLD) % FOLD
    place = (holder % block - here % block + block) % block
    return ((place * FOLD + fold) * resident + row % resident) * MOST + turn


def row_slots(row_ref, here, resident, holders):
    row = row_ref[...]
    shape = (row.shape[1], row.shape[1])
    across = jnp.broadcast_to(row, shape)
    down, lane = lax.broadcasted_iota(jnp.int32, shape, 0), lax.broadcasted_iota(jnp.int32, shape, 1)
    values = across.astype(jnp.float32)
    col = jnp.sum(jnp.where(down == lane, values, 0.0), axis=1, keepdims=True)
    same = jnp.broadcast_to(col, shape) == values
    turn_row = jnp.sum(jnp.where(same & (down < lane), 1.0, 0.0), axis=0, keepdims=True)
    turn_col = jnp.sum(jnp.where(same & (lane < down), 1.0, 0.0), axis=1, keepdims=True)
    place_row = slot_of(row, turn_row.astype(jnp.int32), here, resident, holders)
    place_col = slot_of(
        jnp.broadcast_to(col, shape).astype(jnp.int32),
        jnp.broadcast_to(turn_col, shape).astype(jnp.int32),
        here,
        resident,
        holders,
    )
    return place_row, place_col[:, :1]


def pack_kernel(here_ref, row_ref, *refs, steps, resident, holders, count):
    parts, outs = refs[:-count], refs[-count:]
    slots, rolls = outs[0].shape[0], row_ref.shape[1]
    place, _ = row_slots(row_ref, here_ref[0], resident, holders)
    for d, out in enumerate(outs):
        shape = (slots, rolls)
        slot = (d * slots + lax.broadcasted_iota(jnp.int32, shape, 0)) // steps
        picked = jnp.where(slot == jnp.broadcast_to(place, shape), 1.0, 0.0).astype(jnp.bfloat16)
        total, start = None, 0
        for part in parts:
            rows = part.shape[0]
            shape = (rolls, rows)
            spread = lax.broadcasted_iota(jnp.int32, shape, 0) == (
                start + lax.broadcasted_iota(jnp.int32, shape, 1)
            ) // steps
            chosen = dot_nn(picked, jnp.where(spread, 1.0, 0.0).astype(jnp.bfloat16))
            shape = (slots, rows)
            step = lax.broadcasted_iota(jnp.int32, shape, 0) % steps
            aligned = step == (start + lax.broadcasted_iota(jnp.int32, shape, 1)) % steps
            chosen = jnp.where(aligned, chosen, 0.0).astype(jnp.bfloat16)
            term = dot_nn(chosen, part[...])
            total = term if total is None else total + term
            start += rows
        out[...] = total.astype(jnp.bfloat16)


def pack(here, adapter_row, parts, count, slots, steps, resident, holders):
    width = parts[0].shape[1]
    return pl.pallas_call(
        functools.partial(
            pack_kernel, steps=steps, resident=resident, holders=holders, count=count
        ),
        out_shape=[jax.ShapeDtypeStruct((slots, width), jnp.bfloat16)] * count,
        in_specs=[SMEM] + [VMEM] * (1 + len(parts)),
        out_specs=[VMEM] * count,
        compiler_params=pltpu.CompilerParams(vmem_limit_bytes=12 * MIB),
        cost_estimate=BRIEF,
    )(here, adapter_row, *parts)


def adapter_mask(rows, per_adapter, rank, tile):
    lane = lax.broadcasted_iota(jnp.int32, (rows, HEAD_SIZE), 1) + tile * HEAD_SIZE
    row = lax.broadcasted_iota(jnp.int32, (rows, HEAD_SIZE), 0)
    return lane // rank == row // per_adapter


def shrink_kernel(*refs, per_adapter, rank, count):
    weights, pieces, out = refs[:FOLD], refs[FOLD : FOLD + count], refs[-1]
    rows = pieces[0].shape[0] // FOLD
    found = []
    for k in range(FOLD):
        span = pl.ds(k * rows, rows)
        every = dot_nt(
            jnp.concatenate([p[span, :] for p in pieces], axis=0),
            weights[k][...],
        )
        for d in range(count):
            total = None
            for tile in range(every.shape[1] // HEAD_SIZE):
                x = every[d * rows : (d + 1) * rows, tile * HEAD_SIZE : (tile + 1) * HEAD_SIZE]
                x = jnp.where(adapter_mask(rows, per_adapter, rank, tile), x, 0.0)
                total = x if total is None else total + x
            summed = total
            for turn in range(1, HEAD_SIZE // rank):
                summed = summed + pltpu.roll(total, turn * rank, axis=1)
            found.append(summed)
    lane = lax.broadcasted_iota(jnp.int32, (rows, HEAD_SIZE), 1)
    for d in range(count):
        both = jnp.where(lane < rank, found[d], found[count + d])
        out[pl.ds(d * rows, rows), :] = both


def shrink_rows(weights, pieces, per_adapter, rank):
    count = len(pieces)
    rows, width = pieces[0].shape
    return pl.pallas_call(
        functools.partial(shrink_kernel, per_adapter=per_adapter, rank=rank, count=count),
        out_shape=jax.ShapeDtypeStruct((count * rows // FOLD, HEAD_SIZE), jnp.float32),
        in_specs=[VMEM] * (FOLD + count),
        out_specs=VMEM,
        compiler_params=pltpu.CompilerParams(vmem_limit_bytes=8 * MIB),
        cost_estimate=LENGTHY,
    )(*weights, *pieces)


def expand_kernel(*refs, per_adapter, rank, count, terms):
    weights, sums, outs = refs[:FOLD], refs[FOLD : FOLD + terms], refs[FOLD + terms :]
    depth = weights[0].shape[0]
    rows = outs[0].shape[0] // FOLD
    for k in range(FOLD):
        spread = []
        for d in range(count):
            span = pl.ds(d * rows, rows)
            code = sums[0][span, :].astype(jnp.float32)
            for other in sums[1:]:
                code = code + other[span, :].astype(jnp.float32)
            lane = lax.broadcasted_iota(jnp.int32, (rows, HEAD_SIZE), 1)
            turned = pltpu.roll(code, rank, axis=1)
            code = jnp.where((lane < rank) == (k == 0), code, turned)
            spread.append(
                jnp.concatenate(
                    [
                        jnp.where(adapter_mask(rows, per_adapter, rank, tile), code, 0.0)
                        for tile in range(depth // HEAD_SIZE)
                    ],
                    axis=1,
                ).astype(jnp.bfloat16)
            )
        wide = dot_nn(jnp.concatenate(spread, axis=0), weights[k][...])
        wide = wide.astype(jnp.bfloat16)
        for d in range(count):
            outs[d][pl.ds(k * rows, rows), :] = wide[d * rows : (d + 1) * rows]


def expand_rows(weights, sums, per_adapter, rank, count):
    rows = sums[0].shape[0] // count * FOLD
    width = weights[0].shape[1]
    return pl.pallas_call(
        functools.partial(
            expand_kernel, per_adapter=per_adapter, rank=rank, count=count, terms=len(sums)
        ),
        out_shape=[jax.ShapeDtypeStruct((rows, width), jnp.bfloat16)] * count,
        in_specs=[VMEM] * (FOLD + len(sums)),
        out_specs=[VMEM] * count,
        compiler_params=pltpu.CompilerParams(vmem_limit_bytes=8 * MIB),
        cost_estimate=BRIEF,
    )(*weights, *sums)


def combine_kernel(here_ref, row_ref, *refs, steps, resident, holders, count, starts):
    pieces, sums, out = refs[:count], refs[count:-3], refs[-3]
    chosen_ref, total_ref = refs[-2:]
    slots, rolls = pieces[0].shape[0], row_ref.shape[1]
    rows = out.shape[0] * out.shape[1]

    @pl.when(pl.program_id(0) == 0)
    def _():
        _, place = row_slots(row_ref, here_ref[0], resident, holders)
        shape = (rolls, count * slots)
        slot = lax.broadcasted_iota(jnp.int32, shape, 1) // steps
        picked = jnp.where(slot == jnp.broadcast_to(place, shape), 1.0, 0.0).astype(jnp.bfloat16)
        shape = (rows, rolls)
        roll = lax.broadcasted_iota(jnp.int32, shape, 0) // steps
        spread = roll == lax.broadcasted_iota(jnp.int32, shape, 1)
        chosen = dot_nn(jnp.where(spread, 1.0, 0.0).astype(jnp.bfloat16), picked)
        shape = (rows, count * slots)
        step = lax.broadcasted_iota(jnp.int32, shape, 0) % steps
        aligned = step == lax.broadcasted_iota(jnp.int32, shape, 1) % steps
        chosen_ref[...] = jnp.where(aligned, chosen, 0.0).astype(jnp.bfloat16)

    stacked = jnp.concatenate([x[...] for x in pieces], axis=0)
    total_ref[...] = dot_nn(chosen_ref[...], stacked)
    for start, x in zip(starts, sums):
        span = pl.ds(start, x.shape[0])
        total_ref[span, :] += x[...].astype(jnp.float32)
    out[...] = total_ref[...].reshape(out.shape).astype(jnp.bfloat16)


def combine(here, adapter_row, pieces, sums, steps, resident, holders):
    width = pieces[0].shape[1]
    count = len(pieces)
    starts, flat = zip(*sums)
    rows = adapter_row.shape[1] * steps
    block = min(width, 2 * HEAD_SIZE)

    def columns(x):
        return pl.BlockSpec((x, block), lambda j: (0, j))

    return pl.pallas_call(
        functools.partial(
            combine_kernel,
            steps=steps,
            resident=resident,
            holders=holders,
            count=count,
            starts=starts,
        ),
        grid=(width // block,),
        out_shape=jax.ShapeDtypeStruct((rows // steps, steps, width), jnp.bfloat16),
        in_specs=[SMEM, pl.BlockSpec(adapter_row.shape, lambda j: (0, 0))]
        + [columns(x.shape[0]) for x in (*pieces, *flat)],
        out_specs=pl.BlockSpec((rows // steps, steps, block), lambda j: (0, 0, j)),
        scratch_shapes=[
            pltpu.VMEM((rows, count * pieces[0].shape[0]), jnp.bfloat16),
            pltpu.VMEM((rows, block), jnp.float32),
        ],
        compiler_params=pltpu.CompilerParams(vmem_limit_bytes=20 * MIB),
        cost_estimate=BRIEF,
    )(here, adapter_row, *pieces, *flat)


def local(
    queries,
    shared_prefix_cache,
    rollout_suffix_cache,
    fresh_key_value,
    rollout_prefix_index,
    rollout_suffix_length,
    rollout_adapter_index,
    output_projection_weight,
    adapter_shrink_weight,
    adapter_expand_weight,
):
    rolls, steps, width = queries.shape
    rows = rolls * steps
    prefix_count = shared_prefix_cache.shape[1]
    resident, rank, out_width = adapter_expand_weight.shape
    holders, sides = lax.axis_size("adapter"), lax.axis_size("tensor")
    block, chips = holders // FOLD, sides // 2
    here, side = lax.axis_index("adapter"), lax.axis_index("tensor")
    chip, core = side // 2, side % 2

    def in_block(shift):
        return [(i, i // block * block + (i + shift) % block) for i in range(holders)]

    cores = [(t, t // 2 * 2 + (t + 1) % 2) for t in range(sides)]

    def over_chips(shift):
        return [(t, (t // 2 + shift) % chips * 2 + t % 2) for t in range(sides)]

    own_shrink = adapter_shrink_weight.reshape(resident * rank, width)
    own_expand = adapter_expand_weight.reshape(resident * rank, out_width)
    far = [(i, (i + block) % holders) for i in range(holders)]

    slots = FOLD * resident * MOST * steps
    per_adapter = MOST * steps
    adapter_row = rollout_adapter_index.reshape(1, rolls)
    lengths, prefixes = rollout_suffix_length[None, :], rollout_prefix_index[None, :]
    here = here.reshape(1).astype(jnp.int32)
    core = core.reshape(1).astype(jnp.int32)
    chip_index = chip.reshape(1).astype(jnp.int32)
    tie = lax.optimization_barrier

    def send_over_chips(away, cuts):
        return [
            lax.ppermute(x, "tensor", over_chips(1 + k // cuts)) for k, x in enumerate(away)
        ]

    def placed(start, own, came, cuts):
        rows = own.shape[0] // cuts
        return [(start, own)] + [(start + k % cuts * rows, x) for k, x in enumerate(came)]

    shrink = lax.ppermute(own_shrink, "adapter", far)
    expand = lax.ppermute(own_expand, "adapter", far)
    attended = attend(
        lengths, prefixes, queries, shared_prefix_cache, rollout_suffix_cache, fresh_key_value,
        steps, 0, rolls // BLOCK_ROLLS,
    )
    packed = list(pack(here, adapter_row, [attended], block, slots, steps, resident, holders))
    attended, packed[0] = tie((attended, packed[0]))
    pieces = [packed[0]] + [
        lax.ppermute(packed[d], "adapter", in_block(d)) for d in range(1, block)
    ]
    send, keep = project(core, attended, output_projection_weight, out_width)
    own, *away = pair_sums(chip_index, keep, lax.ppermute(send, "tensor", cores), 1)
    pieces[0], shrink, expand = tie((pieces[0], shrink, expand))
    codes = shrink_rows([own_shrink, shrink], pieces, per_adapter, rank)
    codes = codes + lax.ppermute(codes, "tensor", cores)
    brief = codes.astype(jnp.bfloat16)
    codes = [brief] + [lax.ppermute(brief, "tensor", over_chips(s)) for s in range(1, chips)]
    codes, away = tie((codes, away))
    came = send_over_chips(away, 1)
    wide = expand_rows([own_expand, expand], codes, per_adapter, rank, block)
    back = [wide[0]] + [
        lax.ppermute(wide[d], "adapter", in_block(block - d)) for d in range(1, block)
    ]
    return combine(here, adapter_row, back, placed(0, own, came, 1), steps, resident, holders)


def solution(mesh):
    placed = (
        P("adapter", None, "tensor"),
        P(None, "adapter", None, "tensor"),
        P(None, "adapter", None, "tensor"),
        P(None, "adapter", None, "tensor"),
        P("adapter"),
        P("adapter"),
        P("adapter", None),
        P("tensor", None),
        P("adapter", None, "tensor"),
        P("adapter", None, "tensor"),
    )
    return jax.shard_map(
        local, mesh=mesh, in_specs=placed, out_specs=P("adapter", None, "tensor"), check_vma=False
    )
```

```python
import functools
import math

import jax
import jax.numpy as jnp
from jax import lax
from jax.experimental import pallas as pl
from jax.experimental.pallas import tpu as pltpu
from jax.sharding import PartitionSpec as P

HEAD_SIZE = 128
MOST = 5
FOLD = 2
CUTS = 1
BLOCK_ROLLS = 32
KEY_CHUNK = 512
NEG = float("-inf")
MIB = 1 << 20
BRIEF = pl.CostEstimate(flops=1024, bytes_accessed=1024, transcendentals=0)
LENGTHY = pl.CostEstimate(flops=1 << 36, bytes_accessed=1 << 27, transcendentals=0)
VMEM = pl.BlockSpec(memory_space=pltpu.VMEM)
ANY = pl.BlockSpec(memory_space=pl.ANY)
SMEM = pl.BlockSpec(memory_space=pltpu.SMEM)


def dot_nt(a, b):
    return lax.dot_general(a, b, (((1,), (1,)), ((), ())), preferred_element_type=jnp.float32)


def dot_nn(a, b):
    return jnp.dot(a, b, preferred_element_type=jnp.float32)


def attend_kernel(
    length_hbm, prefix_hbm, q_hbm, kv_hbm, suf_hbm, fr_hbm, o_ref,
    s_ref, m_ref, length_ref, prefix_ref, q_ref, kv_ref, suf_ref, fr_ref, sems,
    *, steps, group, first, blocks
):
    prefix_count, prefix_len = kv_ref.shape[1], kv_ref.shape[2]
    key_heads = kv_ref.shape[3] // HEAD_SIZE
    rolls, suf_len = suf_hbm.shape[1], suf_hbm.shape[2]
    block_rows = BLOCK_ROLLS * steps
    rows = block_rows * group
    last = first + blocks - 1
    suf_rolls = HEAD_SIZE // suf_len
    suf_rows = suf_rolls * steps
    suf_groups = BLOCK_ROLLS // suf_rolls
    window_rolls = HEAD_SIZE // steps
    windows = window_rolls // BLOCK_ROLLS
    factor = HEAD_SIZE ** (-0.5) * math.log2(math.e)
    chunks = prefix_len // KEY_CHUNK
    span = prefix_len

    def row_codes(block):
        shape = (block_rows, rolls)
        mine = block * BLOCK_ROLLS + lax.broadcasted_iota(jnp.int32, shape, 0) // steps
        lane = lax.broadcasted_iota(jnp.int32, shape, 1)
        code = length_ref[...] * prefix_count + prefix_ref[...] % prefix_count
        code = jnp.broadcast_to(code.astype(jnp.float32), shape)
        col = jnp.sum(jnp.where(mine == lane, code, 0.0), axis=1, keepdims=True)
        col = jnp.broadcast_to(col, (block_rows, HEAD_SIZE)).astype(jnp.int32)
        return col // prefix_count, col % prefix_count

    mine = pl.ds(first * BLOCK_ROLLS, blocks * BLOCK_ROLLS)
    loads = []
    for which in range(2):
        loads.append(pltpu.make_async_copy(kv_hbm.at[which], kv_ref.at[which], sems.at[2 * which]))
        loads.append(
            pltpu.make_async_copy(suf_hbm.at[which, mine], suf_ref.at[which], sems.at[2 * which + 1])
        )
    small = [
        pltpu.make_async_copy(src, dst, sems.at[4 + k])
        for k, (src, dst) in enumerate(
            [(q_hbm, q_ref), (fr_hbm, fr_ref), (length_hbm, length_ref), (prefix_hbm, prefix_ref)]
        )
    ]
    for load in [*reversed(small), *loads]:
        load.start()

    def tile_rows(x):
        return jnp.concatenate([x] * group, axis=0)

    def load_q(block, h):
        span = pl.ds(block * BLOCK_ROLLS, BLOCK_ROLLS)
        return [
            q_ref[span, :, pl.ds((h * group + g) * HEAD_SIZE, HEAD_SIZE)].reshape(
                block_rows, HEAD_SIZE
            )
            for g in range(group)
        ]

    def head_lanes(h):
        return pl.ds(h * HEAD_SIZE, HEAD_SIZE)

    def suffix_tile(which, block, i, h):
        start = (block - first) * BLOCK_ROLLS + i * suf_rolls
        tile = suf_ref[which, pl.ds(start, suf_rolls), :, head_lanes(h)]
        return tile.reshape(HEAD_SIZE, HEAD_SIZE)

    def fresh_tile(which, block, h):
        span = pl.ds(block // windows * window_rolls, window_rolls)
        return fr_ref[which, span, :, head_lanes(h)].reshape(HEAD_SIZE, HEAD_SIZE)

    def prefix_tile(which, c, h):
        return jnp.concatenate(
            [
                kv_ref[which, p, pl.ds(c * KEY_CHUNK, KEY_CHUNK), head_lanes(h)]
                for p in range(prefix_count)
            ],
            axis=1,
        )

    def scores(block, h, slot):
        length, local = row_codes(block)
        parts = load_q(block, h)
        stacked = jnp.concatenate(parts, axis=0)
        wide = jnp.concatenate(
            [
                jnp.concatenate(
                    [jnp.where(local == p, x, jnp.zeros_like(x)) for x in parts], axis=0
                )
                for p in range(prefix_count)
            ],
            axis=1,
        )
        shape = (block_rows, HEAD_SIZE)
        row = lax.broadcasted_iota(jnp.int32, shape, 0)
        lane = lax.broadcasted_iota(jnp.int32, shape, 1)
        roll = row // steps
        keep = (roll % suf_rolls == lane // suf_len) & (lane % suf_len < length)
        suf_bias = jnp.where(keep, 0.0, NEG)
        in_window = (block % windows) * BLOCK_ROLLS + roll
        keep = (in_window == lane // steps) & (lane % steps <= row % steps)
        fr_bias = jnp.where(keep, 0.0, NEG)
        suf = []
        for i in range(suf_groups):
            piece = jnp.concatenate(
                [x[i * suf_rows : (i + 1) * suf_rows] for x in parts], axis=0
            )
            suf.append(dot_nt(piece, suffix_tile(0, block, i, h)))
        suf = jnp.concatenate(
            [
                jnp.concatenate([x[g * suf_rows : (g + 1) * suf_rows] for x in suf], axis=0)
                for g in range(group)
            ],
            axis=0,
        ) + tile_rows(suf_bias)
        fr = dot_nt(stacked, fresh_tile(0, block, h)) + tile_rows(fr_bias)
        s_ref[slot, :, pl.ds(span, HEAD_SIZE)] = suf
        s_ref[slot, :, pl.ds(span + HEAD_SIZE, HEAD_SIZE)] = fr
        top = jnp.maximum(suf, fr)
        yield
        for c in range(chunks):
            s = dot_nt(wide, prefix_tile(0, c, h))
            s_ref[slot, :, pl.ds(c * KEY_CHUNK, KEY_CHUNK)] = s
            for j in range(KEY_CHUNK // HEAD_SIZE):
                top = jnp.maximum(top, s[:, j * HEAD_SIZE : (j + 1) * HEAD_SIZE])
            if c == chunks - 1:
                top = jnp.max(top, axis=1, keepdims=True) * factor
                m_ref[slot] = jnp.broadcast_to(top, (rows, HEAD_SIZE))
            yield

    def outputs(block, h, slot):
        top = m_ref[slot]

        def weigh(start, width):
            x = s_ref[slot, :, pl.ds(start, width)]
            wide_top = jnp.concatenate([top] * (width // HEAD_SIZE), axis=1)
            return jnp.exp2(x * factor - wide_top)

        both = weigh(span, 2 * HEAD_SIZE)
        total = both[:, :HEAD_SIZE] + both[:, HEAD_SIZE:]
        both = both.astype(jnp.bfloat16)
        fr = dot_nn(both[:, HEAD_SIZE:], fresh_tile(1, block, h))
        suf = []
        for i in range(suf_groups):
            piece = jnp.concatenate(
                [
                    both[
                        g * block_rows + i * suf_rows : g * block_rows + (i + 1) * suf_rows,
                        :HEAD_SIZE,
                    ]
                    for g in range(group)
                ],
                axis=0,
            )
            suf.append(dot_nn(piece, suffix_tile(1, block, i, h)))
        extra = fr + jnp.concatenate(
            [
                jnp.concatenate([x[g * suf_rows : (g + 1) * suf_rows] for x in suf], axis=0)
                for g in range(group)
            ],
            axis=0,
        )
        yield
        acc = None
        for c in range(chunks):
            p = weigh(c * KEY_CHUNK, KEY_CHUNK)
            for j in range(KEY_CHUNK // HEAD_SIZE):
                total = total + p[:, j * HEAD_SIZE : (j + 1) * HEAD_SIZE]
            part = dot_nn(p.astype(jnp.bfloat16), prefix_tile(1, c, h))
            acc = part if acc is None else acc + part
            if c == chunks - 1:
                _, local = row_codes(block)
                local = tile_rows(local)
                chosen = acc[:, :HEAD_SIZE]
                for q in range(1, prefix_count):
                    chosen = jnp.where(
                        local == q, acc[:, q * HEAD_SIZE : (q + 1) * HEAD_SIZE], chosen
                    )
                weight = 1.0 / jnp.sum(total, axis=1, keepdims=True)
                out = ((chosen + extra) * weight).astype(o_ref.dtype)
                start = pl.multiple_of((block - first) * block_rows, block_rows)
                for g in range(group):
                    o_ref[
                        pl.ds(start, block_rows),
                        pl.ds((h * group + g) * HEAD_SIZE, HEAD_SIZE),
                    ] = out[g * block_rows : (g + 1) * block_rows]
            yield

    def run(*streams):
        for _ in range(chunks + 1):
            for stream in streams:
                next(stream)

    for load in [*reversed(small), *loads[:2]]:
        load.wait()
    run(scores(first, 0, 0))
    for load in loads[2:]:
        load.wait()

    def body(block, carry):
        for h in range(key_heads):
            if h + 1 < key_heads:
                run(scores(block, h + 1, h + 1), outputs(block, h, h))
            elif key_heads > 1:
                following = jnp.minimum(block + 1, last)
                run(scores(following, 0, 0), outputs(block, h, h))
            else:
                run(outputs(block, h, h))
                run(scores(jnp.minimum(block + 1, last), 0, 0))
        return carry

    lax.fori_loop(first, first + blocks, body, 0)


def attend(lengths, prefixes, queries, prefix, suffix, fresh, steps, first, blocks):
    width = queries.shape[-1]
    rows = blocks * BLOCK_ROLLS * steps
    key_heads = prefix.shape[3] // HEAD_SIZE
    group = width // HEAD_SIZE // key_heads
    unit_rows = BLOCK_ROLLS * steps * group
    span = prefix.shape[2] + 2 * HEAD_SIZE
    held = (2, blocks * BLOCK_ROLLS) + suffix.shape[2:]
    return pl.pallas_call(
        functools.partial(attend_kernel, steps=steps, group=group, first=first, blocks=blocks),
        out_shape=jax.ShapeDtypeStruct((rows, width), jnp.bfloat16),
        in_specs=[ANY] * 6,
        out_specs=VMEM,
        scratch_shapes=[
            pltpu.VMEM((key_heads, unit_rows, span), jnp.float32),
            pltpu.VMEM((key_heads, unit_rows, HEAD_SIZE), jnp.float32),
            pltpu.VMEM(lengths.shape, lengths.dtype),
            pltpu.VMEM(prefixes.shape, prefixes.dtype),
            pltpu.VMEM(queries.shape, queries.dtype),
            pltpu.VMEM(prefix.shape, prefix.dtype),
            pltpu.VMEM(held, suffix.dtype),
            pltpu.VMEM(fresh.shape, fresh.dtype),
            pltpu.SemaphoreType.DMA((8,)),
        ],
        compiler_params=pltpu.CompilerParams(vmem_limit_bytes=52 * MIB),
        cost_estimate=LENGTHY,
    )(lengths, prefixes, queries, prefix, suffix, fresh)


def project_kernel(core_ref, a_ref, w_ref, send_ref, keep_ref, *, count):
    step = pl.program_id(0)
    part = dot_nn(a_ref[...], w_ref[...]).astype(jnp.bfloat16)

    @pl.when(step < count)
    def _():
        send_ref[0] = part

    @pl.when(step >= count)
    def _():
        keep_ref[0] = part


def project(core, attended, weight, out_width):
    rows, width = attended.shape
    count = weight.shape[1] // out_width // 2

    def column(j, core):
        parity = jnp.where(j < count, 1 - core[0], core[0])
        return (0, (j % count) * 2 + parity)

    shape = jax.ShapeDtypeStruct((count, rows, out_width), jnp.bfloat16)
    return pl.pallas_call(
        functools.partial(project_kernel, count=count),
        grid_spec=pltpu.PrefetchScalarGridSpec(
            num_scalar_prefetch=1,
            grid=(2 * count,),
            in_specs=[
                pl.BlockSpec((rows, width), lambda j, core: (0, 0)),
                pl.BlockSpec((width, out_width), column),
            ],
            out_specs=[
                pl.BlockSpec((1, rows, out_width), lambda j, core: (jnp.minimum(j, count - 1), 0, 0)),
                pl.BlockSpec((1, rows, out_width), lambda j, core: (jnp.maximum(j - count, 0), 0, 0)),
            ],
        ),
        out_shape=[shape, shape],
        compiler_params=pltpu.CompilerParams(vmem_limit_bytes=8 * MIB),
        cost_estimate=BRIEF,
    )(core, attended, weight)


def pair_kernel(chip_ref, keep_ref, come_ref, own_ref, *outs, cuts):
    chips = keep_ref.shape[0]
    for shift in range(chips):
        index = (chip_ref[0] + shift) % chips
        pair = keep_ref[index].astype(jnp.float32) + come_ref[index].astype(jnp.float32)
        pair = pair.astype(jnp.bfloat16)
        if shift == 0:
            own_ref[...] = pair
        else:
            for k in range(cuts):
                out = outs[(shift - 1) * cuts + k]
                rows = out.shape[0]
                out[...] = pair[k * rows : (k + 1) * rows]


def pair_sums(chip, keep, come, cuts):
    chips, rows, width = keep.shape
    away = [jax.ShapeDtypeStruct((rows // cuts, width), jnp.bfloat16)] * ((chips - 1) * cuts)
    return pl.pallas_call(
        functools.partial(pair_kernel, cuts=cuts),
        out_shape=[jax.ShapeDtypeStruct((rows, width), jnp.bfloat16)] + away,
        in_specs=[SMEM, VMEM, VMEM],
        out_specs=[VMEM] * (1 + len(away)),
        compiler_params=pltpu.CompilerParams(vmem_limit_bytes=12 * MIB),
        cost_estimate=BRIEF,
    )(chip, keep, come)


def slot_of(row, turn, here, resident, holders):
    block = holders // FOLD
    holder = row // resident
    fold = (here // block - holder // block + FOLD) % FOLD
    place = (holder % block - here % block + block) % block
    return ((place * FOLD + fold) * resident + row % resident) * MOST + turn


def row_slots(row_ref, here, resident, holders):
    row = row_ref[...]
    shape = (row.shape[1], row.shape[1])
    across = jnp.broadcast_to(row, shape)
    down, lane = lax.broadcasted_iota(jnp.int32, shape, 0), lax.broadcasted_iota(jnp.int32, shape, 1)
    values = across.astype(jnp.float32)
    col = jnp.sum(jnp.where(down == lane, values, 0.0), axis=1, keepdims=True)
    same = jnp.broadcast_to(col, shape) == values
    turn_row = jnp.sum(jnp.where(same & (down < lane), 1.0, 0.0), axis=0, keepdims=True)
    turn_col = jnp.sum(jnp.where(same & (lane < down), 1.0, 0.0), axis=1, keepdims=True)
    place_row = slot_of(row, turn_row.astype(jnp.int32), here, resident, holders)
    place_col = slot_of(
        jnp.broadcast_to(col, shape).astype(jnp.int32),
        jnp.broadcast_to(turn_col, shape).astype(jnp.int32),
        here,
        resident,
        holders,
    )
    return place_row, place_col[:, :1]


def pack_kernel(here_ref, row_ref, *refs, steps, resident, holders, count):
    parts, outs = refs[:-count], refs[-count:]
    slots, rolls = outs[0].shape[0], row_ref.shape[1]
    place, _ = row_slots(row_ref, here_ref[0], resident, holders)
    for d, out in enumerate(outs):
        shape = (slots, rolls)
        slot = (d * slots + lax.broadcasted_iota(jnp.int32, shape, 0)) // steps
        picked = jnp.where(slot == jnp.broadcast_to(place, shape), 1.0, 0.0).astype(jnp.bfloat16)
        total, start = None, 0
        for part in parts:
            rows = part.shape[0]
            shape = (rolls, rows)
            spread = lax.broadcasted_iota(jnp.int32, shape, 0) == (
                start + lax.broadcasted_iota(jnp.int32, shape, 1)
            ) // steps
            chosen = dot_nn(picked, jnp.where(spread, 1.0, 0.0).astype(jnp.bfloat16))
            shape = (slots, rows)
            step = lax.broadcasted_iota(jnp.int32, shape, 0) % steps
            aligned = step == (start + lax.broadcasted_iota(jnp.int32, shape, 1)) % steps
            chosen = jnp.where(aligned, chosen, 0.0).astype(jnp.bfloat16)
            term = dot_nn(chosen, part[...])
            total = term if total is None else total + term
            start += rows
        out[...] = total.astype(jnp.bfloat16)


def pack(here, adapter_row, parts, count, slots, steps, resident, holders):
    width = parts[0].shape[1]
    return pl.pallas_call(
        functools.partial(
            pack_kernel, steps=steps, resident=resident, holders=holders, count=count
        ),
        out_shape=[jax.ShapeDtypeStruct((slots, width), jnp.bfloat16)] * count,
        in_specs=[SMEM] + [VMEM] * (1 + len(parts)),
        out_specs=[VMEM] * count,
        compiler_params=pltpu.CompilerParams(vmem_limit_bytes=12 * MIB),
        cost_estimate=BRIEF,
    )(here, adapter_row, *parts)


def adapter_mask(rows, per_adapter, rank, tile):
    lane = lax.broadcasted_iota(jnp.int32, (rows, HEAD_SIZE), 1) + tile * HEAD_SIZE
    row = lax.broadcasted_iota(jnp.int32, (rows, HEAD_SIZE), 0)
    return lane // rank == row // per_adapter


def shrink_kernel(*refs, per_adapter, rank, count):
    weights, pieces, out = refs[:FOLD], refs[FOLD : FOLD + count], refs[-1]
    rows = pieces[0].shape[0] // FOLD
    found = []
    for k in range(FOLD):
        span = pl.ds(k * rows, rows)
        every = dot_nt(
            jnp.concatenate([p[span, :] for p in pieces], axis=0),
            weights[k][...],
        )
        for d in range(count):
            total = None
            for tile in range(every.shape[1] // HEAD_SIZE):
                x = every[d * rows : (d + 1) * rows, tile * HEAD_SIZE : (tile + 1) * HEAD_SIZE]
                x = jnp.where(adapter_mask(rows, per_adapter, rank, tile), x, 0.0)
                total = x if total is None else total + x
            summed = total
            for turn in range(1, HEAD_SIZE // rank):
                summed = summed + pltpu.roll(total, turn * rank, axis=1)
            found.append(summed)
    lane = lax.broadcasted_iota(jnp.int32, (rows, HEAD_SIZE), 1)
    for d in range(count):
        both = jnp.where(lane < rank, found[d], found[count + d])
        out[pl.ds(d * rows, rows), :] = both


def shrink_rows(weights, pieces, per_adapter, rank):
    count = len(pieces)
    rows, width = pieces[0].shape
    return pl.pallas_call(
        functools.partial(shrink_kernel, per_adapter=per_adapter, rank=rank, count=count),
        out_shape=jax.ShapeDtypeStruct((count * rows // FOLD, HEAD_SIZE), jnp.float32),
        in_specs=[VMEM] * (FOLD + count),
        out_specs=VMEM,
        compiler_params=pltpu.CompilerParams(vmem_limit_bytes=8 * MIB),
        cost_estimate=LENGTHY,
    )(*weights, *pieces)


def expand_kernel(*refs, per_adapter, rank, count, terms):
    weights, sums, outs = refs[:FOLD], refs[FOLD : FOLD + terms], refs[FOLD + terms :]
    depth = weights[0].shape[0]
    rows = outs[0].shape[0] // FOLD
    for k in range(FOLD):
        spread = []
        for d in range(count):
            span = pl.ds(d * rows, rows)
            code = sums[0][span, :].astype(jnp.float32)
            for other in sums[1:]:
                code = code + other[span, :].astype(jnp.float32)
            lane = lax.broadcasted_iota(jnp.int32, (rows, HEAD_SIZE), 1)
            turned = pltpu.roll(code, rank, axis=1)
            code = jnp.where((lane < rank) == (k == 0), code, turned)
            spread.append(
                jnp.concatenate(
                    [
                        jnp.where(adapter_mask(rows, per_adapter, rank, tile), code, 0.0)
                        for tile in range(depth // HEAD_SIZE)
                    ],
                    axis=1,
                ).astype(jnp.bfloat16)
            )
        wide = dot_nn(jnp.concatenate(spread, axis=0), weights[k][...])
        wide = wide.astype(jnp.bfloat16)
        for d in range(count):
            outs[d][pl.ds(k * rows, rows), :] = wide[d * rows : (d + 1) * rows]


def expand_rows(weights, sums, per_adapter, rank, count):
    rows = sums[0].shape[0] // count * FOLD
    width = weights[0].shape[1]
    return pl.pallas_call(
        functools.partial(
            expand_kernel, per_adapter=per_adapter, rank=rank, count=count, terms=len(sums)
        ),
        out_shape=[jax.ShapeDtypeStruct((rows, width), jnp.bfloat16)] * count,
        in_specs=[VMEM] * (FOLD + len(sums)),
        out_specs=[VMEM] * count,
        compiler_params=pltpu.CompilerParams(vmem_limit_bytes=8 * MIB),
        cost_estimate=LENGTHY,
    )(*weights, *sums)


def choose_kernel(here_ref, row_ref, chosen_ref, *, steps, resident, holders):
    rows, total = chosen_ref.shape
    rolls = row_ref.shape[1]
    _, place = row_slots(row_ref, here_ref[0], resident, holders)
    shape = (rolls, total)
    slot = lax.broadcasted_iota(jnp.int32, shape, 1) // steps
    picked = jnp.where(slot == jnp.broadcast_to(place, shape), 1.0, 0.0).astype(jnp.bfloat16)
    shape = (rows, rolls)
    roll = lax.broadcasted_iota(jnp.int32, shape, 0) // steps
    spread = roll == lax.broadcasted_iota(jnp.int32, shape, 1)
    chosen = dot_nn(jnp.where(spread, 1.0, 0.0).astype(jnp.bfloat16), picked)
    shape = (rows, total)
    step = lax.broadcasted_iota(jnp.int32, shape, 0) % steps
    aligned = step == lax.broadcasted_iota(jnp.int32, shape, 1) % steps
    chosen_ref[...] = jnp.where(aligned, chosen, 0.0).astype(jnp.bfloat16)


def choose(here, adapter_row, total, steps, resident, holders):
    rows = adapter_row.shape[1] * steps
    return pl.pallas_call(
        functools.partial(choose_kernel, steps=steps, resident=resident, holders=holders),
        out_shape=jax.ShapeDtypeStruct((rows, total), jnp.bfloat16),
        in_specs=[SMEM, VMEM],
        out_specs=VMEM,
        compiler_params=pltpu.CompilerParams(vmem_limit_bytes=20 * MIB),
        cost_estimate=BRIEF,
    )(here, adapter_row)


def combine_kernel(chosen_ref, *refs, count, starts):
    pieces, sums, out, total_ref = refs[:count], refs[count:-2], refs[-2], refs[-1]
    stacked = jnp.concatenate([x[...] for x in pieces], axis=0)
    total_ref[...] = dot_nn(chosen_ref[...], stacked)
    for start, x in zip(starts, sums):
        span = pl.ds(start, x.shape[0])
        total_ref[span, :] += x[...].astype(jnp.float32)
    out[...] = total_ref[...].reshape(out.shape).astype(jnp.bfloat16)


def combine(chosen, pieces, sums, steps):
    width = pieces[0].shape[1]
    count = len(pieces)
    starts, flat = zip(*sums)
    rows = chosen.shape[0]
    block = min(width, 2 * HEAD_SIZE)

    def columns(x):
        return pl.BlockSpec((x, block), lambda j: (0, j))

    return pl.pallas_call(
        functools.partial(combine_kernel, count=count, starts=starts),
        grid=(width // block,),
        out_shape=jax.ShapeDtypeStruct((rows // steps, steps, width), jnp.bfloat16),
        in_specs=[pl.BlockSpec(chosen.shape, lambda j: (0, 0))]
        + [columns(x.shape[0]) for x in (*pieces, *flat)],
        out_specs=pl.BlockSpec((rows // steps, steps, block), lambda j: (0, 0, j)),
        scratch_shapes=[pltpu.VMEM((rows, block), jnp.float32)],
        compiler_params=pltpu.CompilerParams(vmem_limit_bytes=20 * MIB),
        cost_estimate=BRIEF,
    )(chosen, *pieces, *flat)


def local(
    queries,
    shared_prefix_cache,
    rollout_suffix_cache,
    fresh_key_value,
    rollout_prefix_index,
    rollout_suffix_length,
    rollout_adapter_index,
    output_projection_weight,
    adapter_shrink_weight,
    adapter_expand_weight,
):
    rolls, steps, width = queries.shape
    rows = rolls * steps
    prefix_count = shared_prefix_cache.shape[1]
    resident, rank, out_width = adapter_expand_weight.shape
    holders, sides = lax.axis_size("adapter"), lax.axis_size("tensor")
    block, chips = holders // FOLD, sides // 2
    here, side = lax.axis_index("adapter"), lax.axis_index("tensor")
    chip, core = side // 2, side % 2

    def in_block(shift):
        return [(i, i // block * block + (i + shift) % block) for i in range(holders)]

    cores = [(t, t // 2 * 2 + (t + 1) % 2) for t in range(sides)]

    def over_chips(shift):
        return [(t, (t // 2 + shift) % chips * 2 + t % 2) for t in range(sides)]

    own_shrink = adapter_shrink_weight.reshape(resident * rank, width)
    own_expand = adapter_expand_weight.reshape(resident * rank, out_width)
    far = [(i, (i + block) % holders) for i in range(holders)]

    slots = FOLD * resident * MOST * steps
    per_adapter = MOST * steps
    adapter_row = rollout_adapter_index.reshape(1, rolls)
    lengths, prefixes = rollout_suffix_length[None, :], rollout_prefix_index[None, :]
    here = here.reshape(1).astype(jnp.int32)
    core = core.reshape(1).astype(jnp.int32)
    chip_index = chip.reshape(1).astype(jnp.int32)
    tie = lax.optimization_barrier

    def send_over_chips(away, cuts):
        return [
            lax.ppermute(x, "tensor", over_chips(1 + k // cuts)) for k, x in enumerate(away)
        ]

    def placed(start, own, came, cuts):
        rows = own.shape[0] // cuts
        return [(start, own)] + [(start + k % cuts * rows, x) for k, x in enumerate(came)]

    shrink = lax.ppermute(own_shrink, "adapter", far)
    attended = attend(
        lengths, prefixes, queries, shared_prefix_cache, rollout_suffix_cache, fresh_key_value,
        steps, 0, rolls // BLOCK_ROLLS,
    )
    packed = list(pack(here, adapter_row, [attended], block, slots, steps, resident, holders))
    attended, packed[0] = tie((attended, packed[0]))
    pieces = [packed[0]] + [
        lax.ppermute(packed[d], "adapter", in_block(d)) for d in range(1, block)
    ]
    send, keep = project(core, attended, output_projection_weight, out_width)
    chosen = choose(here, adapter_row, block * slots, steps, resident, holders)
    send, chosen = tie((send, chosen))
    own, *away = pair_sums(chip_index, keep, lax.ppermute(send, "tensor", cores), 1)
    pieces[0], shrink, moved = tie((pieces[0], shrink, own_expand))
    expand = lax.ppermute(moved, "adapter", far)
    codes = shrink_rows([own_shrink, shrink], pieces, per_adapter, rank)
    codes = codes + lax.ppermute(codes, "tensor", cores)
    brief = codes.astype(jnp.bfloat16)
    codes = [brief] + [lax.ppermute(brief, "tensor", over_chips(s)) for s in range(1, chips)]
    codes, away = tie((codes, away))
    came = send_over_chips(away, 1)
    wide = expand_rows([own_expand, expand], codes, per_adapter, rank, block)
    back = [wide[0]] + [
        lax.ppermute(wide[d], "adapter", in_block(block - d)) for d in range(1, block)
    ]
    return combine(chosen, back, placed(0, own, came, 1), steps)


def solution(mesh):
    placed = (
        P("adapter", None, "tensor"),
        P(None, "adapter", None, "tensor"),
        P(None, "adapter", None, "tensor"),
        P(None, "adapter", None, "tensor"),
        P("adapter"),
        P("adapter"),
        P("adapter", None),
        P("tensor", None),
        P("adapter", None, "tensor"),
        P("adapter", None, "tensor"),
    )
    return jax.shard_map(
        local, mesh=mesh, in_specs=placed, out_specs=P("adapter", None, "tensor"), check_vma=False
    )
```

```python
import functools
import math

import jax
import jax.numpy as jnp
from jax import lax
from jax.experimental import pallas as pl
from jax.experimental.pallas import tpu as pltpu
from jax.sharding import PartitionSpec as P

HEAD_SIZE = 128
MOST = 5
FOLD = 2
BLOCK_ROLLS = 32
KEY_CHUNK = 512
NEG = float("-inf")
MIB = 1 << 20
BRIEF = pl.CostEstimate(flops=1024, bytes_accessed=1024, transcendentals=0)
LENGTHY = pl.CostEstimate(flops=1 << 36, bytes_accessed=1 << 27, transcendentals=0)
VMEM = pl.BlockSpec(memory_space=pltpu.VMEM)
HBM = pl.BlockSpec(memory_space=pltpu.HBM)
SMEM = pl.BlockSpec(memory_space=pltpu.SMEM)


def dot_nt(a, b):
    return lax.dot_general(a, b, (((1,), (1,)), ((), ())), preferred_element_type=jnp.float32)


def dot_nn(a, b):
    return jnp.dot(a, b, preferred_element_type=jnp.float32)


def attend_kernel(
    length_hbm, prefix_hbm, q_hbm, kv_hbm, suf_hbm, fr_hbm, o_ref,
    s_ref, m_ref, length_ref, prefix_ref, q_ref, kv_ref, suf_ref, fr_ref, sems,
    *, steps, group, first, blocks
):
    prefix_count, prefix_len = kv_ref.shape[1], kv_ref.shape[2]
    key_heads = kv_ref.shape[3] // HEAD_SIZE
    rolls, suf_len = suf_hbm.shape[1], suf_hbm.shape[2]
    block_rows = BLOCK_ROLLS * steps
    rows = block_rows * group
    last = first + blocks - 1
    suf_rolls = HEAD_SIZE // suf_len
    suf_rows = suf_rolls * steps
    suf_groups = BLOCK_ROLLS // suf_rolls
    window_rolls = HEAD_SIZE // steps
    windows = window_rolls // BLOCK_ROLLS
    factor = HEAD_SIZE ** (-0.5) * math.log2(math.e)
    chunks = prefix_len // KEY_CHUNK
    span = prefix_len

    def row_codes(block):
        shape = (block_rows, rolls)
        mine = block * BLOCK_ROLLS + lax.broadcasted_iota(jnp.int32, shape, 0) // steps
        lane = lax.broadcasted_iota(jnp.int32, shape, 1)
        code = length_ref[...] * prefix_count + prefix_ref[...] % prefix_count
        code = jnp.broadcast_to(code.astype(jnp.float32), shape)
        col = jnp.sum(jnp.where(mine == lane, code, 0.0), axis=1, keepdims=True)
        col = jnp.broadcast_to(col, (block_rows, HEAD_SIZE)).astype(jnp.int32)
        return col // prefix_count, col % prefix_count

    mine = pl.ds(first * BLOCK_ROLLS, blocks * BLOCK_ROLLS)
    loads = []
    for which in range(2):
        loads.append(pltpu.make_async_copy(kv_hbm.at[which], kv_ref.at[which], sems.at[2 * which]))
        loads.append(
            pltpu.make_async_copy(suf_hbm.at[which, mine], suf_ref.at[which], sems.at[2 * which + 1])
        )
    small = [
        pltpu.make_async_copy(src, dst, sems.at[4 + k])
        for k, (src, dst) in enumerate(
            [(q_hbm, q_ref), (fr_hbm, fr_ref), (length_hbm, length_ref), (prefix_hbm, prefix_ref)]
        )
    ]
    for load in [*reversed(small), *loads]:
        load.start()

    def tile_rows(x):
        return jnp.concatenate([x] * group, axis=0)

    def load_q(block, h):
        span = pl.ds(block * BLOCK_ROLLS, BLOCK_ROLLS)
        return [
            q_ref[span, :, pl.ds((h * group + g) * HEAD_SIZE, HEAD_SIZE)].reshape(
                block_rows, HEAD_SIZE
            )
            for g in range(group)
        ]

    def head_lanes(h):
        return pl.ds(h * HEAD_SIZE, HEAD_SIZE)

    def suffix_tile(which, block, i, h):
        start = (block - first) * BLOCK_ROLLS + i * suf_rolls
        tile = suf_ref[which, pl.ds(start, suf_rolls), :, head_lanes(h)]
        return tile.reshape(HEAD_SIZE, HEAD_SIZE)

    def fresh_tile(which, block, h):
        span = pl.ds(block // windows * window_rolls, window_rolls)
        return fr_ref[which, span, :, head_lanes(h)].reshape(HEAD_SIZE, HEAD_SIZE)

    def prefix_tile(which, c, h):
        return jnp.concatenate(
            [
                kv_ref[which, p, pl.ds(c * KEY_CHUNK, KEY_CHUNK), head_lanes(h)]
                for p in range(prefix_count)
            ],
            axis=1,
        )

    def scores(block, h, slot):
        length, local = row_codes(block)
        parts = load_q(block, h)
        stacked = jnp.concatenate(parts, axis=0)
        wide = jnp.concatenate(
            [
                jnp.concatenate(
                    [jnp.where(local == p, x, jnp.zeros_like(x)) for x in parts], axis=0
                )
                for p in range(prefix_count)
            ],
            axis=1,
        )
        shape = (block_rows, HEAD_SIZE)
        row = lax.broadcasted_iota(jnp.int32, shape, 0)
        lane = lax.broadcasted_iota(jnp.int32, shape, 1)
        roll = row // steps
        keep = (roll % suf_rolls == lane // suf_len) & (lane % suf_len < length)
        suf_bias = jnp.where(keep, 0.0, NEG)
        in_window = (block % windows) * BLOCK_ROLLS + roll
        keep = (in_window == lane // steps) & (lane % steps <= row % steps)
        fr_bias = jnp.where(keep, 0.0, NEG)
        suf = []
        for i in range(suf_groups):
            piece = jnp.concatenate(
                [x[i * suf_rows : (i + 1) * suf_rows] for x in parts], axis=0
            )
            suf.append(dot_nt(piece, suffix_tile(0, block, i, h)))
        suf = jnp.concatenate(
            [
                jnp.concatenate([x[g * suf_rows : (g + 1) * suf_rows] for x in suf], axis=0)
                for g in range(group)
            ],
            axis=0,
        ) + tile_rows(suf_bias)
        fr = dot_nt(stacked, fresh_tile(0, block, h)) + tile_rows(fr_bias)
        s_ref[slot, :, pl.ds(span, HEAD_SIZE)] = suf
        s_ref[slot, :, pl.ds(span + HEAD_SIZE, HEAD_SIZE)] = fr
        top = jnp.maximum(suf, fr)
        yield
        for c in range(chunks):
            s = dot_nt(wide, prefix_tile(0, c, h))
            s_ref[slot, :, pl.ds(c * KEY_CHUNK, KEY_CHUNK)] = s
            for j in range(KEY_CHUNK // HEAD_SIZE):
                top = jnp.maximum(top, s[:, j * HEAD_SIZE : (j + 1) * HEAD_SIZE])
            if c == chunks - 1:
                top = jnp.max(top, axis=1, keepdims=True) * factor
                m_ref[slot] = jnp.broadcast_to(top, (rows, HEAD_SIZE))
            yield

    def outputs(block, h, slot):
        top = m_ref[slot]

        def weigh(start, width):
            x = s_ref[slot, :, pl.ds(start, width)]
            wide_top = jnp.concatenate([top] * (width // HEAD_SIZE), axis=1)
            return jnp.exp2(x * factor - wide_top)

        both = weigh(span, 2 * HEAD_SIZE)
        total = both[:, :HEAD_SIZE] + both[:, HEAD_SIZE:]
        both = both.astype(jnp.bfloat16)
        fr = dot_nn(both[:, HEAD_SIZE:], fresh_tile(1, block, h))
        suf = []
        for i in range(suf_groups):
            piece = jnp.concatenate(
                [
                    both[
                        g * block_rows + i * suf_rows : g * block_rows + (i + 1) * suf_rows,
                        :HEAD_SIZE,
                    ]
                    for g in range(group)
                ],
                axis=0,
            )
            suf.append(dot_nn(piece, suffix_tile(1, block, i, h)))
        extra = fr + jnp.concatenate(
            [
                jnp.concatenate([x[g * suf_rows : (g + 1) * suf_rows] for x in suf], axis=0)
                for g in range(group)
            ],
            axis=0,
        )
        yield
        acc = None
        for c in range(chunks):
            p = weigh(c * KEY_CHUNK, KEY_CHUNK)
            for j in range(KEY_CHUNK // HEAD_SIZE):
                total = total + p[:, j * HEAD_SIZE : (j + 1) * HEAD_SIZE]
            part = dot_nn(p.astype(jnp.bfloat16), prefix_tile(1, c, h))
            acc = part if acc is None else acc + part
            if c == chunks - 1:
                _, local = row_codes(block)
                local = tile_rows(local)
                chosen = acc[:, :HEAD_SIZE]
                for q in range(1, prefix_count):
                    chosen = jnp.where(
                        local == q, acc[:, q * HEAD_SIZE : (q + 1) * HEAD_SIZE], chosen
                    )
                weight = 1.0 / jnp.sum(total, axis=1, keepdims=True)
                out = ((chosen + extra) * weight).astype(o_ref.dtype)
                start = pl.multiple_of((block - first) * block_rows, block_rows)
                for g in range(group):
                    o_ref[
                        pl.ds(start, block_rows),
                        pl.ds((h * group + g) * HEAD_SIZE, HEAD_SIZE),
                    ] = out[g * block_rows : (g + 1) * block_rows]
            yield

    def run(*streams):
        for _ in range(chunks + 1):
            for stream in streams:
                next(stream)

    for load in [*reversed(small), *loads[:2]]:
        load.wait()
    run(scores(first, 0, 0))
    for load in loads[2:]:
        load.wait()

    def body(block, carry):
        for h in range(key_heads):
            if h + 1 < key_heads:
                run(scores(block, h + 1, h + 1), outputs(block, h, h))
            elif key_heads > 1:
                following = jnp.minimum(block + 1, last)
                run(scores(following, 0, 0), outputs(block, h, h))
            else:
                run(outputs(block, h, h))
                run(scores(jnp.minimum(block + 1, last), 0, 0))
        return carry

    lax.fori_loop(first, first + blocks, body, 0)


def attend(lengths, prefixes, queries, prefix, suffix, fresh, steps, first, blocks):
    width = queries.shape[-1]
    rows = blocks * BLOCK_ROLLS * steps
    key_heads = prefix.shape[3] // HEAD_SIZE
    group = width // HEAD_SIZE // key_heads
    unit_rows = BLOCK_ROLLS * steps * group
    span = prefix.shape[2] + 2 * HEAD_SIZE
    held = (2, blocks * BLOCK_ROLLS) + suffix.shape[2:]
    return pl.pallas_call(
        functools.partial(attend_kernel, steps=steps, group=group, first=first, blocks=blocks),
        out_shape=jax.ShapeDtypeStruct((rows, width), jnp.bfloat16),
        in_specs=[HBM] * 6,
        out_specs=VMEM,
        scratch_shapes=[
            pltpu.VMEM((key_heads, unit_rows, span), jnp.float32),
            pltpu.VMEM((key_heads, unit_rows, HEAD_SIZE), jnp.float32),
            pltpu.VMEM(lengths.shape, lengths.dtype),
            pltpu.VMEM(prefixes.shape, prefixes.dtype),
            pltpu.VMEM(queries.shape, queries.dtype),
            pltpu.VMEM(prefix.shape, prefix.dtype),
            pltpu.VMEM(held, suffix.dtype),
            pltpu.VMEM(fresh.shape, fresh.dtype),
            pltpu.SemaphoreType.DMA((8,)),
        ],
        compiler_params=pltpu.CompilerParams(vmem_limit_bytes=52 * MIB),
        cost_estimate=LENGTHY,
    )(lengths, prefixes, queries, prefix, suffix, fresh)


def project_kernel(core_ref, a_ref, w_ref, send_ref, keep_ref, *, count):
    step = pl.program_id(0)
    part = dot_nn(a_ref[...], w_ref[...]).astype(jnp.bfloat16)

    @pl.when(step < count)
    def _():
        send_ref[0] = part

    @pl.when(step >= count)
    def _():
        keep_ref[0] = part


def project(core, attended, weight, out_width):
    rows, width = attended.shape
    count = weight.shape[1] // out_width // 2

    def column(j, core):
        parity = jnp.where(j < count, 1 - core[0], core[0])
        return (0, (j % count) * 2 + parity)

    shape = jax.ShapeDtypeStruct((count, rows, out_width), jnp.bfloat16)
    return pl.pallas_call(
        functools.partial(project_kernel, count=count),
        grid_spec=pltpu.PrefetchScalarGridSpec(
            num_scalar_prefetch=1,
            grid=(2 * count,),
            in_specs=[
                pl.BlockSpec((rows, width), lambda j, core: (0, 0)),
                pl.BlockSpec((width, out_width), column),
            ],
            out_specs=[
                pl.BlockSpec((1, rows, out_width), lambda j, core: (jnp.minimum(j, count - 1), 0, 0)),
                pl.BlockSpec((1, rows, out_width), lambda j, core: (jnp.maximum(j - count, 0), 0, 0)),
            ],
        ),
        out_shape=[shape, shape],
        compiler_params=pltpu.CompilerParams(vmem_limit_bytes=8 * MIB),
        cost_estimate=BRIEF,
    )(core, attended, weight)


def pair_kernel(chip_ref, keep_ref, come_ref, own_ref, *outs, cuts):
    chips = keep_ref.shape[0]
    for shift in range(chips):
        index = (chip_ref[0] + shift) % chips
        pair = keep_ref[index].astype(jnp.float32) + come_ref[index].astype(jnp.float32)
        pair = pair.astype(jnp.bfloat16)
        if shift == 0:
            own_ref[...] = pair
        else:
            for k in range(cuts):
                out = outs[(shift - 1) * cuts + k]
                rows = out.shape[0]
                out[...] = pair[k * rows : (k + 1) * rows]


def pair_sums(chip, keep, come, cuts):
    chips, rows, width = keep.shape
    away = [jax.ShapeDtypeStruct((rows // cuts, width), jnp.bfloat16)] * ((chips - 1) * cuts)
    return pl.pallas_call(
        functools.partial(pair_kernel, cuts=cuts),
        out_shape=[jax.ShapeDtypeStruct((rows, width), jnp.bfloat16)] + away,
        in_specs=[SMEM, VMEM, VMEM],
        out_specs=[VMEM] * (1 + len(away)),
        compiler_params=pltpu.CompilerParams(vmem_limit_bytes=12 * MIB),
        cost_estimate=BRIEF,
    )(chip, keep, come)


def slot_of(row, turn, here, resident, holders):
    block = holders // FOLD
    holder = row // resident
    fold = (here // block - holder // block + FOLD) % FOLD
    place = (holder % block - here % block + block) % block
    return ((place * FOLD + fold) * resident + row % resident) * MOST + turn


def row_slots(row_ref, here, resident, holders):
    row = row_ref[...]
    shape = (row.shape[1], row.shape[1])
    across = jnp.broadcast_to(row, shape)
    down, lane = lax.broadcasted_iota(jnp.int32, shape, 0), lax.broadcasted_iota(jnp.int32, shape, 1)
    values = across.astype(jnp.float32)
    col = jnp.sum(jnp.where(down == lane, values, 0.0), axis=1, keepdims=True)
    same = jnp.broadcast_to(col, shape) == values
    turn_row = jnp.sum(jnp.where(same & (down < lane), 1.0, 0.0), axis=0, keepdims=True)
    turn_col = jnp.sum(jnp.where(same & (lane < down), 1.0, 0.0), axis=1, keepdims=True)
    place_row = slot_of(row, turn_row.astype(jnp.int32), here, resident, holders)
    place_col = slot_of(
        jnp.broadcast_to(col, shape).astype(jnp.int32),
        jnp.broadcast_to(turn_col, shape).astype(jnp.int32),
        here,
        resident,
        holders,
    )
    return place_row, place_col[:, :1]


def pack_kernel(here_ref, row_ref, *refs, steps, resident, holders, count):
    parts, outs = refs[:-count], refs[-count:]
    slots, rolls = outs[0].shape[0], row_ref.shape[1]
    place, _ = row_slots(row_ref, here_ref[0], resident, holders)
    for d, out in enumerate(outs):
        shape = (slots, rolls)
        slot = (d * slots + lax.broadcasted_iota(jnp.int32, shape, 0)) // steps
        picked = jnp.where(slot == jnp.broadcast_to(place, shape), 1.0, 0.0).astype(jnp.bfloat16)
        total, start = None, 0
        for part in parts:
            rows = part.shape[0]
            shape = (rolls, rows)
            spread = lax.broadcasted_iota(jnp.int32, shape, 0) == (
                start + lax.broadcasted_iota(jnp.int32, shape, 1)
            ) // steps
            chosen = dot_nn(picked, jnp.where(spread, 1.0, 0.0).astype(jnp.bfloat16))
            shape = (slots, rows)
            step = lax.broadcasted_iota(jnp.int32, shape, 0) % steps
            aligned = step == (start + lax.broadcasted_iota(jnp.int32, shape, 1)) % steps
            chosen = jnp.where(aligned, chosen, 0.0).astype(jnp.bfloat16)
            term = dot_nn(chosen, part[...])
            total = term if total is None else total + term
            start += rows
        out[...] = total.astype(jnp.bfloat16)


def pack(here, adapter_row, parts, count, slots, steps, resident, holders):
    width = parts[0].shape[1]
    return pl.pallas_call(
        functools.partial(
            pack_kernel, steps=steps, resident=resident, holders=holders, count=count
        ),
        out_shape=[jax.ShapeDtypeStruct((slots, width), jnp.bfloat16)] * count,
        in_specs=[SMEM] + [VMEM] * (1 + len(parts)),
        out_specs=[VMEM] * count,
        compiler_params=pltpu.CompilerParams(vmem_limit_bytes=12 * MIB),
        cost_estimate=BRIEF,
    )(here, adapter_row, *parts)


def adapter_mask(rows, per_adapter, rank, tile):
    lane = lax.broadcasted_iota(jnp.int32, (rows, HEAD_SIZE), 1) + tile * HEAD_SIZE
    row = lax.broadcasted_iota(jnp.int32, (rows, HEAD_SIZE), 0)
    return lane // rank == row // per_adapter


def shrink_kernel(*refs, per_adapter, rank, count):
    weights, pieces, out = refs[:FOLD], refs[FOLD : FOLD + count], refs[-1]
    rows = pieces[0].shape[0] // FOLD
    found = []
    for k in range(FOLD):
        span = pl.ds(k * rows, rows)
        every = dot_nt(
            jnp.concatenate([p[span, :] for p in pieces], axis=0),
            weights[k][...],
        )
        for d in range(count):
            total = None
            for tile in range(every.shape[1] // HEAD_SIZE):
                x = every[d * rows : (d + 1) * rows, tile * HEAD_SIZE : (tile + 1) * HEAD_SIZE]
                x = jnp.where(adapter_mask(rows, per_adapter, rank, tile), x, 0.0)
                total = x if total is None else total + x
            summed = total
            for turn in range(1, HEAD_SIZE // rank):
                summed = summed + pltpu.roll(total, turn * rank, axis=1)
            found.append(summed)
    lane = lax.broadcasted_iota(jnp.int32, (rows, HEAD_SIZE), 1)
    for d in range(count):
        both = jnp.where(lane < rank, found[d], found[count + d])
        out[pl.ds(d * rows, rows), :] = both


def shrink_rows(weights, pieces, per_adapter, rank):
    count = len(pieces)
    rows, width = pieces[0].shape
    return pl.pallas_call(
        functools.partial(shrink_kernel, per_adapter=per_adapter, rank=rank, count=count),
        out_shape=jax.ShapeDtypeStruct((count * rows // FOLD, HEAD_SIZE), jnp.float32),
        in_specs=[VMEM] * (FOLD + count),
        out_specs=VMEM,
        compiler_params=pltpu.CompilerParams(vmem_limit_bytes=8 * MIB),
        cost_estimate=LENGTHY,
    )(*weights, *pieces)


def expand_kernel(*refs, per_adapter, rank, count, terms):
    held = len(refs) - terms - count
    sums, outs = refs[held : held + terms], refs[held + terms :]
    weights = [refs[0][...], jnp.concatenate([x[...] for x in refs[1:held]], axis=0)]
    depth = weights[0].shape[0]
    rows = outs[0].shape[0] // FOLD
    for k in range(FOLD):
        spread = []
        for d in range(count):
            span = pl.ds(d * rows, rows)
            code = sums[0][span, :].astype(jnp.float32)
            for other in sums[1:]:
                code = code + other[span, :].astype(jnp.float32)
            lane = lax.broadcasted_iota(jnp.int32, (rows, HEAD_SIZE), 1)
            turned = pltpu.roll(code, rank, axis=1)
            code = jnp.where((lane < rank) == (k == 0), code, turned)
            spread.append(
                jnp.concatenate(
                    [
                        jnp.where(adapter_mask(rows, per_adapter, rank, tile), code, 0.0)
                        for tile in range(depth // HEAD_SIZE)
                    ],
                    axis=1,
                ).astype(jnp.bfloat16)
            )
        wide = dot_nn(jnp.concatenate(spread, axis=0), weights[k])
        wide = wide.astype(jnp.bfloat16)
        for d in range(count):
            outs[d][pl.ds(k * rows, rows), :] = wide[d * rows : (d + 1) * rows]


def expand_rows(weights, sums, per_adapter, rank, count):
    rows = sums[0].shape[0] // count * FOLD
    width = weights[0].shape[1]
    return pl.pallas_call(
        functools.partial(
            expand_kernel, per_adapter=per_adapter, rank=rank, count=count, terms=len(sums)
        ),
        out_shape=[jax.ShapeDtypeStruct((rows, width), jnp.bfloat16)] * count,
        in_specs=[VMEM] * (len(weights) + len(sums)),
        out_specs=[VMEM] * count,
        compiler_params=pltpu.CompilerParams(vmem_limit_bytes=8 * MIB),
        cost_estimate=LENGTHY,
    )(*weights, *sums)


def choose_kernel(here_ref, row_ref, chosen_ref, *, steps, resident, holders):
    rows, total = chosen_ref.shape
    rolls = row_ref.shape[1]
    _, place = row_slots(row_ref, here_ref[0], resident, holders)
    shape = (rolls, total)
    slot = lax.broadcasted_iota(jnp.int32, shape, 1) // steps
    picked = jnp.where(slot == jnp.broadcast_to(place, shape), 1.0, 0.0).astype(jnp.bfloat16)
    shape = (rows, rolls)
    roll = lax.broadcasted_iota(jnp.int32, shape, 0) // steps
    spread = roll == lax.broadcasted_iota(jnp.int32, shape, 1)
    chosen = dot_nn(jnp.where(spread, 1.0, 0.0).astype(jnp.bfloat16), picked)
    shape = (rows, total)
    step = lax.broadcasted_iota(jnp.int32, shape, 0) % steps
    aligned = step == lax.broadcasted_iota(jnp.int32, shape, 1) % steps
    chosen_ref[...] = jnp.where(aligned, chosen, 0.0).astype(jnp.bfloat16)


def choose(here, adapter_row, total, steps, resident, holders):
    rows = adapter_row.shape[1] * steps
    return pl.pallas_call(
        functools.partial(choose_kernel, steps=steps, resident=resident, holders=holders),
        out_shape=jax.ShapeDtypeStruct((rows, total), jnp.bfloat16),
        in_specs=[SMEM, VMEM],
        out_specs=VMEM,
        compiler_params=pltpu.CompilerParams(vmem_limit_bytes=20 * MIB),
        cost_estimate=BRIEF,
    )(here, adapter_row)


def combine_kernel(chosen_ref, *refs, count, starts):
    pieces, sums, out, total_ref = refs[:count], refs[count:-2], refs[-2], refs[-1]
    stacked = jnp.concatenate([x[...] for x in pieces], axis=0)
    total_ref[...] = dot_nn(chosen_ref[...], stacked)
    for start, x in zip(starts, sums):
        span = pl.ds(start, x.shape[0])
        total_ref[span, :] += x[...].astype(jnp.float32)
    out[...] = total_ref[...].reshape(out.shape).astype(jnp.bfloat16)


def combine(chosen, pieces, sums, steps):
    width = pieces[0].shape[1]
    count = len(pieces)
    starts, flat = zip(*sums)
    rows = chosen.shape[0]
    block = min(width, 2 * HEAD_SIZE)

    def columns(x):
        return pl.BlockSpec((x, block), lambda j: (0, j))

    return pl.pallas_call(
        functools.partial(combine_kernel, count=count, starts=starts),
        grid=(width // block,),
        out_shape=jax.ShapeDtypeStruct((rows // steps, steps, width), jnp.bfloat16),
        in_specs=[pl.BlockSpec(chosen.shape, lambda j: (0, 0))]
        + [columns(x.shape[0]) for x in (*pieces, *flat)],
        out_specs=pl.BlockSpec((rows // steps, steps, block), lambda j: (0, 0, j)),
        scratch_shapes=[pltpu.VMEM((rows, block), jnp.float32)],
        compiler_params=pltpu.CompilerParams(vmem_limit_bytes=20 * MIB),
        cost_estimate=BRIEF,
    )(chosen, *pieces, *flat)


def local(
    queries,
    shared_prefix_cache,
    rollout_suffix_cache,
    fresh_key_value,
    rollout_prefix_index,
    rollout_suffix_length,
    rollout_adapter_index,
    output_projection_weight,
    adapter_shrink_weight,
    adapter_expand_weight,
):
    rolls, steps, width = queries.shape
    rows = rolls * steps
    prefix_count = shared_prefix_cache.shape[1]
    resident, rank, out_width = adapter_expand_weight.shape
    holders, sides = lax.axis_size("adapter"), lax.axis_size("tensor")
    block, chips = holders // FOLD, sides // 2
    here, side = lax.axis_index("adapter"), lax.axis_index("tensor")
    chip, core = side // 2, side % 2

    def in_block(shift):
        return [(i, i // block * block + (i + shift) % block) for i in range(holders)]

    cores = [(t, t // 2 * 2 + (t + 1) % 2) for t in range(sides)]

    def over_chips(shift):
        return [(t, (t // 2 + shift) % chips * 2 + t % 2) for t in range(sides)]

    own_shrink = adapter_shrink_weight.reshape(resident * rank, width)
    own_expand = adapter_expand_weight.reshape(resident * rank, out_width)
    far = [(i, (i + block) % holders) for i in range(holders)]

    slots = FOLD * resident * MOST * steps
    per_adapter = MOST * steps
    adapter_row = rollout_adapter_index.reshape(1, rolls)
    lengths, prefixes = rollout_suffix_length[None, :], rollout_prefix_index[None, :]
    here = here.reshape(1).astype(jnp.int32)
    core = core.reshape(1).astype(jnp.int32)
    chip_index = chip.reshape(1).astype(jnp.int32)
    tie = lax.optimization_barrier

    def send_over_chips(away, cuts):
        return [
            lax.ppermute(x, "tensor", over_chips(1 + k // cuts)) for k, x in enumerate(away)
        ]

    def placed(start, own, came, cuts):
        rows = own.shape[0] // cuts
        return [(start, own)] + [(start + k % cuts * rows, x) for k, x in enumerate(came)]

    shrink = lax.ppermute(own_shrink, "adapter", far)
    attended = attend(
        lengths, prefixes, queries, shared_prefix_cache, rollout_suffix_cache, fresh_key_value,
        steps, 0, rolls // BLOCK_ROLLS,
    )
    packed = list(pack(here, adapter_row, [attended], block, slots, steps, resident, holders))
    cut = own_expand.shape[0] // 2
    halves = [own_expand[:cut], own_expand[cut:]]
    attended, packed[0], halves = tie((attended, packed[0], halves))
    expands = [lax.ppermute(halves[0], "adapter", far)]
    pieces = [packed[0]] + [
        lax.ppermute(packed[d], "adapter", in_block(d)) for d in range(1, block)
    ]
    send, keep = project(core, attended, output_projection_weight, out_width)
    chosen = choose(here, adapter_row, block * slots, steps, resident, holders)
    send, chosen = tie((send, chosen))
    own, *away = pair_sums(chip_index, keep, lax.ppermute(send, "tensor", cores), 1)
    halves[1], expands[0] = tie((halves[1], expands[0]))
    pieces[0], shrink, halves[1] = tie((pieces[0], shrink, halves[1]))
    expands.append(lax.ppermute(halves[1], "adapter", far))
    codes = shrink_rows([own_shrink, shrink], pieces, per_adapter, rank)
    codes = codes + lax.ppermute(codes, "tensor", cores)
    brief = codes.astype(jnp.bfloat16)
    codes = [brief] + [lax.ppermute(brief, "tensor", over_chips(s)) for s in range(1, chips)]
    codes, away = tie((codes, away))
    came = send_over_chips(away, 1)
    wide = expand_rows([own_expand, *expands], codes, per_adapter, rank, block)
    back = [wide[0]] + [
        lax.ppermute(wide[d], "adapter", in_block(block - d)) for d in range(1, block)
    ]
    return combine(chosen, back, placed(0, own, came, 1), steps)


def solution(mesh):
    placed = (
        P("adapter", None, "tensor"),
        P(None, "adapter", None, "tensor"),
        P(None, "adapter", None, "tensor"),
        P(None, "adapter", None, "tensor"),
        P("adapter"),
        P("adapter"),
        P("adapter", None),
        P("tensor", None),
        P("adapter", None, "tensor"),
        P("adapter", None, "tensor"),
    )
    return jax.shard_map(
        local, mesh=mesh, in_specs=placed, out_specs=P("adapter", None, "tensor"), check_vma=False
    )
```

```python
import functools
import math

import jax
import jax.numpy as jnp
from jax import lax
from jax.experimental import pallas as pl
from jax.experimental.pallas import tpu as pltpu
from jax.sharding import PartitionSpec as P

HEAD_SIZE = 128
MOST = 5
FOLD = 2
CUTS = 1
BLOCK_ROLLS = 32
KEY_CHUNK = 512
NEG = float("-inf")
MIB = 1 << 20
BRIEF = pl.CostEstimate(flops=1024, bytes_accessed=1024, transcendentals=0)
LENGTHY = pl.CostEstimate(flops=1 << 36, bytes_accessed=1 << 27, transcendentals=0)
VMEM = pl.BlockSpec(memory_space=pltpu.VMEM)
ANY = pl.BlockSpec(memory_space=pl.ANY)
SMEM = pl.BlockSpec(memory_space=pltpu.SMEM)


def dot_nt(a, b):
    return lax.dot_general(a, b, (((1,), (1,)), ((), ())), preferred_element_type=jnp.float32)


def dot_nn(a, b):
    return jnp.dot(a, b, preferred_element_type=jnp.float32)


def attend_kernel(
    length_hbm, prefix_hbm, q_hbm, kv_hbm, suf_hbm, fr_hbm, o_ref,
    s_ref, m_ref, length_ref, prefix_ref, q_ref, kv_ref, suf_ref, fr_ref, sems,
    *, steps, group, first, blocks
):
    prefix_count, prefix_len = kv_ref.shape[1], kv_ref.shape[2]
    key_heads = kv_ref.shape[3] // HEAD_SIZE
    rolls, suf_len = suf_hbm.shape[1], suf_hbm.shape[2]
    block_rows = BLOCK_ROLLS * steps
    rows = block_rows * group
    last = first + blocks - 1
    suf_rolls = HEAD_SIZE // suf_len
    suf_rows = suf_rolls * steps
    suf_groups = BLOCK_ROLLS // suf_rolls
    window_rolls = HEAD_SIZE // steps
    windows = window_rolls // BLOCK_ROLLS
    factor = HEAD_SIZE ** (-0.5) * math.log2(math.e)
    chunks = prefix_len // KEY_CHUNK
    span = prefix_len

    def row_codes(block):
        shape = (block_rows, rolls)
        mine = block * BLOCK_ROLLS + lax.broadcasted_iota(jnp.int32, shape, 0) // steps
        lane = lax.broadcasted_iota(jnp.int32, shape, 1)
        code = length_ref[...] * prefix_count + prefix_ref[...] % prefix_count
        code = jnp.broadcast_to(code.astype(jnp.float32), shape)
        col = jnp.sum(jnp.where(mine == lane, code, 0.0), axis=1, keepdims=True)
        col = jnp.broadcast_to(col, (block_rows, HEAD_SIZE)).astype(jnp.int32)
        return col // prefix_count, col % prefix_count

    mine = pl.ds(first * BLOCK_ROLLS, blocks * BLOCK_ROLLS)
    loads = []
    for which in range(2):
        loads.append(pltpu.make_async_copy(kv_hbm.at[which], kv_ref.at[which], sems.at[2 * which]))
        loads.append(
            pltpu.make_async_copy(suf_hbm.at[which, mine], suf_ref.at[which], sems.at[2 * which + 1])
        )
    small = [
        pltpu.make_async_copy(src, dst, sems.at[4 + k])
        for k, (src, dst) in enumerate(
            [(q_hbm, q_ref), (fr_hbm, fr_ref), (length_hbm, length_ref), (prefix_hbm, prefix_ref)]
        )
    ]
    for load in [*reversed(small), *loads[:2]]:
        load.start()

    def tile_rows(x):
        return jnp.concatenate([x] * group, axis=0)

    def load_q(block, h):
        span = pl.ds(block * BLOCK_ROLLS, BLOCK_ROLLS)
        return [
            q_ref[span, :, pl.ds((h * group + g) * HEAD_SIZE, HEAD_SIZE)].reshape(
                block_rows, HEAD_SIZE
            )
            for g in range(group)
        ]

    def head_lanes(h):
        return pl.ds(h * HEAD_SIZE, HEAD_SIZE)

    def suffix_tile(which, block, i, h):
        start = (block - first) * BLOCK_ROLLS + i * suf_rolls
        tile = suf_ref[which, pl.ds(start, suf_rolls), :, head_lanes(h)]
        return tile.reshape(HEAD_SIZE, HEAD_SIZE)

    def fresh_tile(which, block, h):
        span = pl.ds(block // windows * window_rolls, window_rolls)
        return fr_ref[which, span, :, head_lanes(h)].reshape(HEAD_SIZE, HEAD_SIZE)

    def prefix_tile(which, c, h):
        return jnp.concatenate(
            [
                kv_ref[which, p, pl.ds(c * KEY_CHUNK, KEY_CHUNK), head_lanes(h)]
                for p in range(prefix_count)
            ],
            axis=1,
        )

    def scores(block, h, slot):
        length, local = row_codes(block)
        parts = load_q(block, h)
        stacked = jnp.concatenate(parts, axis=0)
        wide = jnp.concatenate(
            [
                jnp.concatenate(
                    [jnp.where(local == p, x, jnp.zeros_like(x)) for x in parts], axis=0
                )
                for p in range(prefix_count)
            ],
            axis=1,
        )
        shape = (block_rows, HEAD_SIZE)
        row = lax.broadcasted_iota(jnp.int32, shape, 0)
        lane = lax.broadcasted_iota(jnp.int32, shape, 1)
        roll = row // steps
        keep = (roll % suf_rolls == lane // suf_len) & (lane % suf_len < length)
        suf_bias = jnp.where(keep, 0.0, NEG)
        in_window = (block % windows) * BLOCK_ROLLS + roll
        keep = (in_window == lane // steps) & (lane % steps <= row % steps)
        fr_bias = jnp.where(keep, 0.0, NEG)
        suf = []
        for i in range(suf_groups):
            piece = jnp.concatenate(
                [x[i * suf_rows : (i + 1) * suf_rows] for x in parts], axis=0
            )
            suf.append(dot_nt(piece, suffix_tile(0, block, i, h)))
        suf = jnp.concatenate(
            [
                jnp.concatenate([x[g * suf_rows : (g + 1) * suf_rows] for x in suf], axis=0)
                for g in range(group)
            ],
            axis=0,
        ) + tile_rows(suf_bias)
        fr = dot_nt(stacked, fresh_tile(0, block, h)) + tile_rows(fr_bias)
        s_ref[slot, :, pl.ds(span, HEAD_SIZE)] = suf
        s_ref[slot, :, pl.ds(span + HEAD_SIZE, HEAD_SIZE)] = fr
        top = jnp.maximum(suf, fr)
        yield
        for c in range(chunks):
            s = dot_nt(wide, prefix_tile(0, c, h))
            s_ref[slot, :, pl.ds(c * KEY_CHUNK, KEY_CHUNK)] = s
            for j in range(KEY_CHUNK // HEAD_SIZE):
                top = jnp.maximum(top, s[:, j * HEAD_SIZE : (j + 1) * HEAD_SIZE])
            if c == chunks - 1:
                top = jnp.max(top, axis=1, keepdims=True) * factor
                m_ref[slot] = jnp.broadcast_to(top, (rows, HEAD_SIZE))
            yield

    def outputs(block, h, slot):
        top = m_ref[slot]

        def weigh(start, width):
            x = s_ref[slot, :, pl.ds(start, width)]
            wide_top = jnp.concatenate([top] * (width // HEAD_SIZE), axis=1)
            return jnp.exp2(x * factor - wide_top)

        both = weigh(span, 2 * HEAD_SIZE)
        total = both[:, :HEAD_SIZE] + both[:, HEAD_SIZE:]
        both = both.astype(jnp.bfloat16)
        fr = dot_nn(both[:, HEAD_SIZE:], fresh_tile(1, block, h))
        suf = []
        for i in range(suf_groups):
            piece = jnp.concatenate(
                [
                    both[
                        g * block_rows + i * suf_rows : g * block_rows + (i + 1) * suf_rows,
                        :HEAD_SIZE,
                    ]
                    for g in range(group)
                ],
                axis=0,
            )
            suf.append(dot_nn(piece, suffix_tile(1, block, i, h)))
        extra = fr + jnp.concatenate(
            [
                jnp.concatenate([x[g * suf_rows : (g + 1) * suf_rows] for x in suf], axis=0)
                for g in range(group)
            ],
            axis=0,
        )
        yield
        acc = None
        for c in range(chunks):
            p = weigh(c * KEY_CHUNK, KEY_CHUNK)
            for j in range(KEY_CHUNK // HEAD_SIZE):
                total = total + p[:, j * HEAD_SIZE : (j + 1) * HEAD_SIZE]
            part = dot_nn(p.astype(jnp.bfloat16), prefix_tile(1, c, h))
            acc = part if acc is None else acc + part
            if c == chunks - 1:
                _, local = row_codes(block)
                local = tile_rows(local)
                chosen = acc[:, :HEAD_SIZE]
                for q in range(1, prefix_count):
                    chosen = jnp.where(
                        local == q, acc[:, q * HEAD_SIZE : (q + 1) * HEAD_SIZE], chosen
                    )
                weight = 1.0 / jnp.sum(total, axis=1, keepdims=True)
                out = ((chosen + extra) * weight).astype(o_ref.dtype)
                start = pl.multiple_of((block - first) * block_rows, block_rows)
                for g in range(group):
                    o_ref[
                        pl.ds(start, block_rows),
                        pl.ds((h * group + g) * HEAD_SIZE, HEAD_SIZE),
                    ] = out[g * block_rows : (g + 1) * block_rows]
            yield

    def run(*streams):
        for _ in range(chunks + 1):
            for stream in streams:
                next(stream)

    for load in [*reversed(small), *loads[:2]]:
        load.wait()
    for load in loads[2:]:
        load.start()
    run(scores(first, 0, 0))
    for load in loads[2:]:
        load.wait()

    def step(block, ends):
        for h in range(key_heads):
            if h + 1 < key_heads:
                run(scores(block, h + 1, h + 1), outputs(block, h, h))
            elif ends:
                run(outputs(block, h, h))
            elif key_heads > 1:
                run(scores(block + 1, 0, 0), outputs(block, h, h))
            else:
                run(outputs(block, h, h))
                run(scores(block + 1, 0, 0))

    def body(block, carry):
        step(block, False)
        return carry

    lax.fori_loop(first, last, body, 0)
    step(last, True)


def attend(lengths, prefixes, queries, prefix, suffix, fresh, steps, first, blocks):
    width = queries.shape[-1]
    rows = blocks * BLOCK_ROLLS * steps
    key_heads = prefix.shape[3] // HEAD_SIZE
    group = width // HEAD_SIZE // key_heads
    unit_rows = BLOCK_ROLLS * steps * group
    span = prefix.shape[2] + 2 * HEAD_SIZE
    held = (2, blocks * BLOCK_ROLLS) + suffix.shape[2:]
    return pl.pallas_call(
        functools.partial(attend_kernel, steps=steps, group=group, first=first, blocks=blocks),
        out_shape=jax.ShapeDtypeStruct((rows, width), jnp.bfloat16),
        in_specs=[ANY] * 6,
        out_specs=VMEM,
        scratch_shapes=[
            pltpu.VMEM((key_heads, unit_rows, span), jnp.float32),
            pltpu.VMEM((key_heads, unit_rows, HEAD_SIZE), jnp.float32),
            pltpu.VMEM(lengths.shape, lengths.dtype),
            pltpu.VMEM(prefixes.shape, prefixes.dtype),
            pltpu.VMEM(queries.shape, queries.dtype),
            pltpu.VMEM(prefix.shape, prefix.dtype),
            pltpu.VMEM(held, suffix.dtype),
            pltpu.VMEM(fresh.shape, fresh.dtype),
            pltpu.SemaphoreType.DMA((8,)),
        ],
        compiler_params=pltpu.CompilerParams(vmem_limit_bytes=52 * MIB),
        cost_estimate=LENGTHY,
    )(lengths, prefixes, queries, prefix, suffix, fresh)


def project_kernel(core_ref, a_ref, w_ref, out_ref):
    del core_ref
    out_ref[0] = dot_nn(a_ref[...], w_ref[...]).astype(jnp.bfloat16)


def project(core, attended, weight, out_width):
    rows, width = attended.shape
    count = weight.shape[1] // out_width // 2
    return pl.pallas_call(
        project_kernel,
        grid_spec=pltpu.PrefetchScalarGridSpec(
            num_scalar_prefetch=1,
            grid=(count,),
            in_specs=[
                pl.BlockSpec((rows, width), lambda j, core: (0, 0)),
                pl.BlockSpec((width, out_width), lambda j, core: (0, j * 2 + core[0])),
            ],
            out_specs=pl.BlockSpec((1, rows, out_width), lambda j, core: (j, 0, 0)),
        ),
        out_shape=jax.ShapeDtypeStruct((count, rows, out_width), jnp.bfloat16),
        compiler_params=pltpu.CompilerParams(vmem_limit_bytes=14 * MIB),
        cost_estimate=BRIEF,
    )(core, attended, weight)


def pair_kernel(chip_ref, keep_ref, come_ref, own_ref, *outs, cuts):
    chips = keep_ref.shape[0]
    for shift in range(chips):
        index = (chip_ref[0] + shift) % chips
        pair = keep_ref[index].astype(jnp.float32) + come_ref[index].astype(jnp.float32)
        pair = pair.astype(jnp.bfloat16)
        if shift == 0:
            own_ref[...] = pair
        else:
            for k in range(cuts):
                out = outs[(shift - 1) * cuts + k]
                rows = out.shape[0]
                out[...] = pair[k * rows : (k + 1) * rows]


def pair_sums(chip, keep, come, cuts):
    chips, rows, width = keep.shape
    away = [jax.ShapeDtypeStruct((rows // cuts, width), jnp.bfloat16)] * ((chips - 1) * cuts)
    return pl.pallas_call(
        functools.partial(pair_kernel, cuts=cuts),
        out_shape=[jax.ShapeDtypeStruct((rows, width), jnp.bfloat16)] + away,
        in_specs=[SMEM, VMEM, VMEM],
        out_specs=[VMEM] * (1 + len(away)),
        compiler_params=pltpu.CompilerParams(vmem_limit_bytes=12 * MIB),
        cost_estimate=BRIEF,
    )(chip, keep, come)


def slot_of(row, turn, here, resident, holders):
    block = holders // FOLD
    holder = row // resident
    fold = (here // block - holder // block + FOLD) % FOLD
    place = (holder % block - here % block + block) % block
    return ((place * FOLD + fold) * resident + row % resident) * MOST + turn


def row_slots(row_ref, here, resident, holders):
    row = row_ref[...]
    shape = (row.shape[1], row.shape[1])
    across = jnp.broadcast_to(row, shape)
    down, lane = lax.broadcasted_iota(jnp.int32, shape, 0), lax.broadcasted_iota(jnp.int32, shape, 1)
    values = across.astype(jnp.float32)
    col = jnp.sum(jnp.where(down == lane, values, 0.0), axis=1, keepdims=True)
    same = jnp.broadcast_to(col, shape) == values
    turn_row = jnp.sum(jnp.where(same & (down < lane), 1.0, 0.0), axis=0, keepdims=True)
    turn_col = jnp.sum(jnp.where(same & (lane < down), 1.0, 0.0), axis=1, keepdims=True)
    place_row = slot_of(row, turn_row.astype(jnp.int32), here, resident, holders)
    place_col = slot_of(
        jnp.broadcast_to(col, shape).astype(jnp.int32),
        jnp.broadcast_to(turn_col, shape).astype(jnp.int32),
        here,
        resident,
        holders,
    )
    return place_row, place_col[:, :1]


def pack_kernel(here_ref, row_ref, *refs, steps, resident, holders, count):
    parts, outs = refs[:-count], refs[-count:]
    slots, rolls = outs[0].shape[0], row_ref.shape[1]
    place, _ = row_slots(row_ref, here_ref[0], resident, holders)
    for d, out in enumerate(outs):
        shape = (slots, rolls)
        slot = (d * slots + lax.broadcasted_iota(jnp.int32, shape, 0)) // steps
        picked = jnp.where(slot == jnp.broadcast_to(place, shape), 1.0, 0.0).astype(jnp.bfloat16)
        total, start = None, 0
        for part in parts:
            rows = part.shape[0]
            shape = (rolls, rows)
            spread = lax.broadcasted_iota(jnp.int32, shape, 0) == (
                start + lax.broadcasted_iota(jnp.int32, shape, 1)
            ) // steps
            chosen = dot_nn(picked, jnp.where(spread, 1.0, 0.0).astype(jnp.bfloat16))
            shape = (slots, rows)
            step = lax.broadcasted_iota(jnp.int32, shape, 0) % steps
            aligned = step == (start + lax.broadcasted_iota(jnp.int32, shape, 1)) % steps
            chosen = jnp.where(aligned, chosen, 0.0).astype(jnp.bfloat16)
            term = dot_nn(chosen, part[...])
            total = term if total is None else total + term
            start += rows
        out[...] = total.astype(jnp.bfloat16)


def pack(here, adapter_row, parts, count, slots, steps, resident, holders):
    width = parts[0].shape[1]
    return pl.pallas_call(
        functools.partial(
            pack_kernel, steps=steps, resident=resident, holders=holders, count=count
        ),
        out_shape=[jax.ShapeDtypeStruct((slots, width), jnp.bfloat16)] * count,
        in_specs=[SMEM] + [VMEM] * (1 + len(parts)),
        out_specs=[VMEM] * count,
        compiler_params=pltpu.CompilerParams(vmem_limit_bytes=12 * MIB),
        cost_estimate=BRIEF,
    )(here, adapter_row, *parts)


def adapter_mask(rows, per_adapter, rank, tile):
    lane = lax.broadcasted_iota(jnp.int32, (rows, HEAD_SIZE), 1) + tile * HEAD_SIZE
    row = lax.broadcasted_iota(jnp.int32, (rows, HEAD_SIZE), 0)
    return lane // rank == row // per_adapter


def shrink_kernel(*refs, per_adapter, rank, count):
    weights, pieces, out = refs[:FOLD], refs[FOLD : FOLD + count], refs[-1]
    rows = pieces[0].shape[0] // FOLD
    found = []
    for k in range(FOLD):
        span = pl.ds(k * rows, rows)
        every = dot_nt(
            jnp.concatenate([p[span, :] for p in pieces], axis=0),
            weights[k][...],
        )
        for d in range(count):
            total = None
            for tile in range(every.shape[1] // HEAD_SIZE):
                x = every[d * rows : (d + 1) * rows, tile * HEAD_SIZE : (tile + 1) * HEAD_SIZE]
                x = jnp.where(adapter_mask(rows, per_adapter, rank, tile), x, 0.0)
                total = x if total is None else total + x
            summed = total
            for turn in range(1, HEAD_SIZE // rank):
                summed = summed + pltpu.roll(total, turn * rank, axis=1)
            found.append(summed)
    lane = lax.broadcasted_iota(jnp.int32, (rows, HEAD_SIZE), 1)
    for d in range(count):
        both = jnp.where(lane < rank, found[d], found[count + d])
        out[pl.ds(d * rows, rows), :] = both


def shrink_rows(weights, pieces, per_adapter, rank):
    count = len(pieces)
    rows, width = pieces[0].shape
    return pl.pallas_call(
        functools.partial(shrink_kernel, per_adapter=per_adapter, rank=rank, count=count),
        out_shape=jax.ShapeDtypeStruct((count * rows // FOLD, HEAD_SIZE), jnp.float32),
        in_specs=[VMEM] * (FOLD + count),
        out_specs=VMEM,
        compiler_params=pltpu.CompilerParams(vmem_limit_bytes=8 * MIB),
        cost_estimate=LENGTHY,
    )(*weights, *pieces)


def expand_kernel(*refs, per_adapter, rank, count, terms):
    weights, sums, outs = refs[:FOLD], refs[FOLD : FOLD + terms], refs[FOLD + terms :]
    depth = weights[0].shape[0]
    rows = outs[0].shape[0] // FOLD
    for k in range(FOLD):
        spread = []
        for d in range(count):
            span = pl.ds(d * rows, rows)
            code = sums[0][span, :].astype(jnp.float32)
            for other in sums[1:]:
                code = code + other[span, :].astype(jnp.float32)
            lane = lax.broadcasted_iota(jnp.int32, (rows, HEAD_SIZE), 1)
            turned = pltpu.roll(code, rank, axis=1)
            code = jnp.where((lane < rank) == (k == 0), code, turned)
            spread.append(
                jnp.concatenate(
                    [
                        jnp.where(adapter_mask(rows, per_adapter, rank, tile), code, 0.0)
                        for tile in range(depth // HEAD_SIZE)
                    ],
                    axis=1,
                ).astype(jnp.bfloat16)
            )
        wide = dot_nn(jnp.concatenate(spread, axis=0), weights[k][...])
        wide = wide.astype(jnp.bfloat16)
        for d in range(count):
            outs[d][pl.ds(k * rows, rows), :] = wide[d * rows : (d + 1) * rows]


def expand_rows(weights, sums, per_adapter, rank, count):
    rows = sums[0].shape[0] // count * FOLD
    width = weights[0].shape[1]
    return pl.pallas_call(
        functools.partial(
            expand_kernel, per_adapter=per_adapter, rank=rank, count=count, terms=len(sums)
        ),
        out_shape=[jax.ShapeDtypeStruct((rows, width), jnp.bfloat16)] * count,
        in_specs=[VMEM] * (FOLD + len(sums)),
        out_specs=[VMEM] * count,
        compiler_params=pltpu.CompilerParams(vmem_limit_bytes=8 * MIB),
        cost_estimate=LENGTHY,
    )(*weights, *sums)


def choose_kernel(here_ref, row_ref, chosen_ref, *, steps, resident, holders):
    rows, total = chosen_ref.shape
    rolls = row_ref.shape[1]
    _, place = row_slots(row_ref, here_ref[0], resident, holders)
    shape = (rolls, total)
    slot = lax.broadcasted_iota(jnp.int32, shape, 1) // steps
    picked = jnp.where(slot == jnp.broadcast_to(place, shape), 1.0, 0.0).astype(jnp.bfloat16)
    shape = (rows, rolls)
    roll = lax.broadcasted_iota(jnp.int32, shape, 0) // steps
    spread = roll == lax.broadcasted_iota(jnp.int32, shape, 1)
    chosen = dot_nn(jnp.where(spread, 1.0, 0.0).astype(jnp.bfloat16), picked)
    shape = (rows, total)
    step = lax.broadcasted_iota(jnp.int32, shape, 0) % steps
    aligned = step == lax.broadcasted_iota(jnp.int32, shape, 1) % steps
    chosen_ref[...] = jnp.where(aligned, chosen, 0.0).astype(jnp.bfloat16)


def choose(here, adapter_row, total, steps, resident, holders):
    rows = adapter_row.shape[1] * steps
    return pl.pallas_call(
        functools.partial(choose_kernel, steps=steps, resident=resident, holders=holders),
        out_shape=jax.ShapeDtypeStruct((rows, total), jnp.bfloat16),
        in_specs=[SMEM, VMEM],
        out_specs=VMEM,
        compiler_params=pltpu.CompilerParams(vmem_limit_bytes=20 * MIB),
        cost_estimate=BRIEF,
    )(here, adapter_row)


def combine_kernel(chosen_ref, *refs, count, starts):
    pieces, sums, out, total_ref = refs[:count], refs[count:-2], refs[-2], refs[-1]
    stacked = jnp.concatenate([x[...] for x in pieces], axis=0)
    total_ref[...] = dot_nn(chosen_ref[...], stacked)
    for start, x in zip(starts, sums):
        span = pl.ds(start, x.shape[0])
        total_ref[span, :] += x[...].astype(jnp.float32)
    out[...] = total_ref[...].reshape(out.shape).astype(jnp.bfloat16)


def combine(chosen, pieces, sums, steps):
    width = pieces[0].shape[1]
    count = len(pieces)
    starts, flat = zip(*sums)
    rows = chosen.shape[0]
    block = min(width, 2 * HEAD_SIZE)

    def columns(x):
        return pl.BlockSpec((x, block), lambda j: (0, j))

    return pl.pallas_call(
        functools.partial(combine_kernel, count=count, starts=starts),
        grid=(width // block,),
        out_shape=jax.ShapeDtypeStruct((rows // steps, steps, width), jnp.bfloat16),
        in_specs=[pl.BlockSpec(chosen.shape, lambda j: (0, 0))]
        + [columns(x.shape[0]) for x in (*pieces, *flat)],
        out_specs=pl.BlockSpec((rows // steps, steps, block), lambda j: (0, 0, j)),
        scratch_shapes=[pltpu.VMEM((rows, block), jnp.float32)],
        compiler_params=pltpu.CompilerParams(vmem_limit_bytes=20 * MIB),
        cost_estimate=BRIEF,
    )(chosen, *pieces, *flat)


def local(
    queries,
    shared_prefix_cache,
    rollout_suffix_cache,
    fresh_key_value,
    rollout_prefix_index,
    rollout_suffix_length,
    rollout_adapter_index,
    output_projection_weight,
    adapter_shrink_weight,
    adapter_expand_weight,
):
    rolls, steps, width = queries.shape
    rows = rolls * steps
    prefix_count = shared_prefix_cache.shape[1]
    resident, rank, out_width = adapter_expand_weight.shape
    holders, sides = lax.axis_size("adapter"), lax.axis_size("tensor")
    block, chips = holders // FOLD, sides // 2
    here, side = lax.axis_index("adapter"), lax.axis_index("tensor")
    chip, core = side // 2, side % 2

    def in_block(shift):
        return [(i, i // block * block + (i + shift) % block) for i in range(holders)]

    cores = [(t, t // 2 * 2 + (t + 1) % 2) for t in range(sides)]

    def over_chips(shift):
        return [(t, (t // 2 + shift) % chips * 2 + t % 2) for t in range(sides)]

    own_shrink = adapter_shrink_weight.reshape(resident * rank, width)
    own_expand = adapter_expand_weight.reshape(resident * rank, out_width)
    far = [(i, (i + block) % holders) for i in range(holders)]

    slots = FOLD * resident * MOST * steps
    per_adapter = MOST * steps
    adapter_row = rollout_adapter_index.reshape(1, rolls)
    lengths, prefixes = rollout_suffix_length[None, :], rollout_prefix_index[None, :]
    here = here.reshape(1).astype(jnp.int32)
    core = core.reshape(1).astype(jnp.int32)
    chip_index = chip.reshape(1).astype(jnp.int32)
    tie = lax.optimization_barrier

    def send_over_chips(away, cuts):
        return [
            lax.ppermute(x, "tensor", over_chips(1 + k // cuts)) for k, x in enumerate(away)
        ]

    def placed(start, own, came, cuts):
        rows = own.shape[0] // cuts
        return [(start, own)] + [(start + k % cuts * rows, x) for k, x in enumerate(came)]

    shrink = lax.ppermute(own_shrink, "adapter", far)
    attended = attend(
        lengths, prefixes, queries, shared_prefix_cache, rollout_suffix_cache, fresh_key_value,
        steps, 0, rolls // BLOCK_ROLLS,
    )
    packed = list(pack(here, adapter_row, [attended], block, slots, steps, resident, holders))
    attended, packed[0] = tie((attended, packed[0]))
    pieces = [packed[0]] + [
        lax.ppermute(packed[d], "adapter", in_block(d)) for d in range(1, block)
    ]
    send = project(1 - core, attended, output_projection_weight, out_width)
    chosen = choose(here, adapter_row, block * slots, steps, resident, holders)
    send, chosen = tie((send, chosen))
    come = lax.ppermute(send, "tensor", cores)
    pieces[0], shrink, moved = tie((pieces[0], shrink, own_expand))
    expand = lax.ppermute(moved, "adapter", far)
    codes = shrink_rows([own_shrink, shrink], pieces, per_adapter, rank)
    codes = codes + lax.ppermute(codes, "tensor", cores)
    brief, attended = tie((codes.astype(jnp.bfloat16), attended))
    keep = project(core, attended, output_projection_weight, out_width)
    own, *away = pair_sums(chip_index, keep, come, 1)
    codes = [brief] + [lax.ppermute(brief, "tensor", over_chips(s)) for s in range(1, chips)]
    codes, away = tie((codes, away))
    came = send_over_chips(away, 1)
    wide = expand_rows([own_expand, expand], codes, per_adapter, rank, block)
    back = [wide[0]] + [
        lax.ppermute(wide[d], "adapter", in_block(block - d)) for d in range(1, block)
    ]
    return combine(chosen, back, placed(0, own, came, 1), steps)


def solution(mesh):
    placed = (
        P("adapter", None, "tensor"),
        P(None, "adapter", None, "tensor"),
        P(None, "adapter", None, "tensor"),
        P(None, "adapter", None, "tensor"),
        P("adapter"),
        P("adapter"),
        P("adapter", None),
        P("tensor", None),
        P("adapter", None, "tensor"),
        P("adapter", None, "tensor"),
    )
    return jax.shard_map(
        local, mesh=mesh, in_specs=placed, out_specs=P("adapter", None, "tensor"), check_vma=False
    )
```

```python
import functools
import math

import jax
import jax.numpy as jnp
from jax import lax
from jax.experimental import pallas as pl
from jax.experimental.pallas import tpu as pltpu
from jax.sharding import PartitionSpec as P

HEAD_SIZE = 128
MOST = 5
FOLD = 2
CUTS = 1
BLOCK_ROLLS = 32
KEY_CHUNK = 512
NEG = float("-inf")
MIB = 1 << 20
BRIEF = pl.CostEstimate(flops=1024, bytes_accessed=1024, transcendentals=0)
LENGTHY = pl.CostEstimate(flops=1 << 36, bytes_accessed=1 << 27, transcendentals=0)
VMEM = pl.BlockSpec(memory_space=pltpu.VMEM)
ANY = pl.BlockSpec(memory_space=pl.ANY)
SMEM = pl.BlockSpec(memory_space=pltpu.SMEM)


def dot_nt(a, b):
    return lax.dot_general(a, b, (((1,), (1,)), ((), ())), preferred_element_type=jnp.float32)


def dot_nn(a, b):
    return jnp.dot(a, b, preferred_element_type=jnp.float32)


def attend_kernel(
    length_hbm, prefix_hbm, q_hbm, kv_hbm, suf_hbm, fr_hbm, o_ref,
    s_ref, m_ref, length_ref, prefix_ref, q_ref, kv_ref, suf_ref, fr_ref, sems,
    *, steps, group, first, blocks
):
    prefix_count, prefix_len = kv_ref.shape[1], kv_ref.shape[2]
    key_heads = kv_ref.shape[3] // HEAD_SIZE
    rolls, suf_len = suf_hbm.shape[1], suf_hbm.shape[2]
    block_rows = BLOCK_ROLLS * steps
    rows = block_rows * group
    last = first + blocks - 1
    suf_rolls = HEAD_SIZE // suf_len
    suf_rows = suf_rolls * steps
    suf_groups = BLOCK_ROLLS // suf_rolls
    window_rolls = HEAD_SIZE // steps
    windows = window_rolls // BLOCK_ROLLS
    factor = HEAD_SIZE ** (-0.5) * math.log2(math.e)
    chunks = prefix_len // KEY_CHUNK
    span = prefix_len

    def row_codes(block):
        shape = (block_rows, rolls)
        mine = block * BLOCK_ROLLS + lax.broadcasted_iota(jnp.int32, shape, 0) // steps
        lane = lax.broadcasted_iota(jnp.int32, shape, 1)
        code = length_ref[...] * prefix_count + prefix_ref[...] % prefix_count
        code = jnp.broadcast_to(code.astype(jnp.float32), shape)
        col = jnp.sum(jnp.where(mine == lane, code, 0.0), axis=1, keepdims=True)
        col = jnp.broadcast_to(col, (block_rows, HEAD_SIZE)).astype(jnp.int32)
        return col // prefix_count, col % prefix_count

    mine = pl.ds(first * BLOCK_ROLLS, blocks * BLOCK_ROLLS)
    loads = []
    for which in range(2):
        loads.append(pltpu.make_async_copy(kv_hbm.at[which], kv_ref.at[which], sems.at[2 * which]))
        loads.append(
            pltpu.make_async_copy(suf_hbm.at[which, mine], suf_ref.at[which], sems.at[2 * which + 1])
        )
    small = [
        pltpu.make_async_copy(src, dst, sems.at[4 + k])
        for k, (src, dst) in enumerate(
            [(q_hbm, q_ref), (fr_hbm, fr_ref), (length_hbm, length_ref), (prefix_hbm, prefix_ref)]
        )
    ]
    for load in [*reversed(small), *loads]:
        load.start()

    def tile_rows(x):
        return jnp.concatenate([x] * group, axis=0)

    def load_q(block, h):
        span = pl.ds(block * BLOCK_ROLLS, BLOCK_ROLLS)
        return [
            q_ref[span, :, pl.ds((h * group + g) * HEAD_SIZE, HEAD_SIZE)].reshape(
                block_rows, HEAD_SIZE
            )
            for g in range(group)
        ]

    def head_lanes(h):
        return pl.ds(h * HEAD_SIZE, HEAD_SIZE)

    def suffix_tile(which, block, i, h):
        start = (block - first) * BLOCK_ROLLS + i * suf_rolls
        tile = suf_ref[which, pl.ds(start, suf_rolls), :, head_lanes(h)]
        return tile.reshape(HEAD_SIZE, HEAD_SIZE)

    def fresh_tile(which, block, h):
        span = pl.ds(block // windows * window_rolls, window_rolls)
        return fr_ref[which, span, :, head_lanes(h)].reshape(HEAD_SIZE, HEAD_SIZE)

    def prefix_tile(which, c, h):
        return jnp.concatenate(
            [
                kv_ref[which, p, pl.ds(c * KEY_CHUNK, KEY_CHUNK), head_lanes(h)]
                for p in range(prefix_count)
            ],
            axis=1,
        )

    def scores(block, h, slot):
        length, local = row_codes(block)
        parts = load_q(block, h)
        stacked = jnp.concatenate(parts, axis=0)
        wide = jnp.concatenate(
            [
                jnp.concatenate(
                    [jnp.where(local == p, x, jnp.zeros_like(x)) for x in parts], axis=0
                )
                for p in range(prefix_count)
            ],
            axis=1,
        )
        shape = (block_rows, HEAD_SIZE)
        row = lax.broadcasted_iota(jnp.int32, shape, 0)
        lane = lax.broadcasted_iota(jnp.int32, shape, 1)
        roll = row // steps
        keep = (roll % suf_rolls == lane // suf_len) & (lane % suf_len < length)
        suf_bias = jnp.where(keep, 0.0, NEG)
        in_window = (block % windows) * BLOCK_ROLLS + roll
        keep = (in_window == lane // steps) & (lane % steps <= row % steps)
        fr_bias = jnp.where(keep, 0.0, NEG)
        suf = []
        for i in range(suf_groups):
            piece = jnp.concatenate(
                [x[i * suf_rows : (i + 1) * suf_rows] for x in parts], axis=0
            )
            suf.append(dot_nt(piece, suffix_tile(0, block, i, h)))
        suf = jnp.concatenate(
            [
                jnp.concatenate([x[g * suf_rows : (g + 1) * suf_rows] for x in suf], axis=0)
                for g in range(group)
            ],
            axis=0,
        ) + tile_rows(suf_bias)
        fr = dot_nt(stacked, fresh_tile(0, block, h)) + tile_rows(fr_bias)
        s_ref[slot, :, pl.ds(span, HEAD_SIZE)] = suf
        s_ref[slot, :, pl.ds(span + HEAD_SIZE, HEAD_SIZE)] = fr
        top = jnp.maximum(suf, fr)
        yield
        for c in range(chunks):
            s = dot_nt(wide, prefix_tile(0, c, h))
            s_ref[slot, :, pl.ds(c * KEY_CHUNK, KEY_CHUNK)] = s
            for j in range(KEY_CHUNK // HEAD_SIZE):
                top = jnp.maximum(top, s[:, j * HEAD_SIZE : (j + 1) * HEAD_SIZE])
            if c == chunks - 1:
                top = jnp.max(top, axis=1, keepdims=True) * factor
                m_ref[slot] = jnp.broadcast_to(top, (rows, HEAD_SIZE))
            yield

    def outputs(block, h, slot):
        top = m_ref[slot]

        def weigh(start, width):
            x = s_ref[slot, :, pl.ds(start, width)]
            wide_top = jnp.concatenate([top] * (width // HEAD_SIZE), axis=1)
            return jnp.exp2(x * factor - wide_top)

        both = weigh(span, 2 * HEAD_SIZE)
        total = both[:, :HEAD_SIZE] + both[:, HEAD_SIZE:]
        both = both.astype(jnp.bfloat16)
        fr = dot_nn(both[:, HEAD_SIZE:], fresh_tile(1, block, h))
        suf = []
        for i in range(suf_groups):
            piece = jnp.concatenate(
                [
                    both[
                        g * block_rows + i * suf_rows : g * block_rows + (i + 1) * suf_rows,
                        :HEAD_SIZE,
                    ]
                    for g in range(group)
                ],
                axis=0,
            )
            suf.append(dot_nn(piece, suffix_tile(1, block, i, h)))
        extra = fr + jnp.concatenate(
            [
                jnp.concatenate([x[g * suf_rows : (g + 1) * suf_rows] for x in suf], axis=0)
                for g in range(group)
            ],
            axis=0,
        )
        yield
        acc = None
        for c in range(chunks):
            p = weigh(c * KEY_CHUNK, KEY_CHUNK)
            for j in range(KEY_CHUNK // HEAD_SIZE):
                total = total + p[:, j * HEAD_SIZE : (j + 1) * HEAD_SIZE]
            part = dot_nn(p.astype(jnp.bfloat16), prefix_tile(1, c, h))
            acc = part if acc is None else acc + part
            if c == chunks - 1:
                _, local = row_codes(block)
                local = tile_rows(local)
                chosen = acc[:, :HEAD_SIZE]
                for q in range(1, prefix_count):
                    chosen = jnp.where(
                        local == q, acc[:, q * HEAD_SIZE : (q + 1) * HEAD_SIZE], chosen
                    )
                weight = 1.0 / jnp.sum(total, axis=1, keepdims=True)
                out = ((chosen + extra) * weight).astype(o_ref.dtype)
                start = pl.multiple_of((block - first) * block_rows, block_rows)
                for g in range(group):
                    o_ref[
                        pl.ds(start, block_rows),
                        pl.ds((h * group + g) * HEAD_SIZE, HEAD_SIZE),
                    ] = out[g * block_rows : (g + 1) * block_rows]
            yield

    def run(*streams):
        for _ in range(chunks + 1):
            for stream in streams:
                next(stream)

    for load in [*reversed(small), *loads[:2]]:
        load.wait()
    run(scores(first, 0, 0))
    for load in loads[2:]:
        load.wait()

    def body(block, carry):
        for h in range(key_heads):
            if h + 1 < key_heads:
                run(scores(block, h + 1, h + 1), outputs(block, h, h))
            elif key_heads > 1:
                following = jnp.minimum(block + 1, last)
                run(scores(following, 0, 0), outputs(block, h, h))
            else:
                run(outputs(block, h, h))
                run(scores(jnp.minimum(block + 1, last), 0, 0))
        return carry

    lax.fori_loop(first, first + blocks, body, 0)


def attend(lengths, prefixes, queries, prefix, suffix, fresh, steps, first, blocks):
    width = queries.shape[-1]
    rows = blocks * BLOCK_ROLLS * steps
    key_heads = prefix.shape[3] // HEAD_SIZE
    group = width // HEAD_SIZE // key_heads
    unit_rows = BLOCK_ROLLS * steps * group
    span = prefix.shape[2] + 2 * HEAD_SIZE
    held = (2, blocks * BLOCK_ROLLS) + suffix.shape[2:]
    return pl.pallas_call(
        functools.partial(attend_kernel, steps=steps, group=group, first=first, blocks=blocks),
        out_shape=jax.ShapeDtypeStruct((rows, width), jnp.bfloat16),
        in_specs=[ANY] * 6,
        out_specs=VMEM,
        scratch_shapes=[
            pltpu.VMEM((key_heads, unit_rows, span), jnp.float32),
            pltpu.VMEM((key_heads, unit_rows, HEAD_SIZE), jnp.float32),
            pltpu.VMEM(lengths.shape, lengths.dtype),
            pltpu.VMEM(prefixes.shape, prefixes.dtype),
            pltpu.VMEM(queries.shape, queries.dtype),
            pltpu.VMEM(prefix.shape, prefix.dtype),
            pltpu.VMEM(held, suffix.dtype),
            pltpu.VMEM(fresh.shape, fresh.dtype),
            pltpu.SemaphoreType.DMA((8,)),
        ],
        compiler_params=pltpu.CompilerParams(vmem_limit_bytes=44 * MIB),
        cost_estimate=LENGTHY,
    )(lengths, prefixes, queries, prefix, suffix, fresh)


def project_kernel(core_ref, a_ref, w_ref, out_ref):
    del core_ref
    out_ref[0] = dot_nn(a_ref[...], w_ref[...]).astype(jnp.bfloat16)


def project(core, attended, weight, out_width):
    rows, width = attended.shape
    count = weight.shape[1] // out_width // 2
    return pl.pallas_call(
        project_kernel,
        grid_spec=pltpu.PrefetchScalarGridSpec(
            num_scalar_prefetch=1,
            grid=(count,),
            in_specs=[
                pl.BlockSpec((rows, width), lambda j, core: (0, 0)),
                pl.BlockSpec((width, out_width), lambda j, core: (0, j * 2 + core[0])),
            ],
            out_specs=pl.BlockSpec((1, rows, out_width), lambda j, core: (j, 0, 0)),
        ),
        out_shape=jax.ShapeDtypeStruct((count, rows, out_width), jnp.bfloat16),
        compiler_params=pltpu.CompilerParams(vmem_limit_bytes=14 * MIB),
        cost_estimate=BRIEF,
    )(core, attended, weight)


def pair_kernel(chip_ref, keep_ref, come_ref, own_ref, *outs, cuts):
    chips = keep_ref.shape[0]
    for shift in range(chips):
        index = (chip_ref[0] + shift) % chips
        pair = keep_ref[index].astype(jnp.float32) + come_ref[index].astype(jnp.float32)
        pair = pair.astype(jnp.bfloat16)
        if shift == 0:
            own_ref[...] = pair
        else:
            for k in range(cuts):
                out = outs[(shift - 1) * cuts + k]
                rows = out.shape[0]
                out[...] = pair[k * rows : (k + 1) * rows]


def pair_sums(chip, keep, come, cuts):
    chips, rows, width = keep.shape
    away = [jax.ShapeDtypeStruct((rows // cuts, width), jnp.bfloat16)] * ((chips - 1) * cuts)
    return pl.pallas_call(
        functools.partial(pair_kernel, cuts=cuts),
        out_shape=[jax.ShapeDtypeStruct((rows, width), jnp.bfloat16)] + away,
        in_specs=[SMEM, VMEM, VMEM],
        out_specs=[VMEM] * (1 + len(away)),
        compiler_params=pltpu.CompilerParams(vmem_limit_bytes=12 * MIB),
        cost_estimate=BRIEF,
    )(chip, keep, come)


def slot_of(row, turn, here, resident, holders):
    block = holders // FOLD
    holder = row // resident
    fold = (here // block - holder // block + FOLD) % FOLD
    place = (holder % block - here % block + block) % block
    return ((place * FOLD + fold) * resident + row % resident) * MOST + turn


def row_slots(row_ref, here, resident, holders):
    row = row_ref[...]
    shape = (row.shape[1], row.shape[1])
    across = jnp.broadcast_to(row, shape)
    down, lane = lax.broadcasted_iota(jnp.int32, shape, 0), lax.broadcasted_iota(jnp.int32, shape, 1)
    values = across.astype(jnp.float32)
    col = jnp.sum(jnp.where(down == lane, values, 0.0), axis=1, keepdims=True)
    same = jnp.broadcast_to(col, shape) == values
    turn_row = jnp.sum(jnp.where(same & (down < lane), 1.0, 0.0), axis=0, keepdims=True)
    turn_col = jnp.sum(jnp.where(same & (lane < down), 1.0, 0.0), axis=1, keepdims=True)
    place_row = slot_of(row, turn_row.astype(jnp.int32), here, resident, holders)
    place_col = slot_of(
        jnp.broadcast_to(col, shape).astype(jnp.int32),
        jnp.broadcast_to(turn_col, shape).astype(jnp.int32),
        here,
        resident,
        holders,
    )
    return place_row, place_col[:, :1]


def pack_kernel(here_ref, row_ref, *refs, steps, resident, holders, count):
    parts, outs = refs[:-count], refs[-count:]
    slots, rolls = outs[0].shape[0], row_ref.shape[1]
    place, _ = row_slots(row_ref, here_ref[0], resident, holders)
    for d, out in enumerate(outs):
        shape = (slots, rolls)
        slot = (d * slots + lax.broadcasted_iota(jnp.int32, shape, 0)) // steps
        picked = jnp.where(slot == jnp.broadcast_to(place, shape), 1.0, 0.0).astype(jnp.bfloat16)
        total, start = None, 0
        for part in parts:
            rows = part.shape[0]
            shape = (rolls, rows)
            spread = lax.broadcasted_iota(jnp.int32, shape, 0) == (
                start + lax.broadcasted_iota(jnp.int32, shape, 1)
            ) // steps
            chosen = dot_nn(picked, jnp.where(spread, 1.0, 0.0).astype(jnp.bfloat16))
            shape = (slots, rows)
            step = lax.broadcasted_iota(jnp.int32, shape, 0) % steps
            aligned = step == (start + lax.broadcasted_iota(jnp.int32, shape, 1)) % steps
            chosen = jnp.where(aligned, chosen, 0.0).astype(jnp.bfloat16)
            term = dot_nn(chosen, part[...])
            total = term if total is None else total + term
            start += rows
        out[...] = total.astype(jnp.bfloat16)


def pack(here, adapter_row, parts, count, slots, steps, resident, holders):
    width = parts[0].shape[1]
    return pl.pallas_call(
        functools.partial(
            pack_kernel, steps=steps, resident=resident, holders=holders, count=count
        ),
        out_shape=[jax.ShapeDtypeStruct((slots, width), jnp.bfloat16)] * count,
        in_specs=[SMEM] + [VMEM] * (1 + len(parts)),
        out_specs=[VMEM] * count,
        compiler_params=pltpu.CompilerParams(vmem_limit_bytes=12 * MIB),
        cost_estimate=BRIEF,
    )(here, adapter_row, *parts)


def adapter_mask(rows, per_adapter, rank, tile):
    lane = lax.broadcasted_iota(jnp.int32, (rows, HEAD_SIZE), 1) + tile * HEAD_SIZE
    row = lax.broadcasted_iota(jnp.int32, (rows, HEAD_SIZE), 0)
    return lane // rank == row // per_adapter


def shrink_kernel(*refs, per_adapter, rank, count):
    weights, pieces, out = refs[:FOLD], refs[FOLD : FOLD + count], refs[-1]
    rows = pieces[0].shape[0] // FOLD
    found = []
    for k in range(FOLD):
        span = pl.ds(k * rows, rows)
        every = dot_nt(
            jnp.concatenate([p[span, :] for p in pieces], axis=0),
            weights[k][...],
        )
        for d in range(count):
            total = None
            for tile in range(every.shape[1] // HEAD_SIZE):
                x = every[d * rows : (d + 1) * rows, tile * HEAD_SIZE : (tile + 1) * HEAD_SIZE]
                x = jnp.where(adapter_mask(rows, per_adapter, rank, tile), x, 0.0)
                total = x if total is None else total + x
            summed = total
            for turn in range(1, HEAD_SIZE // rank):
                summed = summed + pltpu.roll(total, turn * rank, axis=1)
            found.append(summed)
    lane = lax.broadcasted_iota(jnp.int32, (rows, HEAD_SIZE), 1)
    for d in range(count):
        both = jnp.where(lane < rank, found[d], found[count + d])
        out[pl.ds(d * rows, rows), :] = both


def shrink_rows(weights, pieces, per_adapter, rank):
    count = len(pieces)
    rows, width = pieces[0].shape
    return pl.pallas_call(
        functools.partial(shrink_kernel, per_adapter=per_adapter, rank=rank, count=count),
        out_shape=jax.ShapeDtypeStruct((count * rows // FOLD, HEAD_SIZE), jnp.float32),
        in_specs=[VMEM] * (FOLD + count),
        out_specs=VMEM,
        compiler_params=pltpu.CompilerParams(vmem_limit_bytes=8 * MIB),
        cost_estimate=LENGTHY,
    )(*weights, *pieces)


def expand_kernel(*refs, per_adapter, rank, count, terms):
    weights, sums, outs = refs[:FOLD], refs[FOLD : FOLD + terms], refs[FOLD + terms :]
    depth = weights[0].shape[0]
    rows = outs[0].shape[0] // FOLD
    for k in range(FOLD):
        spread = []
        for d in range(count):
            span = pl.ds(d * rows, rows)
            code = sums[0][span, :].astype(jnp.float32)
            for other in sums[1:]:
                code = code + other[span, :].astype(jnp.float32)
            lane = lax.broadcasted_iota(jnp.int32, (rows, HEAD_SIZE), 1)
            turned = pltpu.roll(code, rank, axis=1)
            code = jnp.where((lane < rank) == (k == 0), code, turned)
            spread.append(
                jnp.concatenate(
                    [
                        jnp.where(adapter_mask(rows, per_adapter, rank, tile), code, 0.0)
                        for tile in range(depth // HEAD_SIZE)
                    ],
                    axis=1,
                ).astype(jnp.bfloat16)
            )
        wide = dot_nn(jnp.concatenate(spread, axis=0), weights[k][...])
        wide = wide.astype(jnp.bfloat16)
        for d in range(count):
            outs[d][pl.ds(k * rows, rows), :] = wide[d * rows : (d + 1) * rows]


def expand_rows(weights, sums, per_adapter, rank, count):
    rows = sums[0].shape[0] // count * FOLD
    width = weights[0].shape[1]
    return pl.pallas_call(
        functools.partial(
            expand_kernel, per_adapter=per_adapter, rank=rank, count=count, terms=len(sums)
        ),
        out_shape=[jax.ShapeDtypeStruct((rows, width), jnp.bfloat16)] * count,
        in_specs=[VMEM] * (FOLD + len(sums)),
        out_specs=[VMEM] * count,
        compiler_params=pltpu.CompilerParams(vmem_limit_bytes=8 * MIB),
        cost_estimate=LENGTHY,
    )(*weights, *sums)


def choose_kernel(here_ref, row_ref, chosen_ref, *, steps, resident, holders):
    rows, total = chosen_ref.shape
    rolls = row_ref.shape[1]
    _, place = row_slots(row_ref, here_ref[0], resident, holders)
    shape = (rolls, total)
    slot = lax.broadcasted_iota(jnp.int32, shape, 1) // steps
    picked = jnp.where(slot == jnp.broadcast_to(place, shape), 1.0, 0.0).astype(jnp.bfloat16)
    shape = (rows, rolls)
    roll = lax.broadcasted_iota(jnp.int32, shape, 0) // steps
    spread = roll == lax.broadcasted_iota(jnp.int32, shape, 1)
    chosen = dot_nn(jnp.where(spread, 1.0, 0.0).astype(jnp.bfloat16), picked)
    shape = (rows, total)
    step = lax.broadcasted_iota(jnp.int32, shape, 0) % steps
    aligned = step == lax.broadcasted_iota(jnp.int32, shape, 1) % steps
    chosen_ref[...] = jnp.where(aligned, chosen, 0.0).astype(jnp.bfloat16)


def choose(here, adapter_row, total, steps, resident, holders):
    rows = adapter_row.shape[1] * steps
    return pl.pallas_call(
        functools.partial(choose_kernel, steps=steps, resident=resident, holders=holders),
        out_shape=jax.ShapeDtypeStruct((rows, total), jnp.bfloat16),
        in_specs=[SMEM, VMEM],
        out_specs=VMEM,
        compiler_params=pltpu.CompilerParams(vmem_limit_bytes=20 * MIB),
        cost_estimate=BRIEF,
    )(here, adapter_row)


def combine_kernel(chosen_ref, *refs, count, starts):
    pieces, sums, out, total_ref = refs[:count], refs[count:-2], refs[-2], refs[-1]
    stacked = jnp.concatenate([x[...] for x in pieces], axis=0)
    total_ref[...] = dot_nn(chosen_ref[...], stacked)
    for start, x in zip(starts, sums):
        span = pl.ds(start, x.shape[0])
        total_ref[span, :] += x[...].astype(jnp.float32)
    out[...] = total_ref[...].reshape(out.shape).astype(jnp.bfloat16)


def combine(chosen, pieces, sums, steps):
    width = pieces[0].shape[1]
    count = len(pieces)
    starts, flat = zip(*sums)
    rows = chosen.shape[0]
    block = min(width, 2 * HEAD_SIZE)

    def columns(x):
        return pl.BlockSpec((x, block), lambda j: (0, j))

    return pl.pallas_call(
        functools.partial(combine_kernel, count=count, starts=starts),
        grid=(width // block,),
        out_shape=jax.ShapeDtypeStruct((rows // steps, steps, width), jnp.bfloat16),
        in_specs=[pl.BlockSpec(chosen.shape, lambda j: (0, 0))]
        + [columns(x.shape[0]) for x in (*pieces, *flat)],
        out_specs=pl.BlockSpec((rows // steps, steps, block), lambda j: (0, 0, j)),
        scratch_shapes=[pltpu.VMEM((rows, block), jnp.float32)],
        compiler_params=pltpu.CompilerParams(vmem_limit_bytes=20 * MIB),
        cost_estimate=BRIEF,
    )(chosen, *pieces, *flat)


def local(
    queries,
    shared_prefix_cache,
    rollout_suffix_cache,
    fresh_key_value,
    rollout_prefix_index,
    rollout_suffix_length,
    rollout_adapter_index,
    output_projection_weight,
    adapter_shrink_weight,
    adapter_expand_weight,
):
    rolls, steps, width = queries.shape
    rows = rolls * steps
    prefix_count = shared_prefix_cache.shape[1]
    resident, rank, out_width = adapter_expand_weight.shape
    holders, sides = lax.axis_size("adapter"), lax.axis_size("tensor")
    block, chips = holders // FOLD, sides // 2
    here, side = lax.axis_index("adapter"), lax.axis_index("tensor")
    chip, core = side // 2, side % 2

    def in_block(shift):
        return [(i, i // block * block + (i + shift) % block) for i in range(holders)]

    cores = [(t, t // 2 * 2 + (t + 1) % 2) for t in range(sides)]

    def over_chips(shift):
        return [(t, (t // 2 + shift) % chips * 2 + t % 2) for t in range(sides)]

    own_shrink = adapter_shrink_weight.reshape(resident * rank, width)
    own_expand = adapter_expand_weight.reshape(resident * rank, out_width)
    far = [(i, (i + block) % holders) for i in range(holders)]

    slots = FOLD * resident * MOST * steps
    per_adapter = MOST * steps
    adapter_row = rollout_adapter_index.reshape(1, rolls)
    lengths, prefixes = rollout_suffix_length[None, :], rollout_prefix_index[None, :]
    here = here.reshape(1).astype(jnp.int32)
    core = core.reshape(1).astype(jnp.int32)
    chip_index = chip.reshape(1).astype(jnp.int32)
    tie = lax.optimization_barrier

    def send_over_chips(away, cuts):
        return [
            lax.ppermute(x, "tensor", over_chips(1 + k // cuts)) for k, x in enumerate(away)
        ]

    def placed(start, own, came, cuts):
        rows = own.shape[0] // cuts
        return [(start, own)] + [(start + k % cuts * rows, x) for k, x in enumerate(came)]

    shrink = lax.ppermute(own_shrink, "adapter", far)
    attended = attend(
        lengths, prefixes, queries, shared_prefix_cache, rollout_suffix_cache, fresh_key_value,
        steps, 0, rolls // BLOCK_ROLLS,
    )
    packed = list(pack(here, adapter_row, [attended], block, slots, steps, resident, holders))
    attended, packed[0] = tie((attended, packed[0]))
    pieces = [packed[0]] + [
        lax.ppermute(packed[d], "adapter", in_block(d)) for d in range(1, block)
    ]
    send = project(1 - core, attended, output_projection_weight, out_width)
    chosen = choose(here, adapter_row, block * slots, steps, resident, holders)
    send, chosen = tie((send, chosen))
    come = lax.ppermute(send, "tensor", cores)
    pieces[0], shrink, moved = tie((pieces[0], shrink, own_expand))
    expand = lax.ppermute(moved, "adapter", far)
    codes = shrink_rows([own_shrink, shrink], pieces, per_adapter, rank)
    codes = codes + lax.ppermute(codes, "tensor", cores)
    brief, attended = tie((codes.astype(jnp.bfloat16), attended))
    keep = project(core, attended, output_projection_weight, out_width)
    own, *away = pair_sums(chip_index, keep, come, 1)
    codes = [brief] + [lax.ppermute(brief, "tensor", over_chips(s)) for s in range(1, chips)]
    codes, away = tie((codes, away))
    came = send_over_chips(away, 1)
    wide = expand_rows([own_expand, expand], codes, per_adapter, rank, block)
    back = [wide[0]] + [
        lax.ppermute(wide[d], "adapter", in_block(block - d)) for d in range(1, block)
    ]
    return combine(chosen, back, placed(0, own, came, 1), steps)


def solution(mesh):
    placed = (
        P("adapter", None, "tensor"),
        P(None, "adapter", None, "tensor"),
        P(None, "adapter", None, "tensor"),
        P(None, "adapter", None, "tensor"),
        P("adapter"),
        P("adapter"),
        P("adapter", None),
        P("tensor", None),
        P("adapter", None, "tensor"),
        P("adapter", None, "tensor"),
    )
    return jax.shard_map(
        local, mesh=mesh, in_specs=placed, out_specs=P("adapter", None, "tensor"), check_vma=False
    )
```

```python
import functools
import math

import jax
import jax.numpy as jnp
from jax import lax
from jax.experimental import pallas as pl
from jax.experimental.pallas import tpu as pltpu
from jax.sharding import PartitionSpec as P

HEAD_SIZE = 128
MOST = 5
FOLD = 2
CUTS = 1
BLOCK_ROLLS = 32
KEY_CHUNK = 512
NEG = float("-inf")
MIB = 1 << 20
BRIEF = pl.CostEstimate(flops=1024, bytes_accessed=1024, transcendentals=0)
LENGTHY = pl.CostEstimate(flops=1 << 36, bytes_accessed=1 << 27, transcendentals=0)
VMEM = pl.BlockSpec(memory_space=pltpu.VMEM)
ANY = pl.BlockSpec(memory_space=pl.ANY)
SMEM = pl.BlockSpec(memory_space=pltpu.SMEM)


def dot_nt(a, b):
    return lax.dot_general(a, b, (((1,), (1,)), ((), ())), preferred_element_type=jnp.float32)


def dot_nn(a, b):
    return jnp.dot(a, b, preferred_element_type=jnp.float32)


def attend_kernel(
    length_hbm, prefix_hbm, q_hbm, kv_hbm, suf_hbm, fr_hbm, o_ref,
    s_ref, m_ref, length_ref, prefix_ref, q_ref, kv_ref, suf_ref, fr_ref, sems,
    *, steps, group, first, blocks
):
    prefix_count, prefix_len = kv_ref.shape[1], kv_ref.shape[2]
    key_heads = kv_ref.shape[3] // HEAD_SIZE
    rolls, suf_len = suf_hbm.shape[1], suf_hbm.shape[2]
    block_rows = BLOCK_ROLLS * steps
    rows = block_rows * group
    last = first + blocks - 1
    suf_rolls = HEAD_SIZE // suf_len
    suf_rows = suf_rolls * steps
    suf_groups = BLOCK_ROLLS // suf_rolls
    window_rolls = HEAD_SIZE // steps
    windows = window_rolls // BLOCK_ROLLS
    factor = HEAD_SIZE ** (-0.5) * math.log2(math.e)
    chunks = prefix_len // KEY_CHUNK
    span = prefix_len

    def row_codes(block):
        shape = (block_rows, rolls)
        mine = block * BLOCK_ROLLS + lax.broadcasted_iota(jnp.int32, shape, 0) // steps
        lane = lax.broadcasted_iota(jnp.int32, shape, 1)
        code = length_ref[...] * prefix_count + prefix_ref[...] % prefix_count
        code = jnp.broadcast_to(code.astype(jnp.float32), shape)
        col = jnp.sum(jnp.where(mine == lane, code, 0.0), axis=1, keepdims=True)
        col = jnp.broadcast_to(col, (block_rows, HEAD_SIZE)).astype(jnp.int32)
        return col // prefix_count, col % prefix_count

    mine = pl.ds(first * BLOCK_ROLLS, blocks * BLOCK_ROLLS)
    loads = []
    for which in range(2):
        loads.append(pltpu.make_async_copy(kv_hbm.at[which], kv_ref.at[which], sems.at[2 * which]))
        loads.append(
            pltpu.make_async_copy(suf_hbm.at[which, mine], suf_ref.at[which], sems.at[2 * which + 1])
        )
    small = [
        pltpu.make_async_copy(src, dst, sems.at[4 + k])
        for k, (src, dst) in enumerate(
            [(q_hbm, q_ref), (fr_hbm, fr_ref), (length_hbm, length_ref), (prefix_hbm, prefix_ref)]
        )
    ]
    for load in [*reversed(small), *loads]:
        load.start()

    def tile_rows(x):
        return jnp.concatenate([x] * group, axis=0)

    def load_q(block, h):
        span = pl.ds(block * BLOCK_ROLLS, BLOCK_ROLLS)
        return [
            q_ref[span, :, pl.ds((h * group + g) * HEAD_SIZE, HEAD_SIZE)].reshape(
                block_rows, HEAD_SIZE
            )
            for g in range(group)
        ]

    def head_lanes(h):
        return pl.ds(h * HEAD_SIZE, HEAD_SIZE)

    def suffix_tile(which, block, i, h):
        start = (block - first) * BLOCK_ROLLS + i * suf_rolls
        tile = suf_ref[which, pl.ds(start, suf_rolls), :, head_lanes(h)]
        return tile.reshape(HEAD_SIZE, HEAD_SIZE)

    def fresh_tile(which, block, h):
        span = pl.ds(block // windows * window_rolls, window_rolls)
        return fr_ref[which, span, :, head_lanes(h)].reshape(HEAD_SIZE, HEAD_SIZE)

    def prefix_tile(which, c, h):
        return jnp.concatenate(
            [
                kv_ref[which, p, pl.ds(c * KEY_CHUNK, KEY_CHUNK), head_lanes(h)]
                for p in range(prefix_count)
            ],
            axis=1,
        )

    def scores(block, h, slot):
        length, local = row_codes(block)
        parts = load_q(block, h)
        stacked = jnp.concatenate(parts, axis=0)
        wide = jnp.concatenate(
            [
                jnp.concatenate(
                    [jnp.where(local == p, x, jnp.zeros_like(x)) for x in parts], axis=0
                )
                for p in range(prefix_count)
            ],
            axis=1,
        )
        shape = (block_rows, HEAD_SIZE)
        row = lax.broadcasted_iota(jnp.int32, shape, 0)
        lane = lax.broadcasted_iota(jnp.int32, shape, 1)
        roll = row // steps
        keep = (roll % suf_rolls == lane // suf_len) & (lane % suf_len < length)
        suf_bias = jnp.where(keep, 0.0, NEG)
        in_window = (block % windows) * BLOCK_ROLLS + roll
        keep = (in_window == lane // steps) & (lane % steps <= row % steps)
        fr_bias = jnp.where(keep, 0.0, NEG)
        suf = []
        for i in range(suf_groups):
            piece = jnp.concatenate(
                [x[i * suf_rows : (i + 1) * suf_rows] for x in parts], axis=0
            )
            suf.append(dot_nt(piece, suffix_tile(0, block, i, h)))
        suf = jnp.concatenate(
            [
                jnp.concatenate([x[g * suf_rows : (g + 1) * suf_rows] for x in suf], axis=0)
                for g in range(group)
            ],
            axis=0,
        ) + tile_rows(suf_bias)
        fr = dot_nt(stacked, fresh_tile(0, block, h)) + tile_rows(fr_bias)
        s_ref[slot, :, pl.ds(span, HEAD_SIZE)] = suf
        s_ref[slot, :, pl.ds(span + HEAD_SIZE, HEAD_SIZE)] = fr
        top = jnp.maximum(suf, fr)
        yield
        for c in range(chunks):
            s = dot_nt(wide, prefix_tile(0, c, h))
            s_ref[slot, :, pl.ds(c * KEY_CHUNK, KEY_CHUNK)] = s
            for j in range(KEY_CHUNK // HEAD_SIZE):
                top = jnp.maximum(top, s[:, j * HEAD_SIZE : (j + 1) * HEAD_SIZE])
            if c == chunks - 1:
                top = jnp.max(top, axis=1, keepdims=True) * factor
                m_ref[slot] = jnp.broadcast_to(top, (rows, HEAD_SIZE))
            yield

    def outputs(block, h, slot):
        top = m_ref[slot]

        def weigh(start, width):
            x = s_ref[slot, :, pl.ds(start, width)]
            wide_top = jnp.concatenate([top] * (width // HEAD_SIZE), axis=1)
            return jnp.exp2(x * factor - wide_top)

        both = weigh(span, 2 * HEAD_SIZE)
        total = both[:, :HEAD_SIZE] + both[:, HEAD_SIZE:]
        both = both.astype(jnp.bfloat16)
        fr = dot_nn(both[:, HEAD_SIZE:], fresh_tile(1, block, h))
        suf = []
        for i in range(suf_groups):
            piece = jnp.concatenate(
                [
                    both[
                        g * block_rows + i * suf_rows : g * block_rows + (i + 1) * suf_rows,
                        :HEAD_SIZE,
                    ]
                    for g in range(group)
                ],
                axis=0,
            )
            suf.append(dot_nn(piece, suffix_tile(1, block, i, h)))
        extra = fr + jnp.concatenate(
            [
                jnp.concatenate([x[g * suf_rows : (g + 1) * suf_rows] for x in suf], axis=0)
                for g in range(group)
            ],
            axis=0,
        )
        yield
        acc = None
        for c in range(chunks):
            p = weigh(c * KEY_CHUNK, KEY_CHUNK)
            for j in range(KEY_CHUNK // HEAD_SIZE):
                total = total + p[:, j * HEAD_SIZE : (j + 1) * HEAD_SIZE]
            part = dot_nn(p.astype(jnp.bfloat16), prefix_tile(1, c, h))
            acc = part if acc is None else acc + part
            if c == chunks - 1:
                _, local = row_codes(block)
                local = tile_rows(local)
                chosen = acc[:, :HEAD_SIZE]
                for q in range(1, prefix_count):
                    chosen = jnp.where(
                        local == q, acc[:, q * HEAD_SIZE : (q + 1) * HEAD_SIZE], chosen
                    )
                weight = 1.0 / jnp.sum(total, axis=1, keepdims=True)
                out = ((chosen + extra) * weight).astype(o_ref.dtype)
                start = pl.multiple_of((block - first) * block_rows, block_rows)
                for g in range(group):
                    o_ref[
                        pl.ds(start, block_rows),
                        pl.ds((h * group + g) * HEAD_SIZE, HEAD_SIZE),
                    ] = out[g * block_rows : (g + 1) * block_rows]
            yield

    def run(*streams):
        for _ in range(chunks + 1):
            for stream in streams:
                next(stream)

    for load in [*reversed(small), *loads[:2]]:
        load.wait()
    run(scores(first, 0, 0))
    for load in loads[2:]:
        load.wait()

    def body(block, carry):
        for h in range(key_heads):
            if h + 1 < key_heads:
                run(scores(block, h + 1, h + 1), outputs(block, h, h))
            elif key_heads > 1:
                following = jnp.minimum(block + 1, last)
                run(scores(following, 0, 0), outputs(block, h, h))
            else:
                run(outputs(block, h, h))
                run(scores(jnp.minimum(block + 1, last), 0, 0))
        return carry

    lax.fori_loop(first, first + blocks, body, 0)


def attend(lengths, prefixes, queries, prefix, suffix, fresh, steps, first, blocks):
    width = queries.shape[-1]
    rows = blocks * BLOCK_ROLLS * steps
    key_heads = prefix.shape[3] // HEAD_SIZE
    group = width // HEAD_SIZE // key_heads
    unit_rows = BLOCK_ROLLS * steps * group
    span = prefix.shape[2] + 2 * HEAD_SIZE
    held = (2, blocks * BLOCK_ROLLS) + suffix.shape[2:]
    return pl.pallas_call(
        functools.partial(attend_kernel, steps=steps, group=group, first=first, blocks=blocks),
        out_shape=jax.ShapeDtypeStruct((rows, width), jnp.bfloat16),
        in_specs=[ANY] * 6,
        out_specs=VMEM,
        scratch_shapes=[
            pltpu.VMEM((key_heads, unit_rows, span), jnp.float32),
            pltpu.VMEM((key_heads, unit_rows, HEAD_SIZE), jnp.float32),
            pltpu.VMEM(lengths.shape, lengths.dtype),
            pltpu.VMEM(prefixes.shape, prefixes.dtype),
            pltpu.VMEM(queries.shape, queries.dtype),
            pltpu.VMEM(prefix.shape, prefix.dtype),
            pltpu.VMEM(held, suffix.dtype),
            pltpu.VMEM(fresh.shape, fresh.dtype),
            pltpu.SemaphoreType.DMA((8,)),
        ],
        compiler_params=pltpu.CompilerParams(vmem_limit_bytes=60 * MIB),
        cost_estimate=LENGTHY,
    )(lengths, prefixes, queries, prefix, suffix, fresh)


def project_kernel(core_ref, a_ref, w_ref, out_ref):
    del core_ref
    out_ref[0] = dot_nn(a_ref[...], w_ref[...]).astype(jnp.bfloat16)


def project(core, attended, weight, out_width):
    rows, width = attended.shape
    count = weight.shape[1] // out_width // 2
    return pl.pallas_call(
        project_kernel,
        grid_spec=pltpu.PrefetchScalarGridSpec(
            num_scalar_prefetch=1,
            grid=(count,),
            in_specs=[
                pl.BlockSpec((rows, width), lambda j, core: (0, 0)),
                pl.BlockSpec((width, out_width), lambda j, core: (0, j * 2 + core[0])),
            ],
            out_specs=pl.BlockSpec((1, rows, out_width), lambda j, core: (j, 0, 0)),
        ),
        out_shape=jax.ShapeDtypeStruct((count, rows, out_width), jnp.bfloat16),
        compiler_params=pltpu.CompilerParams(vmem_limit_bytes=14 * MIB),
        cost_estimate=BRIEF,
    )(core, attended, weight)


def pair_kernel(chip_ref, keep_ref, come_ref, own_ref, *outs, cuts):
    chips = keep_ref.shape[0]
    for shift in range(chips):
        index = (chip_ref[0] + shift) % chips
        pair = keep_ref[index].astype(jnp.float32) + come_ref[index].astype(jnp.float32)
        pair = pair.astype(jnp.bfloat16)
        if shift == 0:
            own_ref[...] = pair
        else:
            for k in range(cuts):
                out = outs[(shift - 1) * cuts + k]
                rows = out.shape[0]
                out[...] = pair[k * rows : (k + 1) * rows]


def pair_sums(chip, keep, come, cuts):
    chips, rows, width = keep.shape
    away = [jax.ShapeDtypeStruct((rows // cuts, width), jnp.bfloat16)] * ((chips - 1) * cuts)
    return pl.pallas_call(
        functools.partial(pair_kernel, cuts=cuts),
        out_shape=[jax.ShapeDtypeStruct((rows, width), jnp.bfloat16)] + away,
        in_specs=[SMEM, VMEM, VMEM],
        out_specs=[VMEM] * (1 + len(away)),
        compiler_params=pltpu.CompilerParams(vmem_limit_bytes=12 * MIB),
        cost_estimate=BRIEF,
    )(chip, keep, come)


def slot_of(row, turn, here, resident, holders):
    block = holders // FOLD
    holder = row // resident
    fold = (here // block - holder // block + FOLD) % FOLD
    place = (holder % block - here % block + block) % block
    return ((place * FOLD + fold) * resident + row % resident) * MOST + turn


def row_slots(row_ref, here, resident, holders):
    row = row_ref[...]
    shape = (row.shape[1], row.shape[1])
    across = jnp.broadcast_to(row, shape)
    down, lane = lax.broadcasted_iota(jnp.int32, shape, 0), lax.broadcasted_iota(jnp.int32, shape, 1)
    values = across.astype(jnp.float32)
    col = jnp.sum(jnp.where(down == lane, values, 0.0), axis=1, keepdims=True)
    same = jnp.broadcast_to(col, shape) == values
    turn_row = jnp.sum(jnp.where(same & (down < lane), 1.0, 0.0), axis=0, keepdims=True)
    turn_col = jnp.sum(jnp.where(same & (lane < down), 1.0, 0.0), axis=1, keepdims=True)
    place_row = slot_of(row, turn_row.astype(jnp.int32), here, resident, holders)
    place_col = slot_of(
        jnp.broadcast_to(col, shape).astype(jnp.int32),
        jnp.broadcast_to(turn_col, shape).astype(jnp.int32),
        here,
        resident,
        holders,
    )
    return place_row, place_col[:, :1]


def pack_kernel(here_ref, row_ref, *refs, steps, resident, holders, count):
    parts, outs = refs[:-count], refs[-count:]
    slots, rolls = outs[0].shape[0], row_ref.shape[1]
    place, _ = row_slots(row_ref, here_ref[0], resident, holders)
    for d, out in enumerate(outs):
        shape = (slots, rolls)
        slot = (d * slots + lax.broadcasted_iota(jnp.int32, shape, 0)) // steps
        picked = jnp.where(slot == jnp.broadcast_to(place, shape), 1.0, 0.0).astype(jnp.bfloat16)
        total, start = None, 0
        for part in parts:
            rows = part.shape[0]
            shape = (rolls, rows)
            spread = lax.broadcasted_iota(jnp.int32, shape, 0) == (
                start + lax.broadcasted_iota(jnp.int32, shape, 1)
            ) // steps
            chosen = dot_nn(picked, jnp.where(spread, 1.0, 0.0).astype(jnp.bfloat16))
            shape = (slots, rows)
            step = lax.broadcasted_iota(jnp.int32, shape, 0) % steps
            aligned = step == (start + lax.broadcasted_iota(jnp.int32, shape, 1)) % steps
            chosen = jnp.where(aligned, chosen, 0.0).astype(jnp.bfloat16)
            term = dot_nn(chosen, part[...])
            total = term if total is None else total + term
            start += rows
        out[...] = total.astype(jnp.bfloat16)


def pack(here, adapter_row, parts, count, slots, steps, resident, holders):
    width = parts[0].shape[1]
    return pl.pallas_call(
        functools.partial(
            pack_kernel, steps=steps, resident=resident, holders=holders, count=count
        ),
        out_shape=[jax.ShapeDtypeStruct((slots, width), jnp.bfloat16)] * count,
        in_specs=[SMEM] + [VMEM] * (1 + len(parts)),
        out_specs=[VMEM] * count,
        compiler_params=pltpu.CompilerParams(vmem_limit_bytes=12 * MIB),
        cost_estimate=BRIEF,
    )(here, adapter_row, *parts)


def adapter_mask(rows, per_adapter, rank, tile):
    lane = lax.broadcasted_iota(jnp.int32, (rows, HEAD_SIZE), 1) + tile * HEAD_SIZE
    row = lax.broadcasted_iota(jnp.int32, (rows, HEAD_SIZE), 0)
    return lane // rank == row // per_adapter


def shrink_kernel(*refs, per_adapter, rank, count):
    weights, pieces, out = refs[:FOLD], refs[FOLD : FOLD + count], refs[-1]
    rows = pieces[0].shape[0] // FOLD
    found = []
    for k in range(FOLD):
        span = pl.ds(k * rows, rows)
        every = dot_nt(
            jnp.concatenate([p[span, :] for p in pieces], axis=0),
            weights[k][...],
        )
        for d in range(count):
            total = None
            for tile in range(every.shape[1] // HEAD_SIZE):
                x = every[d * rows : (d + 1) * rows, tile * HEAD_SIZE : (tile + 1) * HEAD_SIZE]
                x = jnp.where(adapter_mask(rows, per_adapter, rank, tile), x, 0.0)
                total = x if total is None else total + x
            summed = total
            for turn in range(1, HEAD_SIZE // rank):
                summed = summed + pltpu.roll(total, turn * rank, axis=1)
            found.append(summed)
    lane = lax.broadcasted_iota(jnp.int32, (rows, HEAD_SIZE), 1)
    for d in range(count):
        both = jnp.where(lane < rank, found[d], found[count + d])
        out[pl.ds(d * rows, rows), :] = both


def shrink_rows(weights, pieces, per_adapter, rank):
    count = len(pieces)
    rows, width = pieces[0].shape
    return pl.pallas_call(
        functools.partial(shrink_kernel, per_adapter=per_adapter, rank=rank, count=count),
        out_shape=jax.ShapeDtypeStruct((count * rows // FOLD, HEAD_SIZE), jnp.float32),
        in_specs=[VMEM] * (FOLD + count),
        out_specs=VMEM,
        compiler_params=pltpu.CompilerParams(vmem_limit_bytes=8 * MIB),
        cost_estimate=LENGTHY,
    )(*weights, *pieces)


def expand_kernel(*refs, per_adapter, rank, count, terms):
    weights, sums, outs = refs[:FOLD], refs[FOLD : FOLD + terms], refs[FOLD + terms :]
    depth = weights[0].shape[0]
    rows = outs[0].shape[0] // FOLD
    for k in range(FOLD):
        spread = []
        for d in range(count):
            span = pl.ds(d * rows, rows)
            code = sums[0][span, :].astype(jnp.float32)
            for other in sums[1:]:
                code = code + other[span, :].astype(jnp.float32)
            lane = lax.broadcasted_iota(jnp.int32, (rows, HEAD_SIZE), 1)
            turned = pltpu.roll(code, rank, axis=1)
            code = jnp.where((lane < rank) == (k == 0), code, turned)
            spread.append(
                jnp.concatenate(
                    [
                        jnp.where(adapter_mask(rows, per_adapter, rank, tile), code, 0.0)
                        for tile in range(depth // HEAD_SIZE)
                    ],
                    axis=1,
                ).astype(jnp.bfloat16)
            )
        wide = dot_nn(jnp.concatenate(spread, axis=0), weights[k][...])
        wide = wide.astype(jnp.bfloat16)
        for d in range(count):
            outs[d][pl.ds(k * rows, rows), :] = wide[d * rows : (d + 1) * rows]


def expand_rows(weights, sums, per_adapter, rank, count):
    rows = sums[0].shape[0] // count * FOLD
    width = weights[0].shape[1]
    return pl.pallas_call(
        functools.partial(
            expand_kernel, per_adapter=per_adapter, rank=rank, count=count, terms=len(sums)
        ),
        out_shape=[jax.ShapeDtypeStruct((rows, width), jnp.bfloat16)] * count,
        in_specs=[VMEM] * (FOLD + len(sums)),
        out_specs=[VMEM] * count,
        compiler_params=pltpu.CompilerParams(vmem_limit_bytes=8 * MIB),
        cost_estimate=LENGTHY,
    )(*weights, *sums)


def choose_kernel(here_ref, row_ref, chosen_ref, *, steps, resident, holders):
    rows, total = chosen_ref.shape
    rolls = row_ref.shape[1]
    _, place = row_slots(row_ref, here_ref[0], resident, holders)
    shape = (rolls, total)
    slot = lax.broadcasted_iota(jnp.int32, shape, 1) // steps
    picked = jnp.where(slot == jnp.broadcast_to(place, shape), 1.0, 0.0).astype(jnp.bfloat16)
    shape = (rows, rolls)
    roll = lax.broadcasted_iota(jnp.int32, shape, 0) // steps
    spread = roll == lax.broadcasted_iota(jnp.int32, shape, 1)
    chosen = dot_nn(jnp.where(spread, 1.0, 0.0).astype(jnp.bfloat16), picked)
    shape = (rows, total)
    step = lax.broadcasted_iota(jnp.int32, shape, 0) % steps
    aligned = step == lax.broadcasted_iota(jnp.int32, shape, 1) % steps
    chosen_ref[...] = jnp.where(aligned, chosen, 0.0).astype(jnp.bfloat16)


def choose(here, adapter_row, total, steps, resident, holders):
    rows = adapter_row.shape[1] * steps
    return pl.pallas_call(
        functools.partial(choose_kernel, steps=steps, resident=resident, holders=holders),
        out_shape=jax.ShapeDtypeStruct((rows, total), jnp.bfloat16),
        in_specs=[SMEM, VMEM],
        out_specs=VMEM,
        compiler_params=pltpu.CompilerParams(vmem_limit_bytes=20 * MIB),
        cost_estimate=BRIEF,
    )(here, adapter_row)


def combine_kernel(chosen_ref, *refs, count, starts):
    pieces, sums, out, total_ref = refs[:count], refs[count:-2], refs[-2], refs[-1]
    stacked = jnp.concatenate([x[...] for x in pieces], axis=0)
    total_ref[...] = dot_nn(chosen_ref[...], stacked)
    for start, x in zip(starts, sums):
        span = pl.ds(start, x.shape[0])
        total_ref[span, :] += x[...].astype(jnp.float32)
    out[...] = total_ref[...].reshape(out.shape).astype(jnp.bfloat16)


def combine(chosen, pieces, sums, steps):
    width = pieces[0].shape[1]
    count = len(pieces)
    starts, flat = zip(*sums)
    rows = chosen.shape[0]
    block = min(width, 2 * HEAD_SIZE)

    def columns(x):
        return pl.BlockSpec((x, block), lambda j: (0, j))

    return pl.pallas_call(
        functools.partial(combine_kernel, count=count, starts=starts),
        grid=(width // block,),
        out_shape=jax.ShapeDtypeStruct((rows // steps, steps, width), jnp.bfloat16),
        in_specs=[pl.BlockSpec(chosen.shape, lambda j: (0, 0))]
        + [columns(x.shape[0]) for x in (*pieces, *flat)],
        out_specs=pl.BlockSpec((rows // steps, steps, block), lambda j: (0, 0, j)),
        scratch_shapes=[pltpu.VMEM((rows, block), jnp.float32)],
        compiler_params=pltpu.CompilerParams(vmem_limit_bytes=20 * MIB),
        cost_estimate=BRIEF,
    )(chosen, *pieces, *flat)


def local(
    queries,
    shared_prefix_cache,
    rollout_suffix_cache,
    fresh_key_value,
    rollout_prefix_index,
    rollout_suffix_length,
    rollout_adapter_index,
    output_projection_weight,
    adapter_shrink_weight,
    adapter_expand_weight,
):
    rolls, steps, width = queries.shape
    rows = rolls * steps
    prefix_count = shared_prefix_cache.shape[1]
    resident, rank, out_width = adapter_expand_weight.shape
    holders, sides = lax.axis_size("adapter"), lax.axis_size("tensor")
    block, chips = holders // FOLD, sides // 2
    here, side = lax.axis_index("adapter"), lax.axis_index("tensor")
    chip, core = side // 2, side % 2

    def in_block(shift):
        return [(i, i // block * block + (i + shift) % block) for i in range(holders)]

    cores = [(t, t // 2 * 2 + (t + 1) % 2) for t in range(sides)]

    def over_chips(shift):
        return [(t, (t // 2 + shift) % chips * 2 + t % 2) for t in range(sides)]

    own_shrink = adapter_shrink_weight.reshape(resident * rank, width)
    own_expand = adapter_expand_weight.reshape(resident * rank, out_width)
    far = [(i, (i + block) % holders) for i in range(holders)]

    slots = FOLD * resident * MOST * steps
    per_adapter = MOST * steps
    adapter_row = rollout_adapter_index.reshape(1, rolls)
    lengths, prefixes = rollout_suffix_length[None, :], rollout_prefix_index[None, :]
    here = here.reshape(1).astype(jnp.int32)
    core = core.reshape(1).astype(jnp.int32)
    chip_index = chip.reshape(1).astype(jnp.int32)
    tie = lax.optimization_barrier

    def send_over_chips(away, cuts):
        return [
            lax.ppermute(x, "tensor", over_chips(1 + k // cuts)) for k, x in enumerate(away)
        ]

    def placed(start, own, came, cuts):
        rows = own.shape[0] // cuts
        return [(start, own)] + [(start + k % cuts * rows, x) for k, x in enumerate(came)]

    shrink = lax.ppermute(own_shrink, "adapter", far)
    attended = attend(
        lengths, prefixes, queries, shared_prefix_cache, rollout_suffix_cache, fresh_key_value,
        steps, 0, rolls // BLOCK_ROLLS,
    )
    packed = list(pack(here, adapter_row, [attended], block, slots, steps, resident, holders))
    attended, packed[0] = tie((attended, packed[0]))
    pieces = [packed[0]] + [
        lax.ppermute(packed[d], "adapter", in_block(d)) for d in range(1, block)
    ]
    send = project(1 - core, attended, output_projection_weight, out_width)
    chosen = choose(here, adapter_row, block * slots, steps, resident, holders)
    send, chosen = tie((send, chosen))
    come = lax.ppermute(send, "tensor", cores)
    pieces[0], shrink, moved = tie((pieces[0], shrink, own_expand))
    expand = lax.ppermute(moved, "adapter", far)
    codes = shrink_rows([own_shrink, shrink], pieces, per_adapter, rank)
    codes = codes + lax.ppermute(codes, "tensor", cores)
    brief, attended = tie((codes.astype(jnp.bfloat16), attended))
    keep = project(core, attended, output_projection_weight, out_width)
    own, *away = pair_sums(chip_index, keep, come, 1)
    codes = [brief] + [lax.ppermute(brief, "tensor", over_chips(s)) for s in range(1, chips)]
    codes, away = tie((codes, away))
    came = send_over_chips(away, 1)
    wide = expand_rows([own_expand, expand], codes, per_adapter, rank, block)
    back = [wide[0]] + [
        lax.ppermute(wide[d], "adapter", in_block(block - d)) for d in range(1, block)
    ]
    return combine(chosen, back, placed(0, own, came, 1), steps)


def solution(mesh):
    placed = (
        P("adapter", None, "tensor"),
        P(None, "adapter", None, "tensor"),
        P(None, "adapter", None, "tensor"),
        P(None, "adapter", None, "tensor"),
        P("adapter"),
        P("adapter"),
        P("adapter", None),
        P("tensor", None),
        P("adapter", None, "tensor"),
        P("adapter", None, "tensor"),
    )
    return jax.shard_map(
        local, mesh=mesh, in_specs=placed, out_specs=P("adapter", None, "tensor"), check_vma=False
    )
```

```python
import functools
import math

import jax
import jax.numpy as jnp
from jax import lax
from jax.experimental import pallas as pl
from jax.experimental.pallas import tpu as pltpu
from jax.sharding import PartitionSpec as P

HEAD_SIZE = 128
MOST = 5
FOLD = 2
CUTS = 1
BLOCK_ROLLS = 32
KEY_CHUNK = 512
NEG = float("-inf")
MIB = 1 << 20
BRIEF = pl.CostEstimate(flops=1024, bytes_accessed=1024, transcendentals=0)
LENGTHY = pl.CostEstimate(flops=1 << 36, bytes_accessed=1 << 27, transcendentals=0)
VMEM = pl.BlockSpec(memory_space=pltpu.VMEM)
ANY = pl.BlockSpec(memory_space=pl.ANY)
SMEM = pl.BlockSpec(memory_space=pltpu.SMEM)


def dot_nt(a, b):
    return lax.dot_general(a, b, (((1,), (1,)), ((), ())), preferred_element_type=jnp.float32)


def dot_nn(a, b):
    return jnp.dot(a, b, preferred_element_type=jnp.float32)


def attend_kernel(
    length_hbm, prefix_hbm, q_hbm, kv_hbm, suf_hbm, fr_hbm, o_ref,
    s_ref, m_ref, length_ref, prefix_ref, q_ref, kv_ref, suf_ref, fr_ref, sems,
    *, steps, group, first, blocks
):
    prefix_count, prefix_len = kv_ref.shape[1], kv_ref.shape[2]
    key_heads = kv_ref.shape[3] // HEAD_SIZE
    rolls, suf_len = suf_hbm.shape[1], suf_hbm.shape[2]
    block_rows = BLOCK_ROLLS * steps
    rows = block_rows * group
    last = first + blocks - 1
    suf_rolls = HEAD_SIZE // suf_len
    suf_rows = suf_rolls * steps
    suf_groups = BLOCK_ROLLS // suf_rolls
    window_rolls = HEAD_SIZE // steps
    windows = window_rolls // BLOCK_ROLLS
    factor = HEAD_SIZE ** (-0.5) * math.log2(math.e)
    chunks = prefix_len // KEY_CHUNK
    span = prefix_len

    def row_codes(block):
        shape = (block_rows, rolls)
        mine = block * BLOCK_ROLLS + lax.broadcasted_iota(jnp.int32, shape, 0) // steps
        lane = lax.broadcasted_iota(jnp.int32, shape, 1)
        code = length_ref[...] * prefix_count + prefix_ref[...] % prefix_count
        code = jnp.broadcast_to(code.astype(jnp.float32), shape)
        col = jnp.sum(jnp.where(mine == lane, code, 0.0), axis=1, keepdims=True)
        col = jnp.broadcast_to(col, (block_rows, HEAD_SIZE)).astype(jnp.int32)
        return col // prefix_count, col % prefix_count

    mine = pl.ds(first * BLOCK_ROLLS, blocks * BLOCK_ROLLS)
    loads = []
    for which in range(2):
        loads.append(pltpu.make_async_copy(kv_hbm.at[which], kv_ref.at[which], sems.at[2 * which]))
        loads.append(
            pltpu.make_async_copy(suf_hbm.at[which, mine], suf_ref.at[which], sems.at[2 * which + 1])
        )
    small = [
        pltpu.make_async_copy(src, dst, sems.at[4 + k])
        for k, (src, dst) in enumerate(
            [(q_hbm, q_ref), (fr_hbm, fr_ref), (length_hbm, length_ref), (prefix_hbm, prefix_ref)]
        )
    ]
    for load in [*reversed(small), *loads]:
        load.start()

    def tile_rows(x):
        return jnp.concatenate([x] * group, axis=0)

    def load_q(block, h):
        span = pl.ds(block * BLOCK_ROLLS, BLOCK_ROLLS)
        return [
            q_ref[span, :, pl.ds((h * group + g) * HEAD_SIZE, HEAD_SIZE)].reshape(
                block_rows, HEAD_SIZE
            )
            for g in range(group)
        ]

    def head_lanes(h):
        return pl.ds(h * HEAD_SIZE, HEAD_SIZE)

    def suffix_tile(which, block, i, h):
        start = (block - first) * BLOCK_ROLLS + i * suf_rolls
        tile = suf_ref[which, pl.ds(start, suf_rolls), :, head_lanes(h)]
        return tile.reshape(HEAD_SIZE, HEAD_SIZE)

    def fresh_tile(which, block, h):
        span = pl.ds(block // windows * window_rolls, window_rolls)
        return fr_ref[which, span, :, head_lanes(h)].reshape(HEAD_SIZE, HEAD_SIZE)

    def prefix_tile(which, c, h):
        return jnp.concatenate(
            [
                kv_ref[which, p, pl.ds(c * KEY_CHUNK, KEY_CHUNK), head_lanes(h)]
                for p in range(prefix_count)
            ],
            axis=1,
        )

    def scores(block, h, slot):
        length, local = row_codes(block)
        parts = load_q(block, h)
        stacked = jnp.concatenate(parts, axis=0)
        wide = jnp.concatenate(
            [
                jnp.concatenate(
                    [jnp.where(local == p, x, jnp.zeros_like(x)) for x in parts], axis=0
                )
                for p in range(prefix_count)
            ],
            axis=1,
        )
        shape = (block_rows, HEAD_SIZE)
        row = lax.broadcasted_iota(jnp.int32, shape, 0)
        lane = lax.broadcasted_iota(jnp.int32, shape, 1)
        roll = row // steps
        keep = (roll % suf_rolls == lane // suf_len) & (lane % suf_len < length)
        suf_bias = jnp.where(keep, 0.0, NEG)
        in_window = (block % windows) * BLOCK_ROLLS + roll
        keep = (in_window == lane // steps) & (lane % steps <= row % steps)
        fr_bias = jnp.where(keep, 0.0, NEG)
        suf = []
        for i in range(suf_groups):
            piece = jnp.concatenate(
                [x[i * suf_rows : (i + 1) * suf_rows] for x in parts], axis=0
            )
            suf.append(dot_nt(piece, suffix_tile(0, block, i, h)))
        suf = jnp.concatenate(
            [
                jnp.concatenate([x[g * suf_rows : (g + 1) * suf_rows] for x in suf], axis=0)
                for g in range(group)
            ],
            axis=0,
        ) + tile_rows(suf_bias)
        fr = dot_nt(stacked, fresh_tile(0, block, h)) + tile_rows(fr_bias)
        s_ref[slot, :, pl.ds(span, HEAD_SIZE)] = suf
        s_ref[slot, :, pl.ds(span + HEAD_SIZE, HEAD_SIZE)] = fr
        top = jnp.maximum(suf, fr)
        yield
        for c in range(chunks):
            s = dot_nt(wide, prefix_tile(0, c, h))
            s_ref[slot, :, pl.ds(c * KEY_CHUNK, KEY_CHUNK)] = s
            for j in range(KEY_CHUNK // HEAD_SIZE):
                top = jnp.maximum(top, s[:, j * HEAD_SIZE : (j + 1) * HEAD_SIZE])
            if c == chunks - 1:
                top = jnp.max(top, axis=1, keepdims=True) * factor
                m_ref[slot] = jnp.broadcast_to(top, (rows, HEAD_SIZE))
            yield

    def outputs(block, h, slot):
        top = m_ref[slot]

        def weigh(start, width):
            x = s_ref[slot, :, pl.ds(start, width)]
            wide_top = jnp.concatenate([top] * (width // HEAD_SIZE), axis=1)
            return jnp.exp2(x * factor - wide_top)

        both = weigh(span, 2 * HEAD_SIZE)
        total = both[:, :HEAD_SIZE] + both[:, HEAD_SIZE:]
        both = both.astype(jnp.bfloat16)
        fr = dot_nn(both[:, HEAD_SIZE:], fresh_tile(1, block, h))
        suf = []
        for i in range(suf_groups):
            piece = jnp.concatenate(
                [
                    both[
                        g * block_rows + i * suf_rows : g * block_rows + (i + 1) * suf_rows,
                        :HEAD_SIZE,
                    ]
                    for g in range(group)
                ],
                axis=0,
            )
            suf.append(dot_nn(piece, suffix_tile(1, block, i, h)))
        extra = fr + jnp.concatenate(
            [
                jnp.concatenate([x[g * suf_rows : (g + 1) * suf_rows] for x in suf], axis=0)
                for g in range(group)
            ],
            axis=0,
        )
        yield
        acc = None
        for c in range(chunks):
            p = weigh(c * KEY_CHUNK, KEY_CHUNK)
            for j in range(KEY_CHUNK // HEAD_SIZE):
                total = total + p[:, j * HEAD_SIZE : (j + 1) * HEAD_SIZE]
            part = dot_nn(p.astype(jnp.bfloat16), prefix_tile(1, c, h))
            acc = part if acc is None else acc + part
            if c == chunks - 1:
                _, local = row_codes(block)
                local = tile_rows(local)
                chosen = acc[:, :HEAD_SIZE]
                for q in range(1, prefix_count):
                    chosen = jnp.where(
                        local == q, acc[:, q * HEAD_SIZE : (q + 1) * HEAD_SIZE], chosen
                    )
                weight = 1.0 / jnp.sum(total, axis=1, keepdims=True)
                out = ((chosen + extra) * weight).astype(o_ref.dtype)
                start = pl.multiple_of((block - first) * block_rows, block_rows)
                for g in range(group):
                    o_ref[
                        pl.ds(start, block_rows),
                        pl.ds((h * group + g) * HEAD_SIZE, HEAD_SIZE),
                    ] = out[g * block_rows : (g + 1) * block_rows]
            yield

    def run(*streams):
        for _ in range(chunks + 1):
            for stream in streams:
                next(stream)

    for load in [*reversed(small), *loads[:2]]:
        load.wait()
    run(scores(first, 0, 0))
    for load in loads[2:]:
        load.wait()

    def body(block, carry):
        for h in range(key_heads):
            if h + 1 < key_heads:
                run(scores(block, h + 1, h + 1), outputs(block, h, h))
            elif key_heads > 1:
                following = jnp.minimum(block + 1, last)
                run(scores(following, 0, 0), outputs(block, h, h))
            else:
                run(outputs(block, h, h))
                run(scores(jnp.minimum(block + 1, last), 0, 0))
        return carry

    lax.fori_loop(first, first + blocks, body, 0)


def attend(lengths, prefixes, queries, prefix, suffix, fresh, steps, first, blocks):
    width = queries.shape[-1]
    rows = blocks * BLOCK_ROLLS * steps
    key_heads = prefix.shape[3] // HEAD_SIZE
    group = width // HEAD_SIZE // key_heads
    unit_rows = BLOCK_ROLLS * steps * group
    span = prefix.shape[2] + 2 * HEAD_SIZE
    held = (2, blocks * BLOCK_ROLLS) + suffix.shape[2:]
    return pl.pallas_call(
        functools.partial(attend_kernel, steps=steps, group=group, first=first, blocks=blocks),
        out_shape=jax.ShapeDtypeStruct((rows, width), jnp.bfloat16),
        in_specs=[ANY] * 6,
        out_specs=VMEM,
        scratch_shapes=[
            pltpu.VMEM((key_heads, unit_rows, span), jnp.float32),
            pltpu.VMEM((key_heads, unit_rows, HEAD_SIZE), jnp.float32),
            pltpu.VMEM(lengths.shape, lengths.dtype),
            pltpu.VMEM(prefixes.shape, prefixes.dtype),
            pltpu.VMEM(queries.shape, queries.dtype),
            pltpu.VMEM(prefix.shape, prefix.dtype),
            pltpu.VMEM(held, suffix.dtype),
            pltpu.VMEM(fresh.shape, fresh.dtype),
            pltpu.SemaphoreType.DMA((8,)),
        ],
        compiler_params=pltpu.CompilerParams(vmem_limit_bytes=52 * MIB),
        cost_estimate=LENGTHY,
    )(lengths, prefixes, queries, prefix, suffix, fresh)


def project_kernel(core_ref, a_ref, w_ref, out_ref):
    del core_ref
    out_ref[0] = dot_nn(a_ref[...], w_ref[...]).astype(jnp.bfloat16)


def project(core, attended, weight, out_width):
    rows, width = attended.shape
    count = weight.shape[1] // out_width // 2
    return pl.pallas_call(
        project_kernel,
        grid_spec=pltpu.PrefetchScalarGridSpec(
            num_scalar_prefetch=1,
            grid=(count,),
            in_specs=[
                pl.BlockSpec((rows, width), lambda j, core: (0, 0)),
                pl.BlockSpec((width, out_width), lambda j, core: (0, j * 2 + core[0])),
            ],
            out_specs=pl.BlockSpec((1, rows, out_width), lambda j, core: (j, 0, 0)),
        ),
        out_shape=jax.ShapeDtypeStruct((count, rows, out_width), jnp.bfloat16),
        compiler_params=pltpu.CompilerParams(vmem_limit_bytes=14 * MIB),
        cost_estimate=BRIEF,
    )(core, attended, weight)


def pair_kernel(chip_ref, keep_ref, come_ref, own_ref, *outs, cuts):
    chips = keep_ref.shape[0]
    for shift in range(chips):
        index = (chip_ref[0] + shift) % chips
        pair = keep_ref[index].astype(jnp.float32) + come_ref[index].astype(jnp.float32)
        pair = pair.astype(jnp.bfloat16)
        if shift == 0:
            own_ref[...] = pair
        else:
            for k in range(cuts):
                out = outs[(shift - 1) * cuts + k]
                rows = out.shape[0]
                out[...] = pair[k * rows : (k + 1) * rows]


def pair_sums(chip, keep, come, cuts):
    chips, rows, width = keep.shape
    away = [jax.ShapeDtypeStruct((rows // cuts, width), jnp.bfloat16)] * ((chips - 1) * cuts)
    return pl.pallas_call(
        functools.partial(pair_kernel, cuts=cuts),
        out_shape=[jax.ShapeDtypeStruct((rows, width), jnp.bfloat16)] + away,
        in_specs=[SMEM, VMEM, VMEM],
        out_specs=[VMEM] * (1 + len(away)),
        compiler_params=pltpu.CompilerParams(vmem_limit_bytes=12 * MIB),
        cost_estimate=BRIEF,
    )(chip, keep, come)


def slot_of(row, turn, here, resident, holders):
    block = holders // FOLD
    holder = row // resident
    fold = (here // block - holder // block + FOLD) % FOLD
    place = (holder % block - here % block + block) % block
    return ((place * FOLD + fold) * resident + row % resident) * MOST + turn


def row_slots(row_ref, here, resident, holders):
    row = row_ref[...]
    shape = (row.shape[1], row.shape[1])
    across = jnp.broadcast_to(row, shape)
    down, lane = lax.broadcasted_iota(jnp.int32, shape, 0), lax.broadcasted_iota(jnp.int32, shape, 1)
    values = across.astype(jnp.float32)
    col = jnp.sum(jnp.where(down == lane, values, 0.0), axis=1, keepdims=True)
    same = jnp.broadcast_to(col, shape) == values
    turn_row = jnp.sum(jnp.where(same & (down < lane), 1.0, 0.0), axis=0, keepdims=True)
    turn_col = jnp.sum(jnp.where(same & (lane < down), 1.0, 0.0), axis=1, keepdims=True)
    place_row = slot_of(row, turn_row.astype(jnp.int32), here, resident, holders)
    place_col = slot_of(
        jnp.broadcast_to(col, shape).astype(jnp.int32),
        jnp.broadcast_to(turn_col, shape).astype(jnp.int32),
        here,
        resident,
        holders,
    )
    return place_row, place_col[:, :1]


def pack_kernel(here_ref, row_ref, *refs, steps, resident, holders, count):
    parts, outs = refs[:-count], refs[-count:]
    slots, rolls = outs[0].shape[0], row_ref.shape[1]
    place, _ = row_slots(row_ref, here_ref[0], resident, holders)
    for d, out in enumerate(outs):
        shape = (slots, rolls)
        slot = (d * slots + lax.broadcasted_iota(jnp.int32, shape, 0)) // steps
        picked = jnp.where(slot == jnp.broadcast_to(place, shape), 1.0, 0.0).astype(jnp.bfloat16)
        total, start = None, 0
        for part in parts:
            rows = part.shape[0]
            shape = (rolls, rows)
            spread = lax.broadcasted_iota(jnp.int32, shape, 0) == (
                start + lax.broadcasted_iota(jnp.int32, shape, 1)
            ) // steps
            chosen = dot_nn(picked, jnp.where(spread, 1.0, 0.0).astype(jnp.bfloat16))
            shape = (slots, rows)
            step = lax.broadcasted_iota(jnp.int32, shape, 0) % steps
            aligned = step == (start + lax.broadcasted_iota(jnp.int32, shape, 1)) % steps
            chosen = jnp.where(aligned, chosen, 0.0).astype(jnp.bfloat16)
            term = dot_nn(chosen, part[...])
            total = term if total is None else total + term
            start += rows
        out[...] = total.astype(jnp.bfloat16)


def pack(here, adapter_row, parts, count, slots, steps, resident, holders):
    width = parts[0].shape[1]
    return pl.pallas_call(
        functools.partial(
            pack_kernel, steps=steps, resident=resident, holders=holders, count=count
        ),
        out_shape=[jax.ShapeDtypeStruct((slots, width), jnp.bfloat16)] * count,
        in_specs=[SMEM] + [VMEM] * (1 + len(parts)),
        out_specs=[VMEM] * count,
        compiler_params=pltpu.CompilerParams(vmem_limit_bytes=12 * MIB),
        cost_estimate=BRIEF,
    )(here, adapter_row, *parts)


def adapter_mask(rows, per_adapter, rank, tile):
    lane = lax.broadcasted_iota(jnp.int32, (rows, HEAD_SIZE), 1) + tile * HEAD_SIZE
    row = lax.broadcasted_iota(jnp.int32, (rows, HEAD_SIZE), 0)
    return lane // rank == row // per_adapter


def shrink_kernel(*refs, per_adapter, rank, count):
    weights, pieces, out = refs[:FOLD], refs[FOLD : FOLD + count], refs[-1]
    rows = pieces[0].shape[0] // FOLD
    found = []
    for k in range(FOLD):
        span = pl.ds(k * rows, rows)
        every = dot_nt(
            jnp.concatenate([p[span, :] for p in pieces], axis=0),
            weights[k][...],
        )
        for d in range(count):
            total = None
            for tile in range(every.shape[1] // HEAD_SIZE):
                x = every[d * rows : (d + 1) * rows, tile * HEAD_SIZE : (tile + 1) * HEAD_SIZE]
                x = jnp.where(adapter_mask(rows, per_adapter, rank, tile), x, 0.0)
                total = x if total is None else total + x
            summed = total
            for turn in range(1, HEAD_SIZE // rank):
                summed = summed + pltpu.roll(total, turn * rank, axis=1)
            found.append(summed)
    lane = lax.broadcasted_iota(jnp.int32, (rows, HEAD_SIZE), 1)
    for d in range(count):
        both = jnp.where(lane < rank, found[d], found[count + d])
        out[pl.ds(d * rows, rows), :] = both


def shrink_rows(weights, pieces, per_adapter, rank):
    count = len(pieces)
    rows, width = pieces[0].shape
    return pl.pallas_call(
        functools.partial(shrink_kernel, per_adapter=per_adapter, rank=rank, count=count),
        out_shape=jax.ShapeDtypeStruct((count * rows // FOLD, HEAD_SIZE), jnp.float32),
        in_specs=[VMEM] * (FOLD + count),
        out_specs=VMEM,
        compiler_params=pltpu.CompilerParams(vmem_limit_bytes=8 * MIB),
        cost_estimate=LENGTHY,
    )(*weights, *pieces)


def expand_kernel(*refs, per_adapter, rank, count, terms):
    weights, sums, outs = refs[:FOLD], refs[FOLD : FOLD + terms], refs[FOLD + terms :]
    depth = weights[0].shape[0]
    rows = outs[0].shape[0] // FOLD
    for k in range(FOLD):
        spread = []
        for d in range(count):
            span = pl.ds(d * rows, rows)
            code = sums[0][span, :].astype(jnp.float32)
            for other in sums[1:]:
                code = code + other[span, :].astype(jnp.float32)
            lane = lax.broadcasted_iota(jnp.int32, (rows, HEAD_SIZE), 1)
            turned = pltpu.roll(code, rank, axis=1)
            code = jnp.where((lane < rank) == (k == 0), code, turned)
            spread.append(
                jnp.concatenate(
                    [
                        jnp.where(adapter_mask(rows, per_adapter, rank, tile), code, 0.0)
                        for tile in range(depth // HEAD_SIZE)
                    ],
                    axis=1,
                ).astype(jnp.bfloat16)
            )
        wide = dot_nn(jnp.concatenate(spread, axis=0), weights[k][...])
        wide = wide.astype(jnp.bfloat16)
        for d in range(count):
            outs[d][pl.ds(k * rows, rows), :] = wide[d * rows : (d + 1) * rows]


def expand_rows(weights, sums, per_adapter, rank, count):
    rows = sums[0].shape[0] // count * FOLD
    width = weights[0].shape[1]
    return pl.pallas_call(
        functools.partial(
            expand_kernel, per_adapter=per_adapter, rank=rank, count=count, terms=len(sums)
        ),
        out_shape=[jax.ShapeDtypeStruct((rows, width), jnp.bfloat16)] * count,
        in_specs=[VMEM] * (FOLD + len(sums)),
        out_specs=[VMEM] * count,
        compiler_params=pltpu.CompilerParams(vmem_limit_bytes=8 * MIB),
        cost_estimate=LENGTHY,
    )(*weights, *sums)


def choose_kernel(here_ref, row_ref, chosen_ref, *, steps, resident, holders):
    rows, total = chosen_ref.shape
    rolls = row_ref.shape[1]
    _, place = row_slots(row_ref, here_ref[0], resident, holders)
    shape = (rolls, total)
    slot = lax.broadcasted_iota(jnp.int32, shape, 1) // steps
    picked = jnp.where(slot == jnp.broadcast_to(place, shape), 1.0, 0.0).astype(jnp.bfloat16)
    shape = (rows, rolls)
    roll = lax.broadcasted_iota(jnp.int32, shape, 0) // steps
    spread = roll == lax.broadcasted_iota(jnp.int32, shape, 1)
    chosen = dot_nn(jnp.where(spread, 1.0, 0.0).astype(jnp.bfloat16), picked)
    shape = (rows, total)
    step = lax.broadcasted_iota(jnp.int32, shape, 0) % steps
    aligned = step == lax.broadcasted_iota(jnp.int32, shape, 1) % steps
    chosen_ref[...] = jnp.where(aligned, chosen, 0.0).astype(jnp.bfloat16)


def choose(here, adapter_row, total, steps, resident, holders):
    rows = adapter_row.shape[1] * steps
    return pl.pallas_call(
        functools.partial(choose_kernel, steps=steps, resident=resident, holders=holders),
        out_shape=jax.ShapeDtypeStruct((rows, total), jnp.bfloat16),
        in_specs=[SMEM, VMEM],
        out_specs=VMEM,
        compiler_params=pltpu.CompilerParams(vmem_limit_bytes=20 * MIB),
        cost_estimate=BRIEF,
    )(here, adapter_row)


def combine_kernel(chosen_ref, *refs, count, starts):
    pieces, sums, out, total_ref = refs[:count], refs[count:-2], refs[-2], refs[-1]
    stacked = jnp.concatenate([x[...] for x in pieces], axis=0)
    total_ref[...] = dot_nn(chosen_ref[...], stacked)
    for start, x in zip(starts, sums):
        span = pl.ds(start, x.shape[0])
        total_ref[span, :] += x[...].astype(jnp.float32)
    out[...] = total_ref[...].reshape(out.shape).astype(jnp.bfloat16)


def combine(chosen, pieces, sums, steps):
    width = pieces[0].shape[1]
    count = len(pieces)
    starts, flat = zip(*sums)
    rows = chosen.shape[0]
    block = min(width, 2 * HEAD_SIZE)

    def columns(x):
        return pl.BlockSpec((x, block), lambda j: (0, j))

    return pl.pallas_call(
        functools.partial(combine_kernel, count=count, starts=starts),
        grid=(width // block,),
        out_shape=jax.ShapeDtypeStruct((rows // steps, steps, width), jnp.bfloat16),
        in_specs=[pl.BlockSpec(chosen.shape, lambda j: (0, 0))]
        + [columns(x.shape[0]) for x in (*pieces, *flat)],
        out_specs=pl.BlockSpec((rows // steps, steps, block), lambda j: (0, 0, j)),
        scratch_shapes=[pltpu.VMEM((rows, block), jnp.float32)],
        compiler_params=pltpu.CompilerParams(vmem_limit_bytes=20 * MIB),
        cost_estimate=BRIEF,
    )(chosen, *pieces, *flat)


def local(
    queries,
    shared_prefix_cache,
    rollout_suffix_cache,
    fresh_key_value,
    rollout_prefix_index,
    rollout_suffix_length,
    rollout_adapter_index,
    output_projection_weight,
    adapter_shrink_weight,
    adapter_expand_weight,
):
    rolls, steps, width = queries.shape
    rows = rolls * steps
    prefix_count = shared_prefix_cache.shape[1]
    resident, rank, out_width = adapter_expand_weight.shape
    holders, sides = lax.axis_size("adapter"), lax.axis_size("tensor")
    block, chips = holders // FOLD, sides // 2
    here, side = lax.axis_index("adapter"), lax.axis_index("tensor")
    chip, core = side // 2, side % 2

    def in_block(shift):
        return [(i, i // block * block + (i + shift) % block) for i in range(holders)]

    cores = [(t, t // 2 * 2 + (t + 1) % 2) for t in range(sides)]

    def over_chips(shift):
        return [(t, (t // 2 + shift) % chips * 2 + t % 2) for t in range(sides)]

    own_shrink = adapter_shrink_weight.reshape(resident * rank, width)
    own_expand = adapter_expand_weight.reshape(resident * rank, out_width)
    far = [(i, (i + block) % holders) for i in range(holders)]

    slots = FOLD * resident * MOST * steps
    per_adapter = MOST * steps
    adapter_row = rollout_adapter_index.reshape(1, rolls)
    lengths, prefixes = rollout_suffix_length[None, :], rollout_prefix_index[None, :]
    here = here.reshape(1).astype(jnp.int32)
    core = core.reshape(1).astype(jnp.int32)
    chip_index = chip.reshape(1).astype(jnp.int32)
    tie = lax.optimization_barrier

    def send_over_chips(away, cuts):
        return [
            lax.ppermute(x, "tensor", over_chips(1 + k // cuts)) for k, x in enumerate(away)
        ]

    def placed(start, own, came, cuts):
        rows = own.shape[0] // cuts
        return [(start, own)] + [(start + k % cuts * rows, x) for k, x in enumerate(came)]

    shrink = lax.ppermute(own_shrink, "adapter", far)
    attended = attend(
        lengths, prefixes, queries, shared_prefix_cache, rollout_suffix_cache, fresh_key_value,
        steps, 0, rolls // BLOCK_ROLLS,
    )
    packed = list(pack(here, adapter_row, [attended], block, slots, steps, resident, holders))
    attended, packed[0] = tie((attended, packed[0]))
    pieces = [packed[0]] + [
        lax.ppermute(packed[d], "adapter", in_block(d)) for d in range(1, block)
    ]
    send = project(1 - core, attended, output_projection_weight, out_width)
    chosen = choose(here, adapter_row, block * slots, steps, resident, holders)
    send, chosen = tie((send, chosen))
    come = lax.ppermute(send, "tensor", cores)
    pieces[0], shrink, moved = tie((pieces[0], shrink, own_expand))
    expand = lax.ppermute(moved, "adapter", far)
    codes = shrink_rows([own_shrink, shrink], pieces, per_adapter, rank)
    codes = codes + lax.ppermute(codes, "tensor", cores)
    brief, attended = tie((codes.astype(jnp.bfloat16), attended))
    keep = project(core, attended, output_projection_weight, out_width)
    own, *away = pair_sums(chip_index, keep, come, 1)
    codes = [brief] + [lax.ppermute(brief, "tensor", over_chips(s)) for s in range(1, chips)]
    codes, away = tie((codes, away))
    came = send_over_chips(away, 1)
    wide = expand_rows([own_expand, expand], codes, per_adapter, rank, block)
    back = [wide[0]] + [
        lax.ppermute(wide[d], "adapter", in_block(block - d)) for d in range(1, block)
    ]
    return combine(chosen, back, placed(0, own, came, 1), steps)


def solution(mesh):
    placed = (
        P("adapter", None, "tensor"),
        P(None, "adapter", None, "tensor"),
        P(None, "adapter", None, "tensor"),
        P(None, "adapter", None, "tensor"),
        P("adapter"),
        P("adapter"),
        P("adapter", None),
        P("tensor", None),
        P("adapter", None, "tensor"),
        P("adapter", None, "tensor"),
    )
    return jax.shard_map(
        local, mesh=mesh, in_specs=placed, out_specs=P("adapter", None, "tensor"), check_vma=False
    )
```
